32 devices in a mesh: wide: 8 (over z, x), narrow: 4 (over y, core).
Axes of the slice: x: 2, y: 2, z: 4, core: 2. Of those that a mesh axis runs over, the one named last changes fastest.
Arguments:
- tokens: bfloat16 [2, 32, 256, 640], P(None, ('wide', 'narrow')), may hold values from -6 to 6
- cotangent: bfloat16 [2, 32, 256, 640], P(None, ('wide', 'narrow')), may hold values from -6 to 6
- lengths: int32 [2, 32], P(None, ('wide', 'narrow')), may hold values from 32 to 1056, as said below
- offsets: int32 [2, 32], P(None, ('wide', 'narrow')), may hold values from 0 to 928, as said below
- attn_weight: float32 [640, 2560], P(None, ('wide', 'narrow'))
- attn_first: float32 [640, 2560], P(None, ('wide', 'narrow'))
- attn_second: float32 [640, 2560], P(None, ('wide', 'narrow'))
- up_weight: float32 [640, 2560], P(None, ('wide', 'narrow')), may hold values from -0.25 to 0.25
- up_first: float32 [640, 2560], P(None, ('wide', 'narrow')), may hold values from -24 to 24
- up_second: float32 [640, 2560], P(None, ('wide', 'narrow')), may hold values from 1.47456 to 5.89824
- down_weight: float32 [640, 2560], P(None, ('wide', 'narrow')), may hold values from -0.125 to 0.125
- down_first: float32 [640, 2560], P(None, ('wide', 'narrow')), may hold values from -48 to 48
- down_second: float32 [640, 2560], P(None, ('wide', 'narrow')), may hold values from 5.89824 to 23.59296
- vectors: float32 [13, 640], replicated
- vec_first: float32 [13, 640], replicated, may hold values from -48 to 48
- vec_second: float32 [13, 640], replicated, may hold values from 5.89824 to 23.59296
Outputs:
- output: bfloat16 [2, 32, 256, 640], P(None, ('wide', 'narrow'))
- input_grad: bfloat16 [2, 32, 256, 640], P(None, ('wide', 'narrow'))
- attn_grad: float32 [640, 2560], P(None, ('wide', 'narrow'))
- up_grad: float32 [640, 2560], P(None, ('wide', 'narrow'))
- down_grad: float32 [640, 2560], P(None, ('wide', 'narrow'))
- vector_grad: float32 [13, 640], replicated
- attn_second_new: float32 [640, 2560], P(None, ('wide', 'narrow'))
- up_second_new: float32 [640, 2560], P(None, ('wide', 'narrow'))
- down_second_new: float32 [640, 2560], P(None, ('wide', 'narrow'))
- vec_second_new: float32 [13, 640], replicated
- attn_new: float32 [640, 2560], P(None, ('wide', 'narrow'))
- up_new: float32 [640, 2560], P(None, ('wide', 'narrow'))
- down_new: float32 [640, 2560], P(None, ('wide', 'narrow'))
- vectors_new: float32 [13, 640], replicated
The draws below stay inside these ranges and needn't reach their ends.
Inputs may be any that keep to these rules, and one draw needn't show every extreme that they name: `lengths`: lengths are heavy-tailed; some window holds a protein of each extreme length. `offsets`: A window of a protein no longer than 256 starts at 0; a longer protein's window starts at least 128 positions before its end. So 256 // 8 to 256 keys of a window are visible, and some window has exactly 32.
All inputs are finite; a program needn't handle non-finite values.
Results may differ from the reference program's by a relative error of at most 0.014.
Values may be sent and summed in bfloat16 or wider, within the bound.
No kernel may reach another device: no remote copies, remote signals or barrier semaphores. Data moves between devices by JAX's collectives and lax.ppermute only.
A program may use at most 128 MiB of HBM per device.

```python
import math
import jax
import jax.numpy as jnp
from jax import lax

D = 640
HEADS = 20
HEAD_DIM = 32
FF = 2560
SEQ = 256
MICRO = 2
STEP = 10
BATCH = 32
TOKENS = 16384


def protein_lengths(key):
    integers = jax.random.randint(jax.random.fold_in(key, 101), (MICRO, BATCH), 0, 1024)
    cubed = integers * integers // 1024 * integers // 1024
    lengths_all = SEQ // 8 + cubed * (4 * SEQ) // 1024
    lengths_all = lengths_all.at[0, 0].set(SEQ // 8 + 4 * SEQ).at[0, 1].set(SEQ // 8)
    return lengths_all.astype(jnp.int32)


def column_scale(first_three, last_one):
    column = jnp.arange(4 * D)
    return jnp.where(column < 3 * D, first_three, last_one)


def draw_lengths(key, part):
    lengths_all = protein_lengths(key)
    return lengths_all


def draw_offsets(key, part):
    lengths_all = protein_lengths(key)
    key = jax.random.fold_in(key, 6)
    last_start = jnp.maximum(lengths_all - SEQ // 2, 0)
    crop_start = jax.random.randint(key, (MICRO, BATCH), 0, last_start + 1)
    crop_start = jnp.where(lengths_all > SEQ, crop_start, 0)
    crop_start = crop_start.at[0, 0].set(SEQ // 8 + 4 * SEQ - SEQ // 2)
    return crop_start.astype(jnp.int32)


def draw_attn_weight(key, part):
    key = jax.random.fold_in(key, 21)
    base = jax.random.truncated_normal(key, -4.0, 4.0, (D, 4 * D), jnp.float32)
    return base * column_scale(1.2 * D ** (-0.5), max(D * 16 // SEQ, 8) ** (-0.5))


def draw_attn_first(key, part):
    key = jax.random.fold_in(key, 22)
    base = jax.random.truncated_normal(key, -4.0, 4.0, (D, 4 * D), jnp.float32)
    return base * column_scale(1.0, 0.15) * (0.111 * TOKENS ** 0.5)


def draw_attn_second(key, part):
    key = jax.random.fold_in(key, 23)
    factor = jnp.exp(jax.random.uniform(key, (D, 4 * D), jnp.float32, 0.0, math.log(4.0)))
    magnitude = column_scale(1.0, 0.15)
    return factor * magnitude * magnitude * (0.001001 * TOKENS)


def draw_vectors(key, part):
    key = jax.random.fold_in(key, 31)
    base = jax.random.truncated_normal(key, -4.0, 4.0, (13, D), jnp.float32)
    row_number = jnp.arange(13)[:, None]
    is_gain = (row_number == 0) | (row_number == 6)
    return jnp.where(is_gain, 1.0 + 0.1 * base, 0.2 * base)


def block_levels(stream_key, shape, shards, low, largest):
    loudness, own = 1.0, jax.random.fold_in(stream_key, 6)
    for dim, blocks in shards:
        heights = jnp.exp(jax.random.uniform(jax.random.fold_in(own, dim), (blocks,), jnp.float32, low / len(shards), largest / len(shards)))
        loudness = loudness * jnp.repeat(heights, shape[dim] // blocks).reshape([-1 if axis == dim else 1 for axis in range(len(shape))])
    return loudness


def normal_values(key, dims, deviation, bound, shards=(), kind=jnp.bfloat16):
    gain = block_levels(key, dims, shards, -0.22, 0.18) if shards else 1.0
    array = jax.random.normal(key, dims, jnp.float32) * deviation * gain
    return jnp.minimum(jnp.maximum(array, -bound), bound).astype(kind)


def setup_inputs(seed: int = 0) -> dict:
    streams_of = jax.random.split(jax.random.key(seed), 17)
    return {
        "tokens": normal_values(streams_of[0], (MICRO, BATCH, SEQ, D), 1.0, 6.0, ((1, 32),)),
        "cotangent": normal_values(streams_of[1], (MICRO, BATCH, SEQ, D), 1.0, 6.0, ((1, 32),)),
        "lengths": draw_lengths(jax.random.fold_in(streams_of[16], 71), 0),
        "offsets": draw_offsets(jax.random.fold_in(streams_of[16], 71), 0),
        "attn_weight": draw_attn_weight(jax.random.fold_in(streams_of[16], 71), 0),
        "attn_first": draw_attn_first(jax.random.fold_in(streams_of[16], 71), 0),
        "attn_second": draw_attn_second(jax.random.fold_in(streams_of[16], 71), 0),
        "up_weight": normal_values(streams_of[7], (D, FF), D ** -0.5, 0.25, ((1, 32),), jnp.float32),
        "up_first": normal_values(streams_of[8], (D, FF), (0.0333 * TOKENS ** 0.5), 24.0, ((1, 32),), jnp.float32),
        "up_second": jnp.clip(jnp.exp(math.log(5.89824) - 1.3862944 * jax.random.uniform(streams_of[9], (D, FF), jnp.float32) ** block_levels(streams_of[9], (D, FF), ((1, 32),), -0.2, 0.2)), 1.47456, 5.89824),
        "down_weight": normal_values(streams_of[10], (D, FF), FF ** -0.5, 0.125, ((1, 32),), jnp.float32),
        "down_first": normal_values(streams_of[11], (D, FF), (0.0666 * TOKENS ** 0.5), 48.0, ((1, 32),), jnp.float32),
        "down_second": jnp.clip(jnp.exp(math.log(23.59296) - 1.3862944 * jax.random.uniform(streams_of[12], (D, FF), jnp.float32) ** block_levels(streams_of[12], (D, FF), ((1, 32),), -0.2, 0.2)), 5.89824, 23.59296),
        "vectors": draw_vectors(jax.random.fold_in(streams_of[16], 71), 0),
        "vec_first": normal_values(streams_of[14], (13, D), (0.0666 * TOKENS ** 0.5), 48.0, (), jnp.float32),
        "vec_second": jnp.clip(jnp.exp(jax.random.uniform(streams_of[15], (13, D), jnp.float32, math.log(5.89824), math.log(23.59296))), 5.89824, 23.59296),
    }


@jax.custom_vjp
def low(v):
    return lax.optimization_barrier(v.astype(jnp.bfloat16)).astype(jnp.float32)

@jax.custom_vjp
def low_back(v):
    return v

def low_keep(v):
    return (low(v), None)

def low_pass(kept, grad):
    return (grad,)

def back_keep(v):
    return (v, None)

def back_low(kept, grad):
    return (low(grad),)
low.defvjp(low_keep, low_pass)
low_back.defvjp(back_keep, back_low)
exact_precision = lax.Precision.HIGHEST

def matmul(left, right):
    return jnp.dot(left, right, precision=exact_precision, preferred_element_type=jnp.float32)

def layer_norm(inputs, gain_row, shift_row):
    centered = inputs - lax.optimization_barrier(jnp.mean(inputs, axis=-1, keepdims=True))
    scaled = centered * lax.rsqrt(lax.optimization_barrier(jnp.mean(centered * centered, axis=-1, keepdims=True)) + 1e-05)
    return scaled * gain_row + shift_row

def rotary(inputs):
    position = jnp.arange(SEQ, dtype=jnp.float32)
    frequency = 10000.0 ** (-jnp.arange(0, HEAD_DIM, 2, dtype=jnp.float32) / HEAD_DIM)
    angles = position[:, None] * frequency[None, :]
    angles = jnp.concatenate([angles, angles], axis=-1)[:, None, :]
    half_dim = HEAD_DIM // 2
    turned = jnp.concatenate([-inputs[..., half_dim:], inputs[..., :half_dim]], axis=-1)
    return inputs * jnp.cos(angles) + turned * jnp.sin(angles)

def window(attn_w, up_w, down_w, vecs, inputs, key_count):
    hidden = low(layer_norm(inputs, vecs[0], vecs[1]))
    project = matmul(hidden, attn_w[:, :3 * D]) + vecs[2:5].reshape(3 * D)
    queries = low(rotary(low_back(project[:, :D]).reshape(SEQ, HEADS, HEAD_DIM)))
    keys_rot = low(rotary(low_back(project[:, D:2 * D]).reshape(SEQ, HEADS, HEAD_DIM)))
    values = low(low_back(project[:, 2 * D:])).reshape(SEQ, HEADS, HEAD_DIM)
    raw_scores = jnp.einsum('qhe,khe->hqk', queries, keys_rot, precision=exact_precision) * HEAD_DIM ** (-0.5)
    visible = jnp.arange(SEQ, dtype=jnp.int32) < key_count
    scores = low_back(jnp.where(visible[None, None, :], raw_scores, -1000000000.0))
    row_max = lax.optimization_barrier(jnp.max(scores, axis=-1, keepdims=True))
    exponent = jnp.exp(scores - row_max)
    probabilities = low(exponent / lax.optimization_barrier(jnp.sum(exponent, axis=-1, keepdims=True)))
    mixed_heads = jnp.einsum('hqk,khe->qhe', probabilities, values, precision=exact_precision).reshape(SEQ, D)
    mixed_heads = low_back(low(mixed_heads))
    branch = low_back(matmul(mixed_heads, attn_w[:, 3 * D:]))
    middle = inputs + branch + vecs[5]
    normed = low(layer_norm(middle, vecs[6], vecs[7]))
    pre_act = low_back(matmul(normed, up_w) + vecs[9:].reshape(FF))
    active = low(jax.nn.gelu(pre_act, approximate=False))
    down_part = lax.dot_general(active, down_w, (((1,), (1,)), ((), ())), precision=exact_precision, preferred_element_type=jnp.float32)
    return middle + down_part + vecs[8]

def adamw(weight, first_moment, second_moment, gradient, rate_value):
    first_new = 0.9 * first_moment + 0.1 * gradient
    second_new = 0.999 * second_moment + 0.001 * gradient * gradient
    corrected = first_new / (1.0 - 0.9 ** STEP) / (jnp.sqrt(second_new / (1.0 - 0.999 ** STEP)) + 1e-08)
    return (second_new, weight - rate_value * (corrected + 0.01 * weight))

def reference(tokens, cotangent, lengths, offsets, attn_weight, attn_first, attn_second, up_weight, up_first, up_second, down_weight, down_first, down_second, vectors, vec_first, vec_second):
    window_total = MICRO * BATCH
    group_size = math.gcd(window_total, max(1, 4096 // SEQ))
    group_count = window_total // group_size
    inputs_all = tokens.astype(jnp.float32).reshape(group_count, group_size, SEQ, D)
    back_all = cotangent.astype(jnp.float32).reshape(group_count, group_size, SEQ, D)
    count_all = jnp.minimum(lengths - offsets, SEQ).astype(jnp.int32).reshape(group_count, group_size)

    def run_group(running, batch_in):
        inputs_group, back_group, count_group = batch_in

        def whole_group(attn_w, up_w, down_w, vecs, inputs_x):
            checked = jax.checkpoint(window)
            return jax.vmap(checked, in_axes=(None, None, None, None, 0, 0))(low(attn_w), low(up_w), low(down_w), vecs, inputs_x, count_group)
        result, pullback = jax.vjp(whole_group, attn_weight, up_weight, down_weight, vectors, inputs_group)
        gradients = pullback(back_group)
        running = tuple((running[member] + gradients[member] for member in range(4)))
        return (running, (result.astype(jnp.bfloat16), gradients[4].astype(jnp.bfloat16)))
    zero_grads = (jnp.zeros((D, 4 * D), jnp.float32), jnp.zeros((D, FF), jnp.float32), jnp.zeros((D, FF), jnp.float32), jnp.zeros((13, D), jnp.float32))
    grad_sums, (outputs, input_grads) = lax.scan(run_group, zero_grads, (inputs_all, back_all, count_all))
    output = outputs.reshape(MICRO, BATCH, SEQ, D)
    input_grad = input_grads.reshape(MICRO, BATCH, SEQ, D)
    attn_second_new, attn_new = adamw(attn_weight, attn_first, attn_second, grad_sums[0], 0.1)
    up_second_new, up_new = adamw(up_weight, up_first, up_second, grad_sums[1], 0.1)
    down_second_new, down_new = adamw(down_weight, down_first, down_second, grad_sums[2], 0.1)
    vec_second_new, vectors_new = adamw(vectors, vec_first, vec_second, grad_sums[3], 0.5)
    return (output, input_grad, grad_sums[0], grad_sums[1], grad_sums[2], grad_sums[3], attn_second_new, up_second_new, down_second_new, vec_second_new, attn_new, up_new, down_new, vectors_new)
```

```python
import functools

import jax
import jax.numpy as jnp
from jax import lax
from jax.sharding import PartitionSpec as P

D = 640
HEADS = 20
HEAD_DIM = 32
FF = 2560
SEQ = 256
STEP = 10
AXES = ("wide", "narrow")
GROUPS = 4
GROUP_HEADS = HEADS // GROUPS
GROUP = GROUP_HEADS * HEAD_DIM
BF16 = jnp.bfloat16
F32 = jnp.float32


def nt(left, right):
    return lax.dot_general(left, right, (((1,), (1,)), ((), ())), preferred_element_type=F32)


def nn(left, right):
    return jnp.dot(left, right, preferred_element_type=F32)


def tn(left, right):
    return lax.dot_general(left, right, (((0,), (0,)), ((), ())), preferred_element_type=F32)


def pick(array, index):
    return lax.dynamic_index_in_dim(array, index, 0, keepdims=False)


def normalize(rows):
    centered = rows - jnp.mean(rows, axis=-1, keepdims=True)
    scale = lax.rsqrt(jnp.mean(centered * centered, axis=-1, keepdims=True) + 1e-05)
    return centered * scale, scale


def norm_back(grad, scaled, scale, gain):
    weighted = grad * gain
    mean_one = jnp.mean(weighted, axis=-1, keepdims=True)
    mean_two = jnp.mean(weighted * scaled, axis=-1, keepdims=True)
    return scale * (weighted - mean_one - scaled * mean_two)


def rope_tables():
    position = jnp.arange(SEQ, dtype=F32)
    frequency = 10000.0 ** (-jnp.arange(0, HEAD_DIM, 2, dtype=F32) / HEAD_DIM)
    angles = position[:, None] * frequency[None, :]
    angles = jnp.concatenate([angles, angles], axis=-1)
    return jnp.cos(angles), jnp.sin(angles)


def turn(rows, sign):
    half = HEAD_DIM // 2
    return jnp.concatenate([-sign * rows[..., half:], sign * rows[..., :half]], axis=-1)


def rotate(rows, sign):
    cos, sin = rope_tables()
    shaped = rows.reshape(-1, SEQ, GROUP_HEADS, HEAD_DIM)
    out = shaped * cos[None, :, None, :] + turn(shaped, sign) * sin[None, :, None, :]
    return out.reshape(rows.shape)


def split_heads(rows):
    return rows.reshape(-1, SEQ, GROUP_HEADS, HEAD_DIM)


def attention_forward(hidden, weight, bias, counts):
    q = rotate(nt(hidden, weight[0]) + bias[0], 1.0).astype(BF16)
    k = rotate(nt(hidden, weight[1]) + bias[1], 1.0).astype(BF16)
    v = (nt(hidden, weight[2]) + bias[2]).astype(BF16)
    scores = jnp.einsum("wqhe,wkhe->whqk", split_heads(q), split_heads(k), preferred_element_type=F32)
    scores = scores * HEAD_DIM ** (-0.5)
    visible = jnp.arange(SEQ, dtype=jnp.int32)[None, :] < counts[:, None]
    scores = jnp.where(visible[:, None, None, :], scores, -1000000000.0)
    top = jnp.max(scores, axis=-1, keepdims=True)
    exponent = jnp.exp(scores - top)
    prob = exponent / jnp.sum(exponent, axis=-1, keepdims=True)
    low = prob.astype(BF16)
    mixed = jnp.einsum("whqk,wkhe->wqhe", low, split_heads(v), preferred_element_type=F32)
    return mixed.reshape(hidden.shape[0], GROUP).astype(BF16), (q, k, v, prob)


def attention_backward(saved, grad_mixed):
    q, k, v, prob = saved
    rows = q.shape[0]
    low = prob.astype(BF16)
    do = split_heads(grad_mixed)
    dp = jnp.einsum("wqhe,wkhe->whqk", do, split_heads(v), preferred_element_type=F32)
    ds = (prob * (dp - jnp.sum(prob * dp, axis=-1, keepdims=True))).astype(BF16)
    scale = HEAD_DIM ** (-0.5)
    dq = jnp.einsum("whqk,wkhe->wqhe", ds, split_heads(k), preferred_element_type=F32) * scale
    dk = jnp.einsum("whqk,wqhe->wkhe", ds, split_heads(q), preferred_element_type=F32) * scale
    dv = jnp.einsum("whqk,wqhe->wkhe", low, do, preferred_element_type=F32)
    dq = rotate(dq.reshape(rows, GROUP), -1.0).astype(BF16)
    dk = rotate(dk.reshape(rows, GROUP), -1.0).astype(BF16)
    return dq, dk, dv.reshape(rows, GROUP).astype(BF16)


def adamw(weight, first_moment, second_moment, gradient, rate_value):
    first_new = 0.9 * first_moment + 0.1 * gradient
    second_new = 0.999 * second_moment + 0.001 * gradient * gradient
    corrected = first_new / (1.0 - 0.9**STEP) / (jnp.sqrt(second_new / (1.0 - 0.999**STEP)) + 1e-08)
    return (second_new, weight - rate_value * (corrected + 0.01 * weight))


class Layout:
    def __init__(self, total):
        self.total = total
        self.block = 4 * D // total
        self.stride = total // 4
        self.me = lax.axis_index(AXES)
        self.core = lax.rem(self.me, 2)

    def swap(self, value, mask):
        return lax.ppermute(value, AXES, [(i, i ^ mask) for i in range(self.total)])

    def shift(self, value, steps):
        pairs = [(i, (i + self.stride * steps) % self.total) for i in range(self.total)]
        return lax.ppermute(value, AXES, pairs)


class Ring(Layout):
    def __init__(self, total):
        super().__init__(total)
        self.z = self.me // 8
        self.plane = lax.rem(self.me // 2, 4)

    def along_z(self, value):
        return jnp.stack([value] + [self.shift(value, -s) for s in (1, 2, 3)])

    def in_plane(self, value):
        return [value] + [self.swap(value, 2 * r) for r in (1, 2, 3)]

    def gather_attention(self, shard):
        line = self.along_z(shard)
        groups = []
        for mine in self.in_plane(line):
            other = self.swap(mine, 1)
            first = jnp.where(self.core == 0, mine, other)
            second = jnp.where(self.core == 0, other, mine)
            chip = jnp.concatenate([first, second], axis=1)
            groups.append([pick(chip, lax.rem(part + 4 - self.z, 4)) for part in range(4)])
        return groups

    def gather_hidden(self, shard):
        line = self.along_z(shard)
        return jnp.stack(self.in_plane(line))

    def hidden_index(self):
        order = jnp.arange(16)
        place = lax.rem(self.z + lax.rem(order, 4), 4) * 4 + (self.plane ^ (order // 4))
        return place * 2 + self.core

    def scatter(self, parts):
        total = parts[0].astype(F32)
        for r in (1, 2, 3):
            total = total + self.swap(parts[r], 2 * r).astype(F32)
        low = total.astype(BF16)
        out = total[0]
        for s in (1, 2, 3):
            out = out + self.shift(low[s], s).astype(F32)
        return out

    def scatter_hidden(self, grad):
        parts = grad.reshape(4, 4, -1, D).astype(BF16)
        return self.scatter([parts[r] for r in range(4)])

    def scatter_attention(self, grads):
        parts = []
        for grad in grads:
            halves = grad.reshape(4, 2, -1, D).astype(BF16)
            mine = lax.dynamic_index_in_dim(halves, self.core, 1, keepdims=False)
            other = lax.dynamic_index_in_dim(halves, 1 - self.core, 1, keepdims=False)
            summed = (mine.astype(F32) + self.swap(other, 1).astype(F32)).astype(BF16)
            parts.append(jnp.stack([pick(summed, lax.rem(self.z + s, 4)) for s in range(4)]))
        return self.scatter(parts)


class Whole(Layout):
    def __init__(self, total):
        super().__init__(total)
        self.plane = jnp.int32(0)

    def gather(self, shard):
        return lax.all_gather(shard, AXES, axis=0, tiled=True)

    def gather_attention(self, shard):
        full = self.gather(shard).reshape(4, 4, GROUP, D)
        return [[full[part, r] for part in range(4)] for r in range(4)]

    def gather_hidden(self, shard):
        full = lax.all_gather(shard, AXES, axis=0).reshape(self.total // 2, 2, -1, D)
        return lax.dynamic_index_in_dim(full, self.core, 1, keepdims=False)

    def hidden_index(self):
        return jnp.arange(self.total // 2) * 2 + self.core

    def scatter_hidden(self, grad):
        halves = grad.reshape(self.total // 2, 1, -1, D)
        full = jnp.where(jnp.arange(2)[None, :, None, None] == self.core, halves, 0.0)
        return lax.psum_scatter(full.reshape(-1, D), AXES, scatter_dimension=0, tiled=True)

    def scatter_attention(self, grads):
        full = jnp.stack(grads, axis=1).reshape(4 * D, D)
        return lax.psum_scatter(full, AXES, scatter_dimension=0, tiled=True)


def per_device(
    total,
    tokens,
    cotangent,
    lengths,
    offsets,
    attn_weight,
    attn_first,
    attn_second,
    up_weight,
    up_first,
    up_second,
    down_weight,
    down_first,
    down_second,
    vectors,
    vec_first,
    vec_second,
):
    lay = Ring(total) if total == 32 else Whole(total)
    counts = jnp.minimum(lengths - offsets, SEQ).reshape(-1)
    rows = counts.shape[0] * SEQ

    attn_shard = attn_weight.T.astype(BF16)
    up_shard = up_weight.T.astype(BF16)
    down_shard = down_weight.T.astype(BF16)
    attn_groups = lay.gather_attention(attn_shard)
    up_full = lay.gather_hidden(up_shard).reshape(FF // 2, D)
    down_full = lay.gather_hidden(down_shard).reshape(FF // 2, D)

    flat = tokens.reshape(rows, D).astype(F32)
    back = cotangent.reshape(rows, D)
    back_both = jnp.concatenate([back, lay.swap(back, 1)])
    scaled_one, scale_one = normalize(flat)
    hidden = (scaled_one * vectors[0] + vectors[1]).astype(BF16)

    bias = vectors[2:5].reshape(3, GROUPS, GROUP)
    mixed, saved = [], []
    for r in range(GROUPS):
        group_bias = lax.dynamic_index_in_dim(bias, lay.plane ^ r, 1, keepdims=False)
        mixed_r, saved_r = attention_forward(hidden, attn_groups[r][:3], group_bias, counts)
        mixed.append(mixed_r)
        saved.append(saved_r)
    order = [lay.plane ^ place for place in range(GROUPS)]
    mixed = jnp.stack(mixed)
    mixed_true = jnp.concatenate([pick(mixed, r) for r in order], axis=1)
    out_groups = jnp.stack([group[3] for group in attn_groups])
    out_weight = jnp.concatenate([pick(out_groups, r) for r in order])
    middle = flat + nt(mixed_true, out_weight) + vectors[5]
    scaled_two, scale_two = normalize(middle)
    normed = (scaled_two * vectors[6] + vectors[7]).astype(BF16)

    normed_both = jnp.concatenate([normed, lay.swap(normed, 1)])
    place = lay.hidden_index()
    bias_up = vectors[9:].reshape(total, lay.block)[place].reshape(FF // 2)
    pre = nt(normed_both, up_full) + bias_up
    cdf = 0.5 * (1.0 + lax.erf(pre * (0.5**0.5)))
    active = (pre * cdf).astype(BF16)
    slope = cdf + pre * jnp.exp(-0.5 * pre * pre) * (1.0 / (2.0 * jnp.pi) ** 0.5)
    grad_down = lay.scatter_hidden(tn(active, back_both))
    part = nn(active, down_full)
    grad_pre = (nt(back_both, down_full) * slope).astype(BF16)
    grad_up = lay.scatter_hidden(tn(grad_pre, normed_both))
    grad_bias_up = jnp.sum(grad_pre.astype(F32), axis=0)
    back_part = nn(grad_pre, up_full)

    def both(value):
        return value[:rows] + lay.swap(value[rows:].astype(BF16), 1).astype(F32)

    result = (middle + both(part) + vectors[8]).astype(BF16)
    grad_normed = both(back_part)
    grad_middle = back.astype(F32) + norm_back(grad_normed, scaled_two, scale_two, vectors[6])
    branch = grad_middle.astype(BF16)
    grad_out = tn(branch, mixed_true).reshape(GROUPS, GROUP, D)
    grad_mixed = nn(branch, out_weight).astype(BF16).reshape(rows, GROUPS, GROUP)

    grads, grad_bias, grad_hidden = [], [], 0.0
    for r in range(GROUPS):
        grad_r = lax.dynamic_index_in_dim(grad_mixed, lay.plane ^ r, 1, keepdims=False)
        grad_parts = attention_backward(saved[r], grad_r)
        for part_index in range(3):
            grad_hidden = grad_hidden + nn(grad_parts[part_index], attn_groups[r][part_index])
        grads.append(
            jnp.stack([tn(value, hidden) for value in grad_parts] + [pick(grad_out, lay.plane ^ r)])
        )
        grad_bias.append(jnp.stack([jnp.sum(value.astype(F32), axis=0) for value in grad_parts]))
    grad_attn = lay.scatter_attention(grads)
    grad_bias = jnp.stack(grad_bias)
    grad_bias = jnp.concatenate([pick(grad_bias, r) for r in order], axis=1)
    input_grad = (grad_middle + norm_back(grad_hidden, scaled_one, scale_one, vectors[0])).astype(BF16)

    bias_up_rows = jnp.zeros((total, lay.block), F32).at[place].set(grad_bias_up.reshape(-1, lay.block))
    grad_vec = jnp.concatenate(
        [
            jnp.stack([jnp.sum(grad_hidden * scaled_one, axis=0), jnp.sum(grad_hidden, axis=0)]),
            grad_bias,
            jnp.stack(
                [
                    jnp.sum(grad_middle, axis=0),
                    jnp.sum(grad_normed * scaled_two, axis=0),
                    jnp.sum(grad_normed, axis=0),
                    jnp.sum(back.astype(F32), axis=0),
                ]
            ),
            bias_up_rows.reshape(4, D),
        ]
    )
    grad_vec = lax.psum(grad_vec, AXES)
    grad_attn, grad_up, grad_down = grad_attn.T, grad_up.T, grad_down.T
    attn_second_new, attn_new = adamw(attn_weight, attn_first, attn_second, grad_attn, 0.1)
    up_second_new, up_new = adamw(up_weight, up_first, up_second, grad_up, 0.1)
    down_second_new, down_new = adamw(down_weight, down_first, down_second, grad_down, 0.1)
    vec_second_new, vectors_new = adamw(vectors, vec_first, vec_second, grad_vec, 0.5)
    return (
        result.reshape(tokens.shape),
        input_grad.reshape(tokens.shape),
        grad_attn,
        grad_up,
        grad_down,
        grad_vec,
        attn_second_new,
        up_second_new,
        down_second_new,
        vec_second_new,
        attn_new,
        up_new,
        down_new,
        vectors_new,
    )


def solution(mesh):
    total = mesh.shape["wide"] * mesh.shape["narrow"]
    windows = P(None, AXES, None, None)
    counts = P(None, AXES)
    columns = P(None, AXES)
    in_specs = (windows,) * 2 + (counts,) * 2 + (columns,) * 9 + (P(),) * 3
    out_specs = (windows,) * 2 + (columns,) * 3 + (P(),) + (columns,) * 3 + (P(),) + (columns,) * 3 + (P(),)
    return jax.shard_map(
        functools.partial(per_device, total),
        mesh=mesh,
        in_specs=in_specs,
        out_specs=out_specs,
        check_vma=False,
    )
```

```python
import functools

import jax
import jax.numpy as jnp
from jax import lax
from jax.experimental import pallas as pl
from jax.experimental.pallas import tpu as pltpu
from jax.sharding import PartitionSpec as P

D = 640
HEADS = 20
HEAD_DIM = 32
FF = 2560
SEQ = 256
STEP = 10
AXES = ("wide", "narrow")
GROUPS = 4
GROUP_HEADS = HEADS // GROUPS
GROUP = GROUP_HEADS * HEAD_DIM
HALF = GROUP // 2
WIDE = 256
QUARTER = FF // 8
SCALE = HEAD_DIM ** (-0.5)
BF16 = jnp.bfloat16
F32 = jnp.float32
VMEM_LIMIT = 48 * 1024 * 1024


def nt(left, right):
    return lax.dot_general(left, right, (((1,), (1,)), ((), ())), preferred_element_type=F32)


def nn(left, right):
    return jnp.dot(left, right, preferred_element_type=F32)


def tn(left, right):
    return lax.dot_general(left, right, (((0,), (0,)), ((), ())), preferred_element_type=F32)


def shape(dims, kind=BF16):
    return jax.ShapeDtypeStruct(dims, kind)


def call(kernel, name, outs, place, args, flops, scratch=()):
    size = sum(a.size * a.dtype.itemsize for a in args) + sum(o.size * o.dtype.itemsize for o in outs)
    return pl.pallas_call(
        kernel,
        out_shape=tuple(outs),
        in_specs=[pl.BlockSpec(memory_space=pltpu.SMEM)] + [pl.BlockSpec(memory_space=pltpu.VMEM)] * len(args),
        out_specs=tuple([pl.BlockSpec(memory_space=pltpu.VMEM)] * len(outs)),
        scratch_shapes=list(scratch),
        compiler_params=pltpu.CompilerParams(vmem_limit_bytes=VMEM_LIMIT),
        cost_estimate=pl.CostEstimate(flops=flops, bytes_accessed=size, transcendentals=0),
        name=name,
    )(place, *args)


def normalize(rows):
    centered = rows - jnp.mean(rows, axis=-1, keepdims=True)
    scale = lax.rsqrt(jnp.mean(centered * centered, axis=-1, keepdims=True) + 1e-05)
    return centered * scale, scale


def norm_back(grad, scaled, scale, gain):
    weighted = grad * gain
    mean_one = jnp.mean(weighted, axis=-1, keepdims=True)
    mean_two = jnp.mean(weighted * scaled, axis=-1, keepdims=True)
    return scale * (weighted - mean_one - scaled * mean_two)


def column_sum(rows):
    return jnp.sum(rows, axis=0, keepdims=True)


def rope_tables():
    position = jnp.arange(SEQ, dtype=F32)
    frequency = 10000.0 ** (-jnp.arange(0, HEAD_DIM, 2, dtype=F32) / HEAD_DIM)
    angles = position[:, None] * frequency[None, :]
    cos, sin = jnp.cos(angles), jnp.sin(angles)
    return jnp.tile(cos, (1, 8)), jnp.tile(jnp.concatenate([-sin, sin], axis=1), (1, 4))


def swapped(rows):
    low = lax.broadcasted_iota(jnp.int32, rows.shape, 1) % HEAD_DIM < HEAD_DIM // 2
    return jnp.where(low, pltpu.roll(rows, 128 - HEAD_DIM // 2, 1), pltpu.roll(rows, HEAD_DIM // 2, 1))


def group_heads():
    for head in range(GROUP_HEADS):
        yield head, (head // 4) * 128, head % 4


def head_only(rows, lane):
    owner = lax.broadcasted_iota(jnp.int32, rows.shape, 1) // HEAD_DIM
    return jnp.where(owner == lane, rows, jnp.zeros_like(rows))


def halves(place):
    core = place[1]
    return pl.multiple_of(core * HALF, 16), pl.multiple_of((1 - core) * HALF, 16)


def first_norm_kernel(place, tokens, vectors, hidden):
    scaled, _ = normalize(tokens[...].astype(F32))
    hidden[...] = (scaled * vectors[0:1, :] + vectors[1:2, :]).astype(BF16)


def attention_forward_kernel(
    which, place, hidden, mine, other, bias, cos, sin, weight, weight_out, q_out, k_out, v_out, prob_out, mixed_out
):
    z, group = place[0], place[2] ^ which
    first, second = halves(place)
    for part in range(4):
        source = lax.rem(part + 4 - z, 4)
        if part < 3:
            weight[part, pl.ds(first, HALF), :] = mine[source]
            weight[part, pl.ds(second, HALF), :] = other[source]
            weight[part, GROUP:WIDE, :] = jnp.zeros((WIDE - GROUP, D), BF16)
        else:
            weight_out[pl.ds(first, HALF), :] = mine[source]
            weight_out[pl.ds(second, HALF), :] = other[source]
    rows = hidden[...]
    windows = rows.shape[0] // SEQ
    for part, out in ((0, q_out), (1, k_out), (2, v_out)):
        proj = nt(rows, weight[part]) + bias[group, part : part + 1, :]
        for window in range(windows):
            span = slice(window * SEQ, (window + 1) * SEQ)
            for tile in (0, 128):
                piece = proj[span, tile : tile + 128]
                if part < 2:
                    piece = piece * cos[...] + swapped(piece) * sin[...]
                out[span, tile : tile + 128] = piece.astype(BF16)
    for window in range(windows):
        span = slice(window * SEQ, (window + 1) * SEQ)
        visible = lax.broadcasted_iota(jnp.int32, (SEQ, 1), 0) < place[3 + window]
        values = v_out[span, :].T
        for head, tile, lane in group_heads():
            keys = head_only(k_out[span, tile : tile + 128], lane)
            scores = nt(keys, q_out[span, tile : tile + 128])
            scores = jnp.where(visible, scores, -1e30)
            top = jnp.max(scores, axis=0, keepdims=True)
            exponent = jnp.exp((scores - top) * SCALE)
            prob = (exponent * (1.0 / column_sum(exponent))).astype(BF16)
            prob_out[window * GROUP_HEADS + head] = prob
            rows_out = slice(head * HEAD_DIM, (head + 1) * HEAD_DIM)
            mixed_out[rows_out, span] = nn(values[rows_out], prob).astype(BF16)


def attention_forward(which, place, hidden, mine, other, bias, cos, sin):
    rows = hidden.shape[0]
    outs = [shape((3, WIDE, D)), shape((GROUP, D))] + [shape((rows, WIDE))] * 3
    outs += [shape((rows // SEQ * GROUP_HEADS, SEQ, SEQ)), shape((GROUP, rows))]
    return call(
        functools.partial(attention_forward_kernel, which), "attention_forward", outs, place,
        (hidden, mine, other, bias, cos, sin), 12 * rows * D * GROUP,
    )


def middle_kernel(place, tokens, vectors, *refs):
    mixed_in, weight_in = refs[:4], refs[4:8]
    middle, normed, mixed, weight, stage = refs[8:]
    for which in range(GROUPS):
        offset = pl.multiple_of((place[2] ^ which) * GROUP, 32)
        stage[pl.ds(offset, GROUP), :] = mixed_in[which][...]
        weight[pl.ds(offset, GROUP), :] = weight_in[which][...]
    mixed[...] = stage[...].T
    rows = tokens[...].astype(F32) + nt(mixed[...], weight[...]) + vectors[5:6, :]
    middle[...] = rows
    scaled, _ = normalize(rows)
    normed[...] = (scaled * vectors[6:7, :] + vectors[7:8, :]).astype(BF16)


def middle_layer(place, tokens, vectors, mixed, weights):
    rows = tokens.shape[0]
    outs = [shape((rows, D), F32), shape((rows, D)), shape((rows, D)), shape((D, D))]
    return call(
        middle_kernel, "middle", outs, place, (tokens, vectors, *mixed, *weights), 2 * rows * D * D,
        [pltpu.VMEM((D, rows), BF16)],
    )


def hidden_forward_kernel(place, up, bias, normed, normed_pair, back, back_pair, active, slope, grad_down):
    column = jnp.broadcast_to(bias[...], (8, QUARTER)).T[:, 0:1]
    rows = normed.shape[0]
    total = 0.0
    for part, inputs, grads in ((0, normed, back), (1, normed_pair, back_pair)):
        span = slice(part * rows, (part + 1) * rows)
        pre = nt(up[...], inputs[...]) + column
        cdf = 0.5 + 0.5 * lax.erf(pre * (0.5**0.5))
        low = (pre * cdf).astype(BF16)
        active[:, span] = low
        slope[:, span] = (cdf + pre * jnp.exp(-0.5 * pre * pre) * 0.3989422804014327).astype(BF16)
        total = total + nn(low, grads[...])
    grad_down[...] = total.astype(BF16)


def hidden_forward(place, up, bias, normed, normed_pair, back, back_pair):
    rows = 2 * normed.shape[0]
    outs = [shape((QUARTER, rows)), shape((QUARTER, rows)), shape((QUARTER, D))]
    return call(
        hidden_forward_kernel, "hidden_forward", outs, place, (up, bias, normed, normed_pair, back, back_pair),
        4 * rows * D * QUARTER,
    )


def hidden_backward_kernel(place, down, slope, normed, normed_pair, back, back_pair, grad_pre, grad_up, grad_bias):
    rows = normed.shape[0]
    total, bias = 0.0, 0.0
    for part, inputs, grads in ((0, normed, back), (1, normed_pair, back_pair)):
        span = slice(part * rows, (part + 1) * rows)
        low = (nt(down[...], grads[...]) * slope[:, span].astype(F32)).astype(BF16)
        grad_pre[:, span] = low
        total = total + nn(low, inputs[...])
        bias = bias + jnp.sum(low.astype(F32), axis=1, keepdims=True)
    grad_up[...] = total.astype(BF16)
    grad_bias[...] = jnp.broadcast_to(bias, (QUARTER, 8)).T


def hidden_backward(place, down, slope, normed, normed_pair, back, back_pair):
    rows = 2 * normed.shape[0]
    outs = [shape((QUARTER, rows)), shape((QUARTER, D)), shape((8, QUARTER), F32)]
    return call(
        hidden_backward_kernel, "hidden_backward", outs, place, (down, slope, normed, normed_pair, back, back_pair),
        4 * rows * D * QUARTER,
    )


def project_kernel(place, *refs):
    lefts, rights = refs[:4], refs[4:8]
    own, pair = refs[8:]
    rows = own.shape[0]
    for out, span in ((pair, slice(rows, 2 * rows)), (own, slice(0, rows))):
        total = 0.0
        for left, right in zip(lefts, rights):
            total = total + tn(left[:, span], right[...])
        out[...] = total.astype(out.dtype)


def project(place, name, lefts, rights):
    rows = lefts[0].shape[1] // 2
    outs = [shape((rows, D), F32), shape((rows, D))]
    return call(project_kernel, name, outs, place, (*lefts, *rights), 16 * rows * D * QUARTER)


def middle_backward_kernel(
    place, own, pair, middle, back, vectors, mixed, weight, grad_middle, sums, grad_mixed, mine, other, stage, stage_mixed
):
    grad = own[...] + pair[...].astype(F32)
    scaled, scale = normalize(middle[...])
    wide = back[...].astype(F32)
    total = wide + norm_back(grad, scaled, scale, vectors[6:7, :])
    grad_middle[...] = total
    sums[0:1, :] = column_sum(total)
    sums[1:2, :] = column_sum(grad * scaled)
    sums[2:3, :] = column_sum(grad)
    sums[3:4, :] = column_sum(wide)
    sums[4:8, :] = jnp.zeros((4, D), F32)
    low = total.astype(BF16)
    stage_mixed[...] = nt(weight[...].T, low).astype(BF16)
    stage[...] = tn(low, mixed[...]).astype(BF16)
    first, second = halves(place)
    for which in range(GROUPS):
        offset = (place[2] ^ which) * GROUP
        grad_mixed[which] = stage_mixed[pl.ds(pl.multiple_of(offset, 32), GROUP), :]
        mine[which] = stage[pl.ds(pl.multiple_of(offset + first, 16), HALF), :]
        other[which] = stage[pl.ds(pl.multiple_of(offset + second, 16), HALF), :]


def middle_backward(place, own, pair, middle, back, vectors, mixed, weight):
    rows = own.shape[0]
    outs = [shape((rows, D), F32), shape((8, D), F32), shape((GROUPS, GROUP, rows))]
    outs += [shape((GROUPS, HALF, D)), shape((GROUPS, HALF, D))]
    return call(
        middle_backward_kernel, "middle_backward", outs, place,
        (own, pair, middle, back, vectors, mixed, weight), 4 * rows * D * D,
        [pltpu.VMEM((D, D), BF16), pltpu.VMEM((D, rows), BF16)],
    )


def attention_backward_kernel(
    which, place, grad_mixed, q, k, v, prob_in, hidden, cos, sin, out_mine, out_other,
    dq_out, dk_out, dv_out, mine, other, bias, dq_turned, stage,
):
    rows = hidden.shape[0]
    for window in range(rows // SEQ):
        span = slice(window * SEQ, (window + 1) * SEQ)
        grad = grad_mixed[which, :, span].T
        tail = jnp.concatenate([grad[:, 128:GROUP], jnp.zeros((SEQ, WIDE - GROUP), BF16)], axis=1)
        grads = {0: grad[:, :128], 128: tail}
        keys = k[span, :].T
        dv = {0: 0.0, 128: 0.0}
        dk = {0: 0.0, 128: 0.0}
        for head, tile, lane in group_heads():
            cols = slice(tile, tile + 128)
            low = prob_in[window * GROUP_HEADS + head]
            prob = low.astype(F32)
            weighted = prob * nt(head_only(v[span, cols], lane), grads[tile])
            ds = (weighted - prob * column_sum(weighted)).astype(BF16)
            dv[tile] = dv[tile] + nn(low, head_only(grads[tile], lane))
            dk[tile] = dk[tile] + nn(ds, head_only(q[span, cols], lane))
            rows_out = slice(head * HEAD_DIM, (head + 1) * HEAD_DIM)
            dq_turned[rows_out, span] = nn(keys[rows_out], ds)
        padded = jnp.concatenate([dq_turned[:, span], jnp.zeros((WIDE - GROUP, SEQ), F32)], axis=0).T
        for tile in (0, 128):
            cols = slice(tile, tile + 128)
            piece = dk[tile] * SCALE
            dk_out[span, cols] = (piece * cos[...] - swapped(piece) * sin[...]).astype(BF16)
            piece = padded[:, cols] * SCALE
            dq_out[span, cols] = (piece * cos[...] - swapped(piece) * sin[...]).astype(BF16)
            dv_out[span, cols] = dv[tile].astype(BF16)
    first, second = halves(place)
    bias[...] = jnp.zeros((8, WIDE), F32)
    for part, out in ((0, dq_out), (1, dk_out), (2, dv_out)):
        values = out[...]
        stage[...] = tn(values, hidden[...]).astype(BF16)
        mine[part] = stage[pl.ds(first, HALF), :]
        other[part] = stage[pl.ds(second, HALF), :]
        bias[part : part + 1, :] = column_sum(values.astype(F32))
    mine[3] = out_mine[which]
    other[3] = out_other[which]


def attention_backward(which, place, grad_mixed, q, k, v, prob, hidden, cos, sin, out_mine, out_other):
    rows = hidden.shape[0]
    outs = [shape((rows, WIDE))] * 3 + [shape((4, HALF, D))] * 2 + [shape((8, WIDE), F32)]
    return call(
        functools.partial(attention_backward_kernel, which), "attention_backward", outs, place,
        (grad_mixed, q, k, v, prob, hidden, cos, sin, out_mine, out_other), 12 * rows * D * GROUP,
        [pltpu.VMEM((GROUP, rows), F32), pltpu.VMEM((WIDE, D), BF16)],
    )


def first_backward_kernel(place, tokens, grad_middle, vectors, *refs):
    parts, weights = refs[:12], refs[12:16]
    input_grad, sums = refs[16:]
    grad = 0.0
    for which in range(GROUPS):
        for part in range(3):
            grad = grad + nn(parts[which * 3 + part][...], weights[which][part])
    scaled, scale = normalize(tokens[...].astype(F32))
    input_grad[...] = (grad_middle[...] + norm_back(grad, scaled, scale, vectors[0:1, :])).astype(BF16)
    sums[0:1, :] = column_sum(grad * scaled)
    sums[1:2, :] = column_sum(grad)
    sums[2:8, :] = jnp.zeros((6, D), F32)


def first_backward(place, tokens, grad_middle, vectors, parts, weights):
    rows = tokens.shape[0]
    outs = [shape((rows, D)), shape((8, D), F32)]
    return call(
        first_backward_kernel, "first_backward", outs, place, (tokens, grad_middle, vectors, *parts, *weights),
        24 * rows * D * GROUP,
    )


def pick(array, index):
    return lax.dynamic_index_in_dim(array, index, 0, keepdims=False)


def adamw(weight, first_moment, second_moment, gradient, rate_value):
    first_new = 0.9 * first_moment + 0.1 * gradient
    second_new = 0.999 * second_moment + 0.001 * gradient * gradient
    corrected = first_new / (1.0 - 0.9**STEP) / (jnp.sqrt(second_new / (1.0 - 0.999**STEP)) + 1e-08)
    return (second_new, weight - rate_value * (corrected + 0.01 * weight))


class Layout:
    def __init__(self, total):
        self.total = total
        self.block = 4 * D // total
        self.stride = total // 4
        self.me = lax.axis_index(AXES)
        self.core = lax.rem(self.me, 2)

    def swap(self, value, mask):
        return lax.ppermute(value, AXES, [(i, i ^ mask) for i in range(self.total)])

    def shift(self, value, steps):
        pairs = [(i, (i + self.stride * steps) % self.total) for i in range(self.total)]
        return lax.ppermute(value, AXES, pairs)


class Ring(Layout):
    def __init__(self, total):
        super().__init__(total)
        self.z = self.me // 8
        self.plane = lax.rem(self.me // 2, 4)
        self.place = (self.z, self.core, self.plane)

    def along_z(self, value):
        return jnp.stack([value] + [self.shift(value, -s) for s in (1, 2, 3)])

    def in_plane(self, value):
        return [value] + [self.swap(value, 2 * r) for r in (1, 2, 3)]

    def gather(self, attn, up, down):
        line = self.along_z(attn)
        mine = self.in_plane(line)
        other = [self.swap(value, 1) for value in mine]
        up, down = lax.optimization_barrier((up, down, line))[:2]
        up, down = self.along_z(up), self.along_z(down)
        ups = self.in_plane(lax.optimization_barrier((up, mine))[0])
        downs = self.in_plane(lax.optimization_barrier((down, ups))[0])
        return mine, other, [u.reshape(QUARTER, D) for u in ups], [d.reshape(QUARTER, D) for d in downs]

    def hidden_index(self):
        order = jnp.arange(16)
        place = lax.rem(self.z + lax.rem(order, 4), 4) * 4 + (self.plane ^ (order // 4))
        return place * 2 + self.core

    def scatter(self, parts):
        total = parts[0].astype(F32)
        for r in (1, 2, 3):
            total = total + self.swap(parts[r], 2 * r).astype(F32)
        low = total.astype(BF16)
        out = total[0]
        for s in (1, 2, 3):
            out = out + self.shift(low[s], s).astype(F32)
        return out

    def scatter_hidden(self, grads):
        return self.scatter([grad.reshape(4, -1, D) for grad in grads])

    def scatter_attention(self, mine, other):
        total, swapped_in = 0.0, {}
        for r in (3, 2, 1, 0):
            summed = mine[r].astype(F32) + self.swap(other[r], 1).astype(F32)
            if r:
                summed = self.swap(summed.astype(BF16), 2 * r).astype(F32)
            total = total + summed
        low = total.astype(BF16)
        out = pick(total, self.z)
        for s in (1, 2, 3):
            out = out + self.shift(pick(low, lax.rem(self.z + s, 4)), s).astype(F32)
        return out

    def all_sum(self, value):
        value = value + self.swap(value, 1)
        pair = value + self.swap(value, 2)
        value = pair + self.swap(pair, 4)
        line = self.along_z(value)
        return sum(pick(line, lax.rem(place + 4 - self.z, 4)) for place in range(4))


class Whole(Layout):
    def __init__(self, total):
        super().__init__(total)
        self.plane = jnp.int32(0)
        self.place = (jnp.int32(0),) * 3

    def gather_hidden(self, shard):
        full = lax.all_gather(shard, AXES, axis=0).reshape(self.total // 2, 2, -1, D)
        half = lax.dynamic_index_in_dim(full, self.core, 1, keepdims=False).reshape(4, QUARTER, D)
        return [half[r] for r in range(4)]

    def gather(self, attn, up, down):
        full = lax.all_gather(attn, AXES, axis=0, tiled=True).reshape(4, 4, 2, HALF, D)
        mine = [full[:, r, 0] for r in range(4)]
        other = [full[:, r, 1] for r in range(4)]
        return mine, other, self.gather_hidden(up), self.gather_hidden(down)

    def hidden_index(self):
        return jnp.arange(self.total // 2) * 2 + self.core

    def scatter_hidden(self, grads):
        halves_in = jnp.concatenate(grads).astype(F32).reshape(self.total // 2, 1, -1, D)
        full = jnp.where(jnp.arange(2)[None, :, None, None] == self.core, halves_in, 0.0)
        return lax.psum_scatter(full.reshape(-1, D), AXES, scatter_dimension=0, tiled=True)

    def scatter_attention(self, mine, other):
        full = jnp.stack([jnp.stack(mine, axis=1), jnp.stack(other, axis=1)], axis=2)
        return lax.psum_scatter(full.astype(F32).reshape(4 * D, D), AXES, scatter_dimension=0, tiled=True)

    def all_sum(self, value):
        return lax.psum(value, AXES)


def per_device(
    total,
    tokens,
    cotangent,
    lengths,
    offsets,
    attn_weight,
    attn_first,
    attn_second,
    up_weight,
    up_first,
    up_second,
    down_weight,
    down_first,
    down_second,
    vectors,
    vec_first,
    vec_second,
):
    lay = Ring(total) if total == 32 else Whole(total)
    counts = jnp.minimum(lengths - offsets, SEQ).reshape(-1)
    rows = counts.shape[0] * SEQ
    place = jnp.concatenate([jnp.stack(lay.place).astype(jnp.int32), counts])
    cos, sin = rope_tables()

    mine, other, ups, downs = lay.gather(
        attn_weight.T.astype(BF16), up_weight.T.astype(BF16), down_weight.T.astype(BF16)
    )

    flat = tokens.reshape(rows, D)
    back = cotangent.reshape(rows, D)
    back_pair = lay.swap(back, 1)
    (hidden,) = call(first_norm_kernel, "first_norm", [shape((rows, D))], place, (flat, vectors), 0)

    bias = jnp.pad(vectors[2:5].reshape(3, GROUPS, GROUP).transpose(1, 0, 2), ((0, 0), (0, 0), (0, WIDE - GROUP)))
    forward = [attention_forward(r, place, hidden, mine[r], other[r], bias, cos, sin) for r in range(GROUPS)]
    weights = [group[0] for group in forward]
    middle, normed, mixed, out_weight = middle_layer(
        place, flat, vectors, [group[6] for group in forward], [group[1] for group in forward]
    )

    normed_pair = lay.swap(normed, 1)
    units = lay.hidden_index()
    chosen = (units[:, None] == jnp.arange(total)[None, :]).astype(F32)
    bias_up = jnp.dot(chosen, vectors[9:].reshape(total, lay.block), precision=lax.Precision.HIGHEST)
    bias_up = bias_up.reshape(4, 1, QUARTER)
    active, slope, grad_down = zip(
        *[hidden_forward(place, ups[r], bias_up[r], normed, normed_pair, back, back_pair) for r in range(4)]
    )
    grad_pre, grad_up, grad_bias_up = zip(
        *[hidden_backward(place, downs[r], slope[r], normed, normed_pair, back, back_pair) for r in range(4)]
    )
    grad_down = lay.scatter_hidden(grad_down)
    grad_up = lay.scatter_hidden(grad_up)
    own, pair = project(place, "grad_normed", grad_pre, ups)
    grad_middle, sums, grad_mixed, out_mine, out_other = middle_backward(
        place, own, lay.swap(pair, 1), middle, back, vectors, mixed, out_weight
    )
    backward = {}
    for r in (3, 2, 1, 0):
        _, _, q, k, v, prob, _ = forward[r]
        backward[r] = attention_backward(
            r, place, grad_mixed, q, k, v, prob, hidden, cos, sin, out_mine, out_other
        )
    backward = [backward[r] for r in range(GROUPS)]
    grad_attn = lay.scatter_attention([group[3] for group in backward], [group[4] for group in backward])
    parts = [value for group in backward for value in group[:3]]
    input_grad, first_sums = first_backward(place, flat, grad_middle, vectors, parts, weights)

    own, pair = project(place, "output", active, downs)
    result = (middle + own + lay.swap(pair, 1).astype(F32) + vectors[8]).astype(BF16)

    grad_bias = jnp.stack([group[5][:3, :GROUP] for group in backward])
    grad_bias = jnp.concatenate([pick(grad_bias, lay.plane ^ r) for r in range(GROUPS)], axis=1)
    grad_bias_up = jnp.stack([value[0] for value in grad_bias_up]).reshape(total // 2, lay.block)
    grad_bias_up = jnp.dot(chosen.T, grad_bias_up, precision=lax.Precision.HIGHEST).reshape(4, D)
    grad_vec = lay.all_sum(jnp.concatenate([first_sums[:2], grad_bias, sums[:4], grad_bias_up]))

    grad_attn, grad_up, grad_down = grad_attn.T, grad_up.T, grad_down.T
    attn_second_new, attn_new = adamw(attn_weight, attn_first, attn_second, grad_attn, 0.1)
    up_second_new, up_new = adamw(up_weight, up_first, up_second, grad_up, 0.1)
    down_second_new, down_new = adamw(down_weight, down_first, down_second, grad_down, 0.1)
    vec_second_new, vectors_new = adamw(vectors, vec_first, vec_second, grad_vec, 0.5)
    return (
        result.reshape(tokens.shape),
        input_grad.reshape(tokens.shape),
        grad_attn,
        grad_up,
        grad_down,
        grad_vec,
        attn_second_new,
        up_second_new,
        down_second_new,
        vec_second_new,
        attn_new,
        up_new,
        down_new,
        vectors_new,
    )


def solution(mesh):
    total = mesh.shape["wide"] * mesh.shape["narrow"]
    windows = P(None, AXES, None, None)
    counts = P(None, AXES)
    columns = P(None, AXES)
    in_specs = (windows,) * 2 + (counts,) * 2 + (columns,) * 9 + (P(),) * 3
    out_specs = (windows,) * 2 + (columns,) * 3 + (P(),) + (columns,) * 3 + (P(),) + (columns,) * 3 + (P(),)
    return jax.shard_map(
        functools.partial(per_device, total),
        mesh=mesh,
        in_specs=in_specs,
        out_specs=out_specs,
        check_vma=False,
    )
```

```python
import functools
import math

import jax
import jax.numpy as jnp
from jax import lax
from jax.experimental import pallas as pl
from jax.experimental.pallas import tpu as pltpu
from jax.sharding import PartitionSpec as P

D = 640
HEADS = 20
HEAD_DIM = 32
FF = 2560
SEQ = 256
STEP = 10
AXES = ("wide", "narrow")
GROUPS = 4
GROUP_HEADS = HEADS // GROUPS
GROUP = GROUP_HEADS * HEAD_DIM
HALF = GROUP // 2
WIDE = 256
QUARTER = FF // 8
SCALE = HEAD_DIM ** (-0.5)
BF16 = jnp.bfloat16
F32 = jnp.float32
PACE = 1.15e9
MARGIN = 6 * 1024 * 1024


def nt(left, right):
    return lax.dot_general(left, right, (((1,), (1,)), ((), ())), preferred_element_type=F32)


def nn(left, right):
    return jnp.dot(left, right, preferred_element_type=F32)


def tn(left, right):
    return lax.dot_general(left, right, (((0,), (0,)), ((), ())), preferred_element_type=F32)


def shape(dims, kind=BF16):
    return jax.ShapeDtypeStruct(dims, kind)


class Kept:
    def __init__(self, dims, kind=BF16):
        self.struct = shape(dims, kind)


class Far:
    def __init__(self, value):
        self.value = value


def call(kernel, name, outs, place, args, micros, scratch=(), after=(), copies=None):
    kept = [place_of for place_of, out in enumerate(outs) if isinstance(out, Kept)]
    outs = [out.struct if isinstance(out, Kept) else out for out in outs]
    far = [place_of for place_of, arg in enumerate(args) if isinstance(arg, Far)]
    args = [
        pltpu.with_memory_space_constraint(arg.value, pltpu.HBM) if isinstance(arg, Far) else arg for arg in args
    ]
    buffers = [pltpu.VMEM(a.shape, a.dtype) for a in [outs[k] for k in kept] + [args[k] for k in far]]
    copies = copies or len(kept)
    size = sum(a.size * a.dtype.itemsize for a in args) + sum(o.size * o.dtype.itemsize for o in outs)
    extra = sum(math.prod(s.shape) * s.dtype.itemsize for s in scratch)
    semaphores = [pltpu.SemaphoreType.DMA((copies + len(far),))] if buffers else []

    def body(place_ref, *refs):
        ins, refs = list(refs[: len(args)]), refs[len(args) + len(after) :]
        out_refs, refs = list(refs[: len(outs)]), refs[len(outs) :]
        work, held = refs[: len(scratch)], refs[len(scratch) : len(scratch) + len(buffers)]
        started, targets, coming = [], [], []
        for slot, (k, buffer) in enumerate(zip(far, held[len(kept) :])):
            copy = pltpu.make_async_copy(ins[k], buffer, refs[-1].at[copies + slot])
            copy.start()
            coming.append((buffer, copy))
            ins[k] = buffer
        for k, buffer in zip(kept, held):
            targets.append((buffer, out_refs[k]))
            out_refs[k] = buffer

        def flush(ref, index=None):
            target = next(out for buffer, out in targets if buffer is ref)
            if index is not None:
                ref, target = ref.at[index], target.at[index]
            copy = pltpu.make_async_copy(ref, target, refs[-1].at[len(started)])
            copy.start()
            started.append(copy)

        def fetch(ref):
            next(copy for buffer, copy in coming if buffer is ref).wait()
            return ref

        kernel(place_ref, (flush, fetch), *ins, *out_refs, *work)
        for copy in started:
            copy.wait()

    def spec(space):
        return pl.BlockSpec(memory_space=space)

    return list(pl.pallas_call(
        body,
        out_shape=tuple(pltpu.HBM(o.shape, o.dtype) if k in kept else o for k, o in enumerate(outs)),
        in_specs=[spec(pltpu.SMEM)]
        + [spec(pl.ANY if k in far else pltpu.VMEM) for k in range(len(args))]
        + [spec(pl.ANY)] * len(after),
        out_specs=tuple(spec(pltpu.HBM if k in kept else pltpu.VMEM) for k in range(len(outs))),
        scratch_shapes=list(scratch) + buffers + semaphores,
        compiler_params=pltpu.CompilerParams(vmem_limit_bytes=size + extra + MARGIN),
        cost_estimate=pl.CostEstimate(flops=int(micros * PACE), bytes_accessed=size, transcendentals=0),
        name=name,
    )(place, *args, *after))


def normalize(rows):
    centered = rows - jnp.mean(rows, axis=-1, keepdims=True)
    scale = lax.rsqrt(jnp.mean(centered * centered, axis=-1, keepdims=True) + 1e-05)
    return centered * scale, scale


def norm_back(grad, scaled, scale, gain):
    weighted = grad * gain
    mean_one = jnp.mean(weighted, axis=-1, keepdims=True)
    mean_two = jnp.mean(weighted * scaled, axis=-1, keepdims=True)
    return scale * (weighted - mean_one - scaled * mean_two)


def column_sum(rows):
    return jnp.sum(rows, axis=0, keepdims=True)


def rope_tables():
    position = jnp.arange(SEQ, dtype=F32)
    frequency = 10000.0 ** (-jnp.arange(0, HEAD_DIM, 2, dtype=F32) / HEAD_DIM)
    angles = position[:, None] * frequency[None, :]
    cos, sin = jnp.cos(angles), jnp.sin(angles)
    return jnp.tile(cos, (1, 8)), jnp.tile(jnp.concatenate([-sin, sin], axis=1), (1, 4))


def swapped(rows):
    low = lax.broadcasted_iota(jnp.int32, rows.shape, 1) % HEAD_DIM < HEAD_DIM // 2
    return jnp.where(low, pltpu.roll(rows, 128 - HEAD_DIM // 2, 1), pltpu.roll(rows, HEAD_DIM // 2, 1))


def group_heads():
    for head in range(GROUP_HEADS):
        yield head, (head // 4) * 128, head % 4


def head_only(rows, lane):
    owner = lax.broadcasted_iota(jnp.int32, rows.shape, 1) // HEAD_DIM
    return jnp.where(owner == lane, rows, jnp.zeros_like(rows))


def halves(place):
    core = place[1]
    return pl.multiple_of(core * HALF, 16), pl.multiple_of((1 - core) * HALF, 16)


def first_norm_kernel(place, move, tokens, vectors, hidden):
    scaled, _ = normalize(tokens[...].astype(F32))
    hidden[...] = (scaled * vectors[0:1, :] + vectors[1:2, :]).astype(BF16)


def stack_into(out, parts):
    for source, part in enumerate(parts):
        out[source] = part[...]


def line_kernel(place, move, *refs):
    stack_into(refs[6], refs[:4])
    stack_into(refs[7], refs[4:6])


def make_line(place, parts, pair, after):
    outs = [shape((4, *parts[0].shape)), shape((2, *pair[0].shape))]
    return call(line_kernel, "line", outs, place, (*parts, *pair), 0.7, after=after)


def pack_kernel(place, move, *refs):
    groups, pairs, (packed, ups, downs) = refs[:3], refs[3:5], refs[5:]
    stack_into(packed, groups)
    rows = ups.shape[1]
    for source in range(4):
        shard = pairs[source // 2][source % 2]
        ups[source] = shard[:rows]
        downs[source] = shard[rows:]


def pack(place, groups, pairs, after):
    outs = [shape((3, *groups[0].shape))] + [shape((4, pairs[0].shape[1] // 2, D))] * 2
    return call(pack_kernel, "pack", outs, place, (*groups, *pairs), 1.0, after=after)


def attention_forward_kernel(groups, place, move, hidden, bias, cos, sin, *refs):
    flush, fetch = move
    count = len(groups)
    mine, other, *refs = refs
    weights, weights_out, qs, ks, vs, probs, mixed = [refs[part * count : (part + 1) * count] for part in range(7)]
    z = place[0]
    first, second = halves(place)
    rows = hidden[...]
    windows = rows.shape[0] // SEQ
    for step, which in enumerate(groups):
        weight, prob_out = weights[step], probs[step]
        group = place[2] ^ which
        for part in range(4):
            source = lax.rem(part + 4 - z, 4)
            pieces = mine[step, source], other[step, source]
            for offset, piece in zip((first, second), pieces):
                if part < 3:
                    weight[part, pl.ds(offset, HALF), :] = piece
                else:
                    weights_out[step][pl.ds(offset, HALF), :] = piece
            if part < 3:
                weight[part, GROUP:WIDE, :] = jnp.zeros((WIDE - GROUP, D), BF16)
        flush(weight)
        for part, out in ((0, qs[step]), (1, ks[step]), (2, vs[step])):
            proj = nt(rows, weight[part]) + bias[group, part : part + 1, :]
            for window in range(windows):
                span = slice(window * SEQ, (window + 1) * SEQ)
                for tile in (0, 128):
                    piece = proj[span, tile : tile + 128]
                    if part < 2:
                        piece = piece * cos[...] + swapped(piece) * sin[...]
                    out[span, tile : tile + 128] = piece.astype(BF16)
            flush(out)
        for window in range(windows):
            span = slice(window * SEQ, (window + 1) * SEQ)
            visible = lax.broadcasted_iota(jnp.int32, (SEQ, 1), 0) < place[4 + window]
            values = vs[step][span, :].T
            for head, tile, lane in group_heads():
                keys = head_only(ks[step][span, tile : tile + 128], lane)
                scores = nt(keys, qs[step][span, tile : tile + 128])
                scores = jnp.where(visible, scores, -1e30)
                top = jnp.max(scores, axis=0, keepdims=True)
                exponent = jnp.exp((scores - top) * SCALE)
                prob = (exponent * (1.0 / column_sum(exponent))).astype(BF16)
                prob_out[window * GROUP_HEADS + head] = prob
                flush(prob_out, window * GROUP_HEADS + head)
                rows_out = slice(head * HEAD_DIM, (head + 1) * HEAD_DIM)
                mixed[step][rows_out, span] = nn(values[rows_out], prob).astype(BF16)


def attention_forward(groups, place, hidden, bias, cos, sin, mine, other, after):
    rows = hidden.shape[0]
    maps = rows // SEQ * GROUP_HEADS
    count = len(groups)
    kinds = [Kept((3, WIDE, D)), shape((GROUP, D))] + [Kept((rows, WIDE))] * 3
    kinds += [Kept((maps, SEQ, SEQ)), shape((GROUP, rows))]
    out = call(
        functools.partial(attention_forward_kernel, groups), "attention_forward",
        [kind for kind in kinds for _ in groups], place, (hidden, bias, cos, sin, mine, other), 4.8 * count,
        after=after, copies=count * (4 + maps),
    )
    return [out[step::count] for step in range(count)]


def middle_kernel(place, move, tokens, vectors, *refs):
    flush, fetch = move
    mixed_in, weight_in, *refs = refs[:4], refs[4:8], *refs[8:]
    middle, normed, mixed, weight, stage = refs
    for which in range(GROUPS):
        offset = pl.multiple_of((place[2] ^ which) * GROUP, 32)
        stage[pl.ds(offset, GROUP), :] = mixed_in[which][...]
        weight[pl.ds(offset, GROUP), :] = weight_in[which][...]
    mixed[...] = stage[...].T
    flush(weight)
    flush(mixed)
    rows = tokens[...].astype(F32) + nt(mixed[...], weight[...]) + vectors[5:6, :]
    middle[...] = rows
    flush(middle)
    scaled, _ = normalize(rows)
    normed[...] = (scaled * vectors[6:7, :] + vectors[7:8, :]).astype(BF16)


def middle_layer(place, tokens, vectors, mixed, weights, after):
    rows = tokens.shape[0]
    outs = [Kept((rows, D), F32), shape((rows, D)), Kept((rows, D)), Kept((D, D))]
    return call(
        middle_kernel, "middle", outs, place, (tokens, vectors, *mixed, *weights), 2.5,
        [pltpu.VMEM((D, rows), BF16)], after,
    )


def quarter(parts, which):
    if which < 3:
        return parts[which][...]
    return jnp.concatenate([parts[3][...], parts[4][...]], axis=0)


def hidden_forward_kernel(place, move, *refs):
    flush, fetch = move
    ups, (bias, normed, normed_pair, back, back_pair), refs = refs[:5], refs[5:10], refs[10:]
    active, slopes, grads_down = refs[0], refs[1:5], refs[5:]
    rows = normed.shape[0]
    for which in range(4):
        for part in (which,) if which < 3 else (3, 4):
            fetch(ups[part])
        up = quarter(ups, which)
        column = jnp.broadcast_to(bias[which], (8, QUARTER)).T[:, 0:1]
        total = 0.0
        for part, inputs, grads in ((0, normed, back), (1, normed_pair, back_pair)):
            span = slice(part * rows, (part + 1) * rows)
            pre = nt(up, inputs[...]) + column
            cdf = 0.5 + 0.5 * lax.erf(pre * (0.5**0.5))
            low = (pre * cdf).astype(BF16)
            active[which, :, span] = low
            slopes[which][:, span] = (cdf + pre * jnp.exp(-0.5 * pre * pre) * 0.3989422804014327).astype(BF16)
            total = total + nn(low, grads[...])
        flush(active, which)
        grads_down[which][...] = total.astype(BF16)
        flush(grads_down[which])


def hidden_forward(place, ups, bias, normed, normed_pair, back, back_pair):
    rows = 2 * normed.shape[0]
    outs = [Kept((4, QUARTER, rows))] + [shape((QUARTER, rows))] * 4 + [Kept((QUARTER, D))] * 4
    active, *rest = call(
        hidden_forward_kernel, "hidden_forward", outs, place,
        (*[Far(up) for up in ups], bias, normed, normed_pair, back, back_pair), 7.5, copies=8,
    )
    return active, rest[:4], rest[4:]


def hidden_backward_kernel(place, move, *refs):
    downs, ups, slopes, (back, back_pair), refs = refs[:5], refs[5:10], refs[10:14], refs[14:16], refs[16:]
    grad_pre, own, pair, up = refs
    rows = back.shape[0]
    for down in downs:
        move[1](down)
    for which in range(4):
        units = slice(which * QUARTER, (which + 1) * QUARTER)
        up[units, :] = quarter(ups, which)
        down = quarter(downs, which)
        for part, grads in ((0, back), (1, back_pair)):
            span = slice(part * rows, (part + 1) * rows)
            wide = nt(down, grads[...]) * slopes[which][:, span].astype(F32)
            grad_pre[units, span] = wide.astype(BF16)
    for out, span in ((pair, slice(rows, 2 * rows)), (own, slice(0, rows))):
        out[...] = tn(grad_pre[:, span], up[...]).astype(out.dtype)


def hidden_backward(place, downs, ups, slopes, back, back_pair):
    rows = back.shape[0]
    outs = [shape((4 * QUARTER, 2 * rows)), shape((rows, D), F32), shape((rows, D))]
    return call(
        hidden_backward_kernel, "hidden_backward", outs, place,
        (*[Far(down) for down in downs], *ups, *slopes, back, back_pair), 6.0, [pltpu.VMEM((4 * QUARTER, D), BF16)],
    )


def up_gradient_kernel(place, move, grad_pre, normed, normed_pair, *refs):
    grads, grad_bias = refs[:4], refs[4]
    rows = normed.shape[0]
    for which in range(4):
        units = slice(which * QUARTER, (which + 1) * QUARTER)
        low = grad_pre[units, :]
        grads[which][...] = (nn(low[:, :rows], normed[...]) + nn(low[:, rows:], normed_pair[...])).astype(BF16)
        move[0](grads[which])
        bias = jnp.sum(low.astype(F32), axis=1, keepdims=True)
        for source in range(4):
            grad_bias[4 * which + source] = jnp.broadcast_to(bias[source * 80 : (source + 1) * 80], (80, 8)).T


def up_gradient(place, grad_pre, normed, normed_pair, after):
    outs = [Kept((QUARTER, D))] * 4 + [shape((16, 8, 80), F32)]
    *grads, bias = call(
        up_gradient_kernel, "up_gradient", outs, place, (grad_pre, normed, normed_pair), 4.0, after=after
    )
    return grads, bias


def output_kernel(place, move, active, *refs):
    downs, (own, pair) = refs[:5], refs[5:]
    rows = own.shape[0]
    down = jnp.concatenate([value[...] for value in downs], axis=0)
    for out, span in ((pair, slice(rows, 2 * rows)), (own, slice(0, rows))):
        left = jnp.concatenate([active[which, :, span] for which in range(4)], axis=0)
        out[...] = tn(left, down).astype(out.dtype)


def output_layer(place, active, downs, after):
    rows = active.shape[2] // 2
    outs = [shape((rows, D), F32), shape((rows, D))]
    return call(output_kernel, "output", outs, place, (active, *downs), 3.0, after=after)


def middle_backward_kernel(
    place, move, own, pair, middle, back, vectors, mixed, weight, grad_middle, sums, grad_mixed, mine, other, stage, stage_mixed
):
    grad = own[...] + pair[...].astype(F32)
    scaled, scale = normalize(middle[...])
    wide = back[...].astype(F32)
    total = wide + norm_back(grad, scaled, scale, vectors[6:7, :])
    grad_middle[...] = total
    sums[0:1, :] = column_sum(total)
    sums[1:2, :] = column_sum(grad * scaled)
    sums[2:3, :] = column_sum(grad)
    sums[3:4, :] = column_sum(wide)
    sums[4:8, :] = jnp.zeros((4, D), F32)
    low = total.astype(BF16)
    stage_mixed[...] = nt(weight[...].T, low).astype(BF16)
    stage[...] = tn(low, mixed[...]).astype(BF16)
    first, second = halves(place)
    for which in range(GROUPS):
        offset = (place[2] ^ which) * GROUP
        grad_mixed[which] = stage_mixed[pl.ds(pl.multiple_of(offset, 32), GROUP), :]
        mine[which] = stage[pl.ds(pl.multiple_of(offset + first, 16), HALF), :]
        other[which] = stage[pl.ds(pl.multiple_of(offset + second, 16), HALF), :]


def middle_backward(place, own, pair, middle, back, vectors, mixed, weight, after):
    rows = own.shape[0]
    outs = [shape((rows, D), F32), shape((8, D), F32), shape((GROUPS, GROUP, rows))]
    outs += [shape((GROUPS, HALF, D)), shape((GROUPS, HALF, D))]
    return call(
        middle_backward_kernel, "middle_backward", outs, place,
        (own, pair, middle, back, vectors, mixed, weight), 3.0,
        [pltpu.VMEM((D, D), BF16), pltpu.VMEM((D, rows), BF16)], after,
    )


def attention_backward_kernel(
    which, place, move, grad_mixed, q, k, v, prob_in, hidden, cos, sin, out_mine, out_other,
    dq_out, dk_out, dv_out, mine, other, bias, dq_turned, stage,
):
    rows = hidden.shape[0]
    for window in range(rows // SEQ):
        span = slice(window * SEQ, (window + 1) * SEQ)
        grad = grad_mixed[which, :, span].T
        tail = jnp.concatenate([grad[:, 128:GROUP], jnp.zeros((SEQ, WIDE - GROUP), BF16)], axis=1)
        grads = {0: grad[:, :128], 128: tail}
        keys = k[span, :].T
        dv = {0: 0.0, 128: 0.0}
        dk = {0: 0.0, 128: 0.0}
        for head, tile, lane in group_heads():
            cols = slice(tile, tile + 128)
            low = prob_in[window * GROUP_HEADS + head]
            prob = low.astype(F32)
            weighted = prob * nt(head_only(v[span, cols], lane), grads[tile])
            ds = (weighted - prob * column_sum(weighted)).astype(BF16)
            dv[tile] = dv[tile] + nn(low, head_only(grads[tile], lane))
            dk[tile] = dk[tile] + nn(ds, head_only(q[span, cols], lane))
            rows_out = slice(head * HEAD_DIM, (head + 1) * HEAD_DIM)
            dq_turned[rows_out, span] = nn(keys[rows_out], ds)
        padded = jnp.concatenate([dq_turned[:, span], jnp.zeros((WIDE - GROUP, SEQ), F32)], axis=0).T
        for tile in (0, 128):
            cols = slice(tile, tile + 128)
            piece = dk[tile] * SCALE
            dk_out[span, cols] = (piece * cos[...] - swapped(piece) * sin[...]).astype(BF16)
            piece = padded[:, cols] * SCALE
            dq_out[span, cols] = (piece * cos[...] - swapped(piece) * sin[...]).astype(BF16)
            dv_out[span, cols] = dv[tile].astype(BF16)
    first, second = halves(place)
    bias[...] = jnp.zeros((8, WIDE), F32)
    for part, out in ((0, dq_out), (1, dk_out), (2, dv_out)):
        values = out[...]
        stage[...] = tn(values, hidden[...]).astype(BF16)
        mine[part] = stage[pl.ds(first, HALF), :]
        other[part] = stage[pl.ds(second, HALF), :]
        bias[part : part + 1, :] = column_sum(values.astype(F32))
    mine[3] = out_mine[which]
    other[3] = out_other[which]


def attention_backward(which, place, grad_mixed, q, k, v, prob, hidden, cos, sin, out_mine, out_other, after):
    rows = hidden.shape[0]
    outs = [shape((rows, WIDE))] * 3 + [shape((4, HALF, D))] * 2 + [shape((8, WIDE), F32)]
    return call(
        functools.partial(attention_backward_kernel, which), "attention_backward", outs, place,
        (grad_mixed, q, k, v, prob, hidden, cos, sin, out_mine, out_other), 1.5,
        [pltpu.VMEM((GROUP, rows), F32), pltpu.VMEM((WIDE, D), BF16)], after,
    )


def first_backward_kernel(place, move, tokens, grad_middle, vectors, *refs):
    parts, weights, biases, (middle_sums, units), refs = refs[:12], refs[12:16], refs[16:20], refs[20:22], refs[22:]
    input_grad, sums, unit_rows = refs
    z, plane, core = place[0], place[2], place[3]
    grad = 0.0
    for which in range(GROUPS):
        for part in range(3):
            grad = grad + nn(parts[which * 3 + part][...], weights[which][part])
    scaled, scale = normalize(tokens[...].astype(F32))
    input_grad[...] = (grad_middle[...] + norm_back(grad, scaled, scale, vectors[0:1, :])).astype(BF16)
    sums[...] = jnp.zeros((24, D), F32)
    sums[0:1, :] = column_sum(grad * scaled)
    sums[1:2, :] = column_sum(grad)
    sums[2:6, :] = middle_sums[0:4, :]
    for group in range(GROUPS):
        value = sum(jnp.where((plane ^ which) == group, biases[which][...], 0.0) for which in range(GROUPS))
        row, column = 8 + 4 * (group // 2), WIDE * (group % 2)
        sums[row : row + 4, column : column + WIDE] = value[0:4]
    unit_rows[...] = jnp.zeros((4, 8, 128), F32)
    for which in range(4):
        for source in range(4):
            row = (plane ^ which) * 2 + core
            unit_rows[z ^ source, pl.ds(row, 1), 0:80] = units[4 * which + source, 0:1, :]
    for line in range(4):
        sums[16:24, line * 128 : (line + 1) * 128] = unit_rows[line]


def first_backward(place, tokens, grad_middle, vectors, parts, weights, biases, middle_sums, units, after):
    rows = tokens.shape[0]
    outs = [shape((rows, D)), shape((24, D), F32)]
    return call(
        first_backward_kernel, "first_backward", outs, place,
        (tokens, grad_middle, vectors, *parts, *weights, *biases, middle_sums, units),
        4.8, [pltpu.VMEM((4, 8, 128), F32)], after,
    )


def unpack_vector(sums):
    group_rows = [sums[8 + 4 * (g // 2) :, WIDE * (g % 2) :][:3, :GROUP] for g in range(GROUPS)]
    units = sums[16:24, :512].reshape(8, 4, 128)[:, :, :80].transpose(1, 0, 2).reshape(4, D)
    return jnp.concatenate([sums[0:2], jnp.concatenate(group_rows, axis=1), sums[2:6], units])


def ordered_sum_kernel(which, place, move, *refs):
    total = 0.0
    for index in range(4):
        total = total + sum(jnp.where((place[which] ^ step) == index, refs[step][...], 0.0) for step in range(4))
    refs[4][...] = total


def ordered_sum(place, which, parts, after=()):
    outs = [shape(parts[0].shape, F32)]
    return call(functools.partial(ordered_sum_kernel, which), "ordered_sum", outs, place, parts, 0.6, after=after)[0]


def plane_sum_kernel(turned, count, place, move, *refs):
    parts, refs = refs[:count], refs[count:]
    rest = (len(refs) - 5) // 2
    (own, *sent), stage = refs[rest : rest + 4], refs[-1]
    stage[...] = sum(value[...].astype(F32) for value in parts)
    for steps, out in enumerate((own, *sent)):
        out[...] = stage[lax.rem(place[0] + steps, 4) if turned else steps].astype(out.dtype)
    for source in range(rest):
        refs[rest + 4 + source][...] = refs[source][...]


def plane_sum(turned, place, parts, after=(), rest=()):
    dims = parts[0].shape
    outs = [shape(dims[1:], F32)] + [shape(dims[1:])] * 3 + [shape(value.shape, value.dtype) for value in rest]
    return call(
        functools.partial(plane_sum_kernel, turned, len(parts)), "plane_sum", outs, place, (*parts, *rest), 1.0,
        [pltpu.VMEM(dims, F32)], after,
    )


def merge_kernel(place, move, along_y, along_x, first, second, out_y, out_x):
    out_y[0:2] = along_y[0:2]
    out_y[2:4] = (along_y[2:4].astype(F32) + second[...].astype(F32)).astype(BF16)
    out_x[0:2] = (along_x[0:2].astype(F32) + first[...].astype(F32)).astype(BF16)
    out_x[2:4] = along_x[2:4]


def merge(place, along_y, along_x, first, second, after):
    outs = [shape(along_y.shape)] * 2
    return call(merge_kernel, "merge", outs, place, (along_y, along_x, first, second), 0.7, after=after)


def cores_sum_kernel(where, place, move, mine, other, *refs):
    total = mine[...].astype(F32) + other[...].astype(F32)
    if where is None:
        for out in refs:
            base = 0 if out is refs[0] else 2
            out[...] = total[base : base + 2].astype(BF16)
    else:
        half, out = refs
        out[2 - where : 4 - where] = total[2 - where : 4 - where].astype(BF16)
        out[where : where + 2] = (total[where : where + 2] + half[...].astype(F32)).astype(BF16)


def cores_sum(where, place, mine, other, half, after):
    dims = mine.shape
    outs = [shape((2, *dims[1:]))] * 2 if where is None else [shape(dims)]
    return call(
        functools.partial(cores_sum_kernel, where), "cores_sum", outs, place, (mine, other, *half), 0.7, after=after
    )


def core_runs(place):
    for which in range(4):
        for source in range(4):
            run = ((place[0] ^ source) * 4 + (place[2] ^ which)) * 2 + place[3]
            yield which, source, pl.ds(pl.multiple_of(run * 80, 16), 80)


def take_runs_kernel(place, move, full, *outs):
    for which, source, rows in core_runs(place):
        part, offset = (which, source) if which < 3 else (3 + source // 2, source % 2)
        outs[part][offset * 80 : (offset + 1) * 80, :] = full[rows, :]


def take_runs(place, full):
    outs = [shape((QUARTER, D))] * 3 + [shape((QUARTER // 2, D))] * 2
    return call(take_runs_kernel, "take_runs", outs, place, (full,), 1.0)


def place_runs_kernel(place, move, *refs):
    full = refs[4]
    full[...] = jnp.zeros_like(full)
    for which, source, rows in core_runs(place):
        full[rows, :] = refs[which][source * 80 : (source + 1) * 80, :].astype(F32)


def place_runs(place, quarters):
    return call(place_runs_kernel, "place_runs", [shape((FF, D), F32)], place, quarters, 2.0)[0]


def pick(array, index):
    return lax.dynamic_index_in_dim(array, index, 0, keepdims=False)


def finish_kernel(rate, place, move, own, one, two, three, weight, first, second, grad, second_new, new):
    for ref in (weight, first, second):
        move[1](ref)
    total = own[...]
    for value in (one, two, three):
        total = total + value[...].astype(F32)
    grad[...] = total
    second_new[...], new[...] = adamw(weight[...], first[...], second[...], total, rate)


def finish(place, rate, own, line, weight, first, second, after=()):
    out = call(
        functools.partial(finish_kernel, rate), "finish", [shape(own.shape, F32)] * 3, place,
        (own, *line, Far(weight.T), Far(first.T), Far(second.T)), 1.5, after=after,
    )
    return [value.T for value in out]


def adamw(weight, first_moment, second_moment, gradient, rate_value):
    first_new = 0.9 * first_moment + 0.1 * gradient
    second_new = 0.999 * second_moment + 0.001 * gradient * gradient
    corrected = first_new / (1.0 - 0.9**STEP) / (jnp.sqrt(second_new / (1.0 - 0.999**STEP)) + 1e-08)
    return (second_new, weight - rate_value * (corrected + 0.01 * weight))


class Layout:
    def __init__(self, total):
        self.total = total
        self.block = 4 * D // total
        self.stride = total // 4
        self.me = lax.axis_index(AXES)
        self.core = lax.rem(self.me, 2)

    def swap(self, value, mask):
        return lax.ppermute(value, AXES, [(i, i ^ mask) for i in range(self.total)])

    def shift(self, value, steps):
        pairs = [(i, (i + self.stride * steps) % self.total) for i in range(self.total)]
        return lax.ppermute(value, AXES, pairs)


    def hidden_index(self):
        order = jnp.arange(16)
        z, plane = self.place[0], self.place[2]
        return ((z ^ lax.rem(order, 4)) * 4 + (plane ^ (order // 4))) * 2 + self.core


class Ring(Layout):
    def __init__(self, total):
        super().__init__(total)
        self.ring = True
        self.z = self.me // 8
        self.plane = lax.rem(self.me // 2, 4)
        self.place = (self.z, self.core, self.plane)

    def along_z(self, value):
        return [value] + [self.shift(value, -s) for s in (1, 2, 3)]

    def in_plane(self, value, each=None):
        return [value] + [self.swap(each[r].reshape(value.shape) if each else value, 2 * r) for r in (1, 2, 3)]

    def spread(self, line):
        along_y, along_x = self.swap(line, 2), self.swap(line, 4)
        return [line, along_y, along_x, self.swap(along_x[0:2], 2), self.swap(along_y[2:4], 4)]

    def corner(self, value):
        return [self.swap(value[0:2], 2), self.swap(value[2:4], 4)]

    def send_plane(self, along_y, along_x):
        return [self.swap(along_y, 2), self.swap(along_x, 4)]

    def scatter(self, turned, parts, after=(), rest=()):
        own, one, two, three, *rest = plane_sum(turned, self.vector, parts, after, rest)
        if turned:
            line = [self.shift(value, s) for value, s in ((one, 1), (two, 2), (three, 3))]
        else:
            line = [self.swap(value, 8 * s) for value, s in ((one, 1), (two, 2), (three, 3))]
        return own, line, *rest

    def all_sum(self, value):
        value = ordered_sum(self.vector, 2, self.in_plane(value + self.swap(value, 1)))
        return ordered_sum(self.vector, 0, [value] + [self.swap(value, 8 * s) for s in (1, 2, 3)])


class Whole(Layout):
    def __init__(self, total):
        super().__init__(total)
        self.ring = False
        self.plane = jnp.int32(0)
        self.place = (jnp.int32(0),) * 3

    def gather_core(self, shard):
        return take_runs(self.vector, lax.all_gather(shard, AXES, axis=0, tiled=True))

    def gather(self, attn, up, down):
        full = lax.all_gather(attn, AXES, axis=0, tiled=True).reshape(4, 4, 2, HALF, D)
        mine = [full[:, r, 0] for r in range(4)]
        other = [full[:, r, 1] for r in range(4)]
        return mine, other, self.gather_core(up), self.gather_core(down)

    def scatter_hidden(self, grads):
        return lax.psum_scatter(place_runs(self.vector, grads), AXES, scatter_dimension=0, tiled=True)

    def scatter_attention(self, mine, other):
        full = jnp.stack([jnp.stack(mine, axis=1), jnp.stack(other, axis=1)], axis=2)
        return lax.psum_scatter(full.astype(F32).reshape(4 * D, D), AXES, scatter_dimension=0, tiled=True)

    def all_sum(self, value):
        return lax.psum(value, AXES)


def per_device(
    total,
    tokens,
    cotangent,
    lengths,
    offsets,
    attn_weight,
    attn_first,
    attn_second,
    up_weight,
    up_first,
    up_second,
    down_weight,
    down_first,
    down_second,
    vectors,
    vec_first,
    vec_second,
):
    lay = Ring(total) if total == 32 else Whole(total)
    counts = jnp.minimum(lengths - offsets, SEQ).reshape(-1)
    rows = counts.shape[0] * SEQ
    place = lay.vector = jnp.concatenate([jnp.stack([*lay.place, lay.core]).astype(jnp.int32), counts])
    cos, sin = rope_tables()

    flat = tokens.reshape(rows, D)
    back = cotangent.reshape(rows, D)
    back_pair = lay.swap(back, 1)
    (hidden,) = call(first_norm_kernel, "first_norm", [shape((rows, D))], place, (flat, vectors), 1.0)
    bias = jnp.pad(vectors[2:5].reshape(3, GROUPS, GROUP).transpose(1, 0, 2), ((0, 0), (0, 0), (0, WIDE - GROUP)))

    if lay.ring:
        shards = jnp.concatenate([up_weight.T, down_weight.T]).astype(BF16)
        attn_parts = lay.along_z(attn_weight.T.astype(BF16))
        line, pair = make_line(place, attn_parts, [shards, lay.swap(shards, 8)], [hidden])
        groups = lay.in_plane(line)[1:]
        other = lay.swap(line, 1)
        pairs = pair, lay.swap(pair, 16)
        mine = line[None]
    else:
        mine, other, ups, downs = lay.gather(
            attn_weight.T.astype(BF16), up_weight.T.astype(BF16), down_weight.T.astype(BF16)
        )
        mine, packed = mine[0][None], jnp.stack(mine[1:])
        other, packed_other = other[0], jnp.stack(other[1:])
    forward = attention_forward((0,), place, hidden, bias, cos, sin, mine, other[None], [])
    if lay.ring:
        packed, up_line, down_line = pack(place, groups, pairs, [forward[0][2]])
        ups, downs = [[v.reshape(-1, D) for v in lay.spread(value)] for value in (up_line, down_line)]
        packed_other = lay.swap(packed, 1)
    forward += attention_forward((1, 2, 3), place, hidden, bias, cos, sin, packed, packed_other, [forward[0][2]])
    weights = [group[0] for group in forward]
    middle, normed, mixed, out_weight = middle_layer(
        place, flat, vectors, [group[6] for group in forward], [group[1] for group in forward],
        ups[1:3] + downs[1:3] if lay.ring else [],
    )
    normed_pair = lay.swap(normed, 1)
    units = lay.hidden_index()
    chosen = (units[:, None] == jnp.arange(32)[None, :]).astype(F32)
    bias_up = jnp.dot(chosen, vectors[9:].reshape(32, 80), precision=lax.Precision.HIGHEST)
    both = (normed, normed_pair, back, back_pair)
    active, slope, grad_down = hidden_forward(place, ups, bias_up.reshape(4, 1, QUARTER), *both)
    if lay.ring:
        grad_down = [value.reshape(4, -1, D) for value in grad_down]
        down_corner = lay.corner(grad_down[3])
    grad_pre, own, pair = hidden_backward(place, downs, ups, slope, back, back_pair)
    gradient_after = []
    if lay.ring:
        down_sent = merge(place, *grad_down[1:3], *down_corner, [own])
        gradient_after = down_sent[:1]
        down_sent = lay.send_plane(*down_sent)
    grad_up, grad_bias_up = up_gradient(place, grad_pre, normed, normed_pair, gradient_after)
    if lay.ring:
        grad_up = [value.reshape(4, -1, D) for value in grad_up]
        up_corner = lay.corner(grad_up[3])
    grad_middle, sums, grad_mixed, out_mine, out_other = middle_backward(
        place, own, lay.swap(pair, 1), middle, back, vectors, mixed, out_weight, [grad_bias_up]
    )
    backward, after = {}, []
    for r in (3, 2, 1, 0):
        _, _, q, k, v, prob, _ = forward[r][:7]
        backward[r] = attention_backward(
            r, place, grad_mixed, q, k, v, prob, hidden, cos, sin, out_mine, out_other, after
        )
        after = [backward[r][0]]
        if not lay.ring:
            continue
        mine_r, other_r = backward[r][3], lay.swap(backward[r][4], 1)
        if r == 3:
            up_sent = merge(place, *grad_up[1:3], *up_corner, after)
            after = up_sent[:1] + down_sent
            up_sent = lay.send_plane(*up_sent)
            last = mine_r, other_r
        elif r == 2:
            attn_corner = cores_sum(None, place, *last, [], after)
            after = after + attn_corner[:1]
            attn_corner = [lay.swap(attn_corner[0], 2), lay.swap(attn_corner[1], 4)]
            along_x = mine_r, other_r
        elif r == 1:
            (along_x,) = cores_sum(0, place, *along_x, attn_corner[:1], after)
            after = after + [along_x]
            along_x = lay.swap(along_x, 4)
            along_y = mine_r, other_r
        else:
            (along_y,) = cores_sum(2, place, *along_y, attn_corner[1:], after)
            after = after + [along_y] + up_sent
            along_y = lay.swap(along_y, 2)
            attn_parts = mine_r, other_r, along_y, along_x
    backward = [backward[r] for r in range(GROUPS)]
    if lay.ring:
        grad_down, grad_up = [grad_down[0], *down_sent], [grad_up[0], *up_sent]
        down_own, down_z = lay.scatter(False, grad_down, [backward[2][0]])
    else:
        grad_down, grad_up = lay.scatter_hidden(grad_down), lay.scatter_hidden(grad_up)
        grad_attn = lay.scatter_attention([group[3] for group in backward], [group[4] for group in backward])

    def step(rate, sums_in, *state, after=()):
        if lay.ring:
            return finish(place, rate, *sums_in, *state, after)
        grad = sums_in.T
        return grad, *adamw(*state, grad, rate)

    parts = [value for group in backward for value in group[:3]]
    input_grad, vec_sums = first_backward(
        place, flat, grad_middle, vectors, parts, weights, [group[5] for group in backward], sums, grad_bias_up, after
    )

    late = [input_grad]
    if lay.ring:
        attn_own, attn_z, vec_sums = lay.scatter(True, attn_parts, late + down_z, [vec_sums])
        late = [attn_own]
        up_own, up_z = lay.scatter(False, grad_up, late)
    own, pair = output_layer(place, active, downs, late)
    result = (middle + own + lay.swap(pair, 1).astype(F32) + vectors[8]).astype(BF16)

    grad_vec = unpack_vector(lay.all_sum(vec_sums))
    if lay.ring:
        grad_attn, grad_up, grad_down = (attn_own, attn_z), (up_own, up_z), (down_own, down_z)
    late = [own]
    grad_down, down_second_new, down_new = step(0.1, grad_down, down_weight, down_first, down_second, after=late)
    grad_up, up_second_new, up_new = step(0.1, grad_up, up_weight, up_first, up_second, after=[down_new])
    grad_attn, attn_second_new, attn_new = step(0.1, grad_attn, attn_weight, attn_first, attn_second)
    vec_second_new, vectors_new = adamw(vectors, vec_first, vec_second, grad_vec, 0.5)
    return (
        result.reshape(tokens.shape),
        input_grad.reshape(tokens.shape),
        grad_attn,
        grad_up,
        grad_down,
        grad_vec,
        attn_second_new,
        up_second_new,
        down_second_new,
        vec_second_new,
        attn_new,
        up_new,
        down_new,
        vectors_new,
    )


def solution(mesh):
    total = mesh.shape["wide"] * mesh.shape["narrow"]
    windows = P(None, AXES, None, None)
    counts = P(None, AXES)
    columns = P(None, AXES)
    in_specs = (windows,) * 2 + (counts,) * 2 + (columns,) * 9 + (P(),) * 3
    out_specs = (windows,) * 2 + (columns,) * 3 + (P(),) + (columns,) * 3 + (P(),) + (columns,) * 3 + (P(),)
    return jax.shard_map(
        functools.partial(per_device, total),
        mesh=mesh,
        in_specs=in_specs,
        out_specs=out_specs,
        check_vma=False,
    )
```

```python
import functools
import math

import jax
import jax.numpy as jnp
from jax import lax
from jax.experimental import pallas as pl
from jax.experimental.pallas import tpu as pltpu
from jax.sharding import PartitionSpec as P

D = 640
HEADS = 20
HEAD_DIM = 32
FF = 2560
SEQ = 256
STEP = 10
AXES = ("wide", "narrow")
GROUPS = 4
GROUP_HEADS = HEADS // GROUPS
GROUP = GROUP_HEADS * HEAD_DIM
HALF = GROUP // 2
WIDE = 256
QUARTER = FF // 8
SCALE = HEAD_DIM ** (-0.5)
BF16 = jnp.bfloat16
F32 = jnp.float32
PACE = 1.15e9
MARGIN = 6 * 1024 * 1024


def nt(left, right):
    return lax.dot_general(left, right, (((1,), (1,)), ((), ())), preferred_element_type=F32)


def nn(left, right):
    return jnp.dot(left, right, preferred_element_type=F32)


def tn(left, right):
    return lax.dot_general(left, right, (((0,), (0,)), ((), ())), preferred_element_type=F32)


def shape(dims, kind=BF16):
    return jax.ShapeDtypeStruct(dims, kind)


class Kept:
    def __init__(self, dims, kind=BF16):
        self.struct = shape(dims, kind)


class Far:
    def __init__(self, value):
        self.value = value


def call(kernel, name, outs, place, args, micros, scratch=(), after=(), copies=None):
    kept = [place_of for place_of, out in enumerate(outs) if isinstance(out, Kept)]
    outs = [out.struct if isinstance(out, Kept) else out for out in outs]
    far = [place_of for place_of, arg in enumerate(args) if isinstance(arg, Far)]
    args = [
        pltpu.with_memory_space_constraint(arg.value, pltpu.HBM) if isinstance(arg, Far) else arg for arg in args
    ]
    buffers = [pltpu.VMEM(a.shape, a.dtype) for a in [outs[k] for k in kept] + [args[k] for k in far]]
    copies = copies or len(kept)
    size = sum(a.size * a.dtype.itemsize for a in args) + sum(o.size * o.dtype.itemsize for o in outs)
    extra = sum(math.prod(s.shape) * s.dtype.itemsize for s in scratch)
    semaphores = [pltpu.SemaphoreType.DMA((copies + len(far),))] if buffers else []

    def body(place_ref, *refs):
        ins, refs = list(refs[: len(args)]), refs[len(args) + len(after) :]
        out_refs, refs = list(refs[: len(outs)]), refs[len(outs) :]
        work, held = refs[: len(scratch)], refs[len(scratch) : len(scratch) + len(buffers)]
        started, targets, coming = [], [], []
        for slot, (k, buffer) in enumerate(zip(far, held[len(kept) :])):
            copy = pltpu.make_async_copy(ins[k], buffer, refs[-1].at[copies + slot])
            copy.start()
            coming.append((buffer, copy))
            ins[k] = buffer
        for k, buffer in zip(kept, held):
            targets.append((buffer, out_refs[k]))
            out_refs[k] = buffer

        def flush(ref, index=None):
            target = next(out for buffer, out in targets if buffer is ref)
            if index is not None:
                ref, target = ref.at[index], target.at[index]
            copy = pltpu.make_async_copy(ref, target, refs[-1].at[len(started)])
            copy.start()
            started.append(copy)

        def fetch(ref):
            next(copy for buffer, copy in coming if buffer is ref).wait()
            return ref

        kernel(place_ref, (flush, fetch), *ins, *out_refs, *work)
        for copy in started:
            copy.wait()

    def spec(space):
        return pl.BlockSpec(memory_space=space)

    return list(pl.pallas_call(
        body,
        out_shape=tuple(pltpu.HBM(o.shape, o.dtype) if k in kept else o for k, o in enumerate(outs)),
        in_specs=[spec(pltpu.SMEM)]
        + [spec(pl.ANY if k in far else pltpu.VMEM) for k in range(len(args))]
        + [spec(pl.ANY)] * len(after),
        out_specs=tuple(spec(pltpu.HBM if k in kept else pltpu.VMEM) for k in range(len(outs))),
        scratch_shapes=list(scratch) + buffers + semaphores,
        compiler_params=pltpu.CompilerParams(vmem_limit_bytes=size + extra + MARGIN),
        cost_estimate=pl.CostEstimate(flops=int(micros * PACE), bytes_accessed=size, transcendentals=0),
        name=name,
    )(place, *args, *after))


def normalize(rows):
    centered = rows - jnp.mean(rows, axis=-1, keepdims=True)
    scale = lax.rsqrt(jnp.mean(centered * centered, axis=-1, keepdims=True) + 1e-05)
    return centered * scale, scale


def norm_back(grad, scaled, scale, gain):
    weighted = grad * gain
    mean_one = jnp.mean(weighted, axis=-1, keepdims=True)
    mean_two = jnp.mean(weighted * scaled, axis=-1, keepdims=True)
    return scale * (weighted - mean_one - scaled * mean_two)


def column_sum(rows):
    return jnp.sum(rows, axis=0, keepdims=True)


def rope_tables():
    position = jnp.arange(SEQ, dtype=F32)
    frequency = 10000.0 ** (-jnp.arange(0, HEAD_DIM, 2, dtype=F32) / HEAD_DIM)
    angles = position[:, None] * frequency[None, :]
    cos, sin = jnp.cos(angles), jnp.sin(angles)
    return jnp.tile(cos, (1, 8)), jnp.tile(jnp.concatenate([-sin, sin], axis=1), (1, 4))


def swapped(rows):
    low = lax.broadcasted_iota(jnp.int32, rows.shape, 1) % HEAD_DIM < HEAD_DIM // 2
    return jnp.where(low, pltpu.roll(rows, 128 - HEAD_DIM // 2, 1), pltpu.roll(rows, HEAD_DIM // 2, 1))


def group_heads():
    for head in range(GROUP_HEADS):
        yield head, (head // 4) * 128, head % 4


def head_only(rows, lane):
    owner = lax.broadcasted_iota(jnp.int32, rows.shape, 1) // HEAD_DIM
    return jnp.where(owner == lane, rows, jnp.zeros_like(rows))


def halves(place):
    core = place[1]
    return pl.multiple_of(core * HALF, 16), pl.multiple_of((1 - core) * HALF, 16)


def first_norm_kernel(place, move, tokens, vectors, hidden):
    scaled, _ = normalize(tokens[...].astype(F32))
    hidden[...] = (scaled * vectors[0:1, :] + vectors[1:2, :]).astype(BF16)


def stack_into(out, parts):
    for source, part in enumerate(parts):
        out[source] = part[...]


def line_kernel(place, move, *refs):
    stack_into(refs[4], refs[:4])


def make_line(place, parts, after):
    return call(line_kernel, "line", [shape((4, *parts[0].shape))], place, parts, 0.6, after=after)[0]


def pack_kernel(place, move, *refs):
    groups, shards, (packed, ups, downs) = refs[:3], refs[3:7], refs[7:]
    stack_into(packed, groups)
    rows = ups.shape[1]
    for source in range(4):
        ups[source] = shards[source][:rows, :]
        downs[source] = shards[source][rows:, :]


def pack(place, groups, shards, after):
    outs = [shape((3, *groups[0].shape))] + [shape((4, shards[0].shape[0] // 2, D))] * 2
    return call(pack_kernel, "pack", outs, place, (*groups, *shards), 1.0, after=after)


def attention_forward_kernel(groups, place, move, hidden, bias, cos, sin, *refs):
    flush, fetch = move
    count = len(groups)
    mine, other, *refs = refs
    if len(refs) > 7 * count:
        refs[-1][...] = refs[0][...]
        refs = refs[1:-1]
    weights, weights_out, qs, ks, vs, probs, mixed = [refs[part * count : (part + 1) * count] for part in range(7)]
    z = place[0]
    first, second = halves(place)
    rows = hidden[...]
    windows = rows.shape[0] // SEQ
    for step, which in enumerate(groups):
        weight, prob_out = weights[step], probs[step]
        group = place[2] ^ which
        for part in range(4):
            source = lax.rem(part + 4 - z, 4)
            pieces = mine[step, source], other[step, source]
            for offset, piece in zip((first, second), pieces):
                if part < 3:
                    weight[part, pl.ds(offset, HALF), :] = piece
                else:
                    weights_out[step][pl.ds(offset, HALF), :] = piece
            if part < 3:
                weight[part, GROUP:WIDE, :] = jnp.zeros((WIDE - GROUP, D), BF16)
        flush(weight)
        for part, out in ((0, qs[step]), (1, ks[step]), (2, vs[step])):
            proj = nt(rows, weight[part]) + bias[group, part : part + 1, :]
            for window in range(windows):
                span = slice(window * SEQ, (window + 1) * SEQ)
                for tile in (0, 128):
                    piece = proj[span, tile : tile + 128]
                    if part < 2:
                        piece = piece * cos[...] + swapped(piece) * sin[...]
                    out[span, tile : tile + 128] = piece.astype(BF16)
            flush(out)
        for window in range(windows):
            span = slice(window * SEQ, (window + 1) * SEQ)
            visible = lax.broadcasted_iota(jnp.int32, (SEQ, 1), 0) < place[4 + window]
            values = vs[step][span, :].T
            for head, tile, lane in group_heads():
                keys = head_only(ks[step][span, tile : tile + 128], lane)
                scores = nt(keys, qs[step][span, tile : tile + 128])
                scores = jnp.where(visible, scores, -1e30)
                top = jnp.max(scores, axis=0, keepdims=True)
                exponent = jnp.exp((scores - top) * SCALE)
                prob = (exponent * (1.0 / column_sum(exponent))).astype(BF16)
                prob_out[window * GROUP_HEADS + head] = prob
                flush(prob_out, window * GROUP_HEADS + head)
                rows_out = slice(head * HEAD_DIM, (head + 1) * HEAD_DIM)
                mixed[step][rows_out, span] = nn(values[rows_out], prob).astype(BF16)


def attention_forward(groups, place, hidden, bias, cos, sin, mine, other, after, cargo=()):
    rows = hidden.shape[0]
    maps = rows // SEQ * GROUP_HEADS
    count = len(groups)
    kinds = [Kept((3, WIDE, D)), shape((GROUP, D))] + [Kept((rows, WIDE))] * 3
    kinds += [Kept((maps, SEQ, SEQ)), shape((GROUP, rows))]
    out = call(
        functools.partial(attention_forward_kernel, groups), "attention_forward",
        [kind for kind in kinds for _ in groups] + [shape(value.shape) for value in cargo], place,
        (hidden, bias, cos, sin, mine, other, *cargo), 4.8 * count,
        after=after, copies=count * (4 + maps),
    )
    return [out[step : 7 * count : count] for step in range(count)] + out[7 * count :]


def middle_kernel(place, move, tokens, vectors, *refs):
    flush, fetch = move
    mixed_in, weight_in, *refs = refs[:4], refs[4:8], *refs[8:]
    if len(refs) > 5:
        for source in range(2):
            along_y, along_x = refs[2 * source : 2 * source + 2]
            refs[8 + 2 * source][...] = along_x[0:160, :]
            refs[9 + 2 * source][...] = along_y[160:320, :]
        refs = refs[4:8] + refs[12:]
    middle, normed, mixed, weight, stage = refs
    for which in range(GROUPS):
        offset = pl.multiple_of((place[2] ^ which) * GROUP, 32)
        stage[pl.ds(offset, GROUP), :] = mixed_in[which][...]
        weight[pl.ds(offset, GROUP), :] = weight_in[which][...]
    mixed[...] = stage[...].T
    flush(weight)
    flush(mixed)
    rows = tokens[...].astype(F32) + nt(mixed[...], weight[...]) + vectors[5:6, :]
    middle[...] = rows
    flush(middle)
    scaled, _ = normalize(rows)
    normed[...] = (scaled * vectors[6:7, :] + vectors[7:8, :]).astype(BF16)


def middle_layer(place, tokens, vectors, mixed, weights, lines):
    rows = tokens.shape[0]
    outs = [Kept((rows, D), F32), shape((rows, D)), Kept((rows, D)), Kept((D, D))]
    outs += [shape((2 * 80, D)) for _ in lines]
    return call(
        middle_kernel, "middle", outs, place, (tokens, vectors, *mixed, *weights, *lines), 2.5,
        [pltpu.VMEM((D, rows), BF16)],
    )


def store_quarter(outs, which, value, flush):
    low = value.astype(BF16)
    if which < 3:
        outs[which][...] = low
    else:
        outs[3][...], outs[4][...] = low[: QUARTER // 2], low[QUARTER // 2 :]
    for out in outs[which : which + 1] if which < 3 else outs[3:5]:
        flush(out)


def five_parts():
    return [Kept((QUARTER, D))] * 3 + [Kept((QUARTER // 2, D))] * 2


def quarter(parts, which):
    if which < 3:
        return parts[which][...]
    return jnp.concatenate([parts[3][...], parts[4][...]], axis=0)


def hidden_forward_kernel(place, move, *refs):
    flush, fetch = move
    ups, (bias, normed, normed_pair, back, back_pair), refs = refs[:5], refs[5:10], refs[10:]
    active, slopes, grads_down = refs[0], refs[1:5], refs[5:]
    rows = normed.shape[0]
    for which in range(4):
        if which < 3:
            fetch(ups[which])
        up = quarter(ups, which)
        column = jnp.broadcast_to(bias[which], (8, QUARTER)).T[:, 0:1]
        total = 0.0
        for part, inputs, grads in ((0, normed, back), (1, normed_pair, back_pair)):
            span = slice(part * rows, (part + 1) * rows)
            pre = nt(up, inputs[...]) + column
            cdf = 0.5 + 0.5 * lax.erf(pre * (0.5**0.5))
            low = (pre * cdf).astype(BF16)
            active[which, :, span] = low
            slopes[which][:, span] = (cdf + pre * jnp.exp(-0.5 * pre * pre) * 0.3989422804014327).astype(BF16)
            total = total + nn(low, grads[...])
        flush(active, which)
        store_quarter(grads_down, which, total, flush)


def hidden_forward(place, ups, bias, normed, normed_pair, back, back_pair):
    rows = 2 * normed.shape[0]
    outs = [Kept((4, QUARTER, rows))] + [shape((QUARTER, rows))] * 4 + five_parts()
    active, *rest = call(
        hidden_forward_kernel, "hidden_forward", outs, place,
        (*[Far(up) for up in ups[:3]], *ups[3:], bias, normed, normed_pair, back, back_pair), 7.5, copies=9,
    )
    return active, rest[:4], rest[4:]


def hidden_backward_kernel(place, move, *refs):
    downs, ups, slopes, (back, back_pair), refs = refs[:5], refs[5:10], refs[10:14], refs[14:16], refs[16:]
    grad_pre, own, pair, up = refs
    rows = back.shape[0]
    for down in downs[:3]:
        move[1](down)
    for which in range(4):
        units = slice(which * QUARTER, (which + 1) * QUARTER)
        up[units, :] = quarter(ups, which)
        down = quarter(downs, which)
        for part, grads in ((0, back), (1, back_pair)):
            span = slice(part * rows, (part + 1) * rows)
            wide = nt(down, grads[...]) * slopes[which][:, span].astype(F32)
            grad_pre[units, span] = wide.astype(BF16)
    for out, span in ((pair, slice(rows, 2 * rows)), (own, slice(0, rows))):
        out[...] = tn(grad_pre[:, span], up[...]).astype(out.dtype)


def hidden_backward(place, downs, ups, slopes, back, back_pair):
    rows = back.shape[0]
    outs = [shape((4 * QUARTER, 2 * rows)), shape((rows, D), F32), shape((rows, D))]
    return call(
        hidden_backward_kernel, "hidden_backward", outs, place,
        (*[Far(down) for down in downs[:3]], *downs[3:], *ups, *slopes, back, back_pair), 6.0, [pltpu.VMEM((4 * QUARTER, D), BF16)],
    )


def up_gradient_kernel(place, move, grad_pre, normed, normed_pair, *refs):
    grads, grad_bias = refs[:5], refs[5]
    rows = normed.shape[0]
    for which in range(4):
        units = slice(which * QUARTER, (which + 1) * QUARTER)
        low = grad_pre[units, :]
        store_quarter(grads, which, nn(low[:, :rows], normed[...]) + nn(low[:, rows:], normed_pair[...]), move[0])
        bias = jnp.sum(low.astype(F32), axis=1, keepdims=True)
        for source in range(4):
            grad_bias[4 * which + source] = jnp.broadcast_to(bias[source * 80 : (source + 1) * 80], (80, 8)).T


def up_gradient(place, grad_pre, normed, normed_pair, after):
    outs = five_parts() + [shape((16, 8, 80), F32)]
    *grads, bias = call(
        up_gradient_kernel, "up_gradient", outs, place, (grad_pre, normed, normed_pair), 4.0, after=after
    )
    return grads, bias


def output_kernel(place, move, active, *refs):
    downs, (own, pair) = refs[:5], refs[5:]
    rows = own.shape[0]
    down = jnp.concatenate([value[...] for value in downs], axis=0)
    for out, span in ((pair, slice(rows, 2 * rows)), (own, slice(0, rows))):
        left = jnp.concatenate([active[which, :, span] for which in range(4)], axis=0)
        out[...] = tn(left, down).astype(out.dtype)


def output_layer(place, active, downs, after):
    rows = active.shape[2] // 2
    outs = [shape((rows, D), F32), shape((rows, D))]
    return call(output_kernel, "output", outs, place, (active, *downs), 2.8, after=after)


def middle_backward_kernel(
    place, move, own, pair, middle, back, vectors, mixed, weight, grad_middle, sums, grad_mixed, mine, other, stage, stage_mixed
):
    grad = own[...] + pair[...].astype(F32)
    scaled, scale = normalize(middle[...])
    wide = back[...].astype(F32)
    total = wide + norm_back(grad, scaled, scale, vectors[6:7, :])
    grad_middle[...] = total
    sums[0:1, :] = column_sum(total)
    sums[1:2, :] = column_sum(grad * scaled)
    sums[2:3, :] = column_sum(grad)
    sums[3:4, :] = column_sum(wide)
    sums[4:8, :] = jnp.zeros((4, D), F32)
    low = total.astype(BF16)
    stage_mixed[...] = nt(weight[...].T, low).astype(BF16)
    stage[...] = tn(low, mixed[...]).astype(BF16)
    first, second = halves(place)
    for which in range(GROUPS):
        offset = (place[2] ^ which) * GROUP
        grad_mixed[which] = stage_mixed[pl.ds(pl.multiple_of(offset, 32), GROUP), :]
        mine[which] = stage[pl.ds(pl.multiple_of(offset + first, 16), HALF), :]
        other[which] = stage[pl.ds(pl.multiple_of(offset + second, 16), HALF), :]


def middle_backward(place, own, pair, middle, back, vectors, mixed, weight, after):
    rows = own.shape[0]
    outs = [shape((rows, D), F32), shape((8, D), F32), shape((GROUPS, GROUP, rows))]
    outs += [shape((GROUPS, HALF, D)), shape((GROUPS, HALF, D))]
    return call(
        middle_backward_kernel, "middle_backward", outs, place,
        (own, pair, middle, back, vectors, mixed, weight), 3.0,
        [pltpu.VMEM((D, D), BF16), pltpu.VMEM((D, rows), BF16)], after,
    )


def attention_backward_kernel(groups, place, move, grad_mixed, hidden, cos, sin, out_mine, out_other, *refs):
    count = len(groups)
    qs, ks, vs, probs, dqs, dks, dvs = [refs[part * count : (part + 1) * count] for part in range(7)]
    biases, (mine, other, dq_turned, stage) = refs[7 * count : 8 * count], refs[8 * count :]
    rows = hidden.shape[0]
    first, second = halves(place)
    for step, which in enumerate(groups):
        q, k, v, prob_in, dq_out, dk_out, dv_out = (
            qs[step], ks[step], vs[step], probs[step], dqs[step], dks[step], dvs[step]
        )
        for window in range(rows // SEQ):
            span = slice(window * SEQ, (window + 1) * SEQ)
            grad = grad_mixed[which, :, span].T
            tail = jnp.concatenate([grad[:, 128:GROUP], jnp.zeros((SEQ, WIDE - GROUP), BF16)], axis=1)
            grads = {0: grad[:, :128], 128: tail}
            keys = k[span, :].T
            dv = {0: 0.0, 128: 0.0}
            dk = {0: 0.0, 128: 0.0}
            for head, tile, lane in group_heads():
                cols = slice(tile, tile + 128)
                low = prob_in[window * GROUP_HEADS + head]
                prob = low.astype(F32)
                weighted = prob * nt(head_only(v[span, cols], lane), grads[tile])
                ds = (weighted - prob * column_sum(weighted)).astype(BF16)
                dv[tile] = dv[tile] + nn(low, head_only(grads[tile], lane))
                dk[tile] = dk[tile] + nn(ds, head_only(q[span, cols], lane))
                rows_out = slice(head * HEAD_DIM, (head + 1) * HEAD_DIM)
                dq_turned[step, rows_out, span] = nn(keys[rows_out], ds)
            padded = jnp.concatenate([dq_turned[step, :, span], jnp.zeros((WIDE - GROUP, SEQ), F32)], axis=0).T
            for tile in (0, 128):
                cols = slice(tile, tile + 128)
                piece = dk[tile] * SCALE
                dk_out[span, cols] = (piece * cos[...] - swapped(piece) * sin[...]).astype(BF16)
                piece = padded[:, cols] * SCALE
                dq_out[span, cols] = (piece * cos[...] - swapped(piece) * sin[...]).astype(BF16)
                dv_out[span, cols] = dv[tile].astype(BF16)
        biases[step][...] = jnp.zeros((8, WIDE), F32)
        for part, out in ((0, dq_out), (1, dk_out), (2, dv_out)):
            values = out[...]
            stage[step, part] = tn(values, hidden[...]).astype(BF16)
            mine[step, part] = stage[step, part, pl.ds(first, HALF), :]
            other[step, part] = stage[step, part, pl.ds(second, HALF), :]
            biases[step][part : part + 1, :] = column_sum(values.astype(F32))
        mine[step, 3] = out_mine[which]
        other[step, 3] = out_other[which]


def attention_backward(groups, place, grad_mixed, hidden, cos, sin, out_mine, out_other, saved, after):
    rows = hidden.shape[0]
    count = len(groups)
    outs = [shape((rows, WIDE))] * (3 * count) + [shape((8, WIDE), F32)] * count + [shape((count, 4, HALF, D))] * 2
    *out, mine, other = call(
        functools.partial(attention_backward_kernel, groups), "attention_backward", outs, place,
        (grad_mixed, hidden, cos, sin, out_mine, out_other, *[group[k] for k in range(4) for group in saved]),
        4.7 * count,
        [pltpu.VMEM((count, GROUP, rows), F32), pltpu.VMEM((count, 3, WIDE, D), BF16)], after,
    )
    return [out[step::count] for step in range(count)], mine, other


def first_backward_kernel(place, move, tokens, grad_middle, vectors, *refs):
    parts, weights, biases, (middle_sums, units), refs = refs[:12], refs[12:16], refs[16:20], refs[20:22], refs[22:]
    input_grad, sums, unit_rows = refs
    z, plane, core = place[0], place[2], place[3]
    grad = 0.0
    for which in range(GROUPS):
        for part in range(3):
            grad = grad + nn(parts[which * 3 + part][...], weights[which][part])
    scaled, scale = normalize(tokens[...].astype(F32))
    input_grad[...] = (grad_middle[...] + norm_back(grad, scaled, scale, vectors[0:1, :])).astype(BF16)
    sums[...] = jnp.zeros((24, D), F32)
    sums[0:1, :] = column_sum(grad * scaled)
    sums[1:2, :] = column_sum(grad)
    sums[2:6, :] = middle_sums[0:4, :]
    for group in range(GROUPS):
        value = sum(jnp.where((plane ^ which) == group, biases[which][...], 0.0) for which in range(GROUPS))
        row, column = 8 + 4 * (group // 2), WIDE * (group % 2)
        sums[row : row + 4, column : column + WIDE] = value[0:4]
    unit_rows[...] = jnp.zeros((4, 8, 128), F32)
    for which in range(4):
        for source in range(4):
            row = (plane ^ which) * 2 + core
            unit_rows[z ^ source, pl.ds(row, 1), 0:80] = units[4 * which + source, 0:1, :]
    for line in range(4):
        sums[16:24, line * 128 : (line + 1) * 128] = unit_rows[line]


def first_backward(place, tokens, grad_middle, vectors, parts, weights, biases, middle_sums, units, after):
    rows = tokens.shape[0]
    outs = [shape((rows, D)), shape((24, D), F32)]
    return call(
        first_backward_kernel, "first_backward", outs, place,
        (tokens, grad_middle, vectors, *parts, *weights, *biases, middle_sums, units),
        4.6, [pltpu.VMEM((4, 8, 128), F32)], after,
    )


def unpack_vector(sums):
    group_rows = [sums[8 + 4 * (g // 2) :, WIDE * (g % 2) :][:3, :GROUP] for g in range(GROUPS)]
    units = sums[16:24, :512].reshape(8, 4, 128)[:, :, :80].transpose(1, 0, 2).reshape(4, D)
    return jnp.concatenate([sums[0:2], jnp.concatenate(group_rows, axis=1), sums[2:6], units])


def ordered_sum_kernel(which, place, move, *refs):
    total = 0.0
    for index in range(4):
        total = total + sum(jnp.where((place[which] ^ step) == index, refs[step][...], 0.0) for step in range(4))
    refs[4][...] = total


def ordered_sum(place, which, parts, after=()):
    outs = [shape(parts[0].shape, F32)]
    return call(functools.partial(ordered_sum_kernel, which), "ordered_sum", outs, place, parts, 0.6, after=after)[0]


VEC_ROWS = 24
SENT_ROWS = HALF + 32


def attention_sum_kernel(place, move, *refs):
    parts, vec, (own, own_vec, *sent), stage = refs[:4], refs[4], refs[5:10], refs[10]
    stage[...] = sum(value[...].astype(F32) for value in parts[2:]) + sum(value[1].astype(F32) for value in parts[:2])
    low = vec[...].astype(BF16)
    own[...] = stage[place[0]]
    own_vec[...] = low.astype(F32)
    for steps, out in enumerate(sent):
        out[0:HALF, :] = stage[lax.rem(place[0] + steps + 1, 4)].astype(BF16)
        out[HALF : HALF + VEC_ROWS, :] = low
        out[HALF + VEC_ROWS :, :] = jnp.zeros((SENT_ROWS - HALF - VEC_ROWS, D), BF16)


def attention_sum(place, parts, vec, after):
    dims = parts[2].shape
    outs = [shape(dims[1:], F32), shape(vec.shape, F32)] + [shape((SENT_ROWS, D))] * 3
    return call(
        attention_sum_kernel, "attention_sum", outs, place, (*parts, vec), 1.0, [pltpu.VMEM(dims, F32)], after=after
    )


def add(out, *parts):
    out[...] = sum(part.astype(F32) for part in parts).astype(out.dtype)


def keep_and_send(parts, keep, sent):
    total = sum(part[...].astype(F32) for part in parts)
    keep[...] = total[0:2]
    sent[...] = total[2:4].astype(BF16)


def merge_into(along_y, along_x, first, second, out_y, out_x):
    out_y[0:2] = along_y[0:2]
    add(out_y.at[2:4], along_y[2:4], second[...])
    add(out_x.at[0:2], along_x[0:2], first[...])
    out_x[2:4] = along_x[2:4]


def merge_kernel(place, move, along_y, along_x, *refs):
    for ref in (along_y, along_x):
        move[1](ref)
    merge_into(along_y, along_x, *refs)


def merge(place, along_y, along_x, first, second, after):
    outs = [shape(along_y.shape)] * 2
    return call(merge_kernel, "merge", outs, place, (Far(along_y), Far(along_x), first, second), 1.5, after=after)


def exchange_one_kernel(place, move, *refs):
    downs, (along_y, along_x, first, second), refs = refs[:3], refs[3:7], refs[7:]
    keep, sent, out_y, out_x = refs
    for ref in (downs[0], along_y, along_x):
        move[1](ref)
    keep_and_send(downs, keep, sent)
    merge_into(along_y, along_x, first, second, out_y, out_x)


def exchange_one(place, downs, ups, after):
    dims = downs[0].shape
    outs = [shape((2, *dims[1:]), F32), shape((2, *dims[1:]))] + [shape(dims)] * 2
    return call(
        exchange_one_kernel, "exchange_one", outs, place,
        (Far(downs[0]), *downs[1:], Far(ups[0]), Far(ups[1]), *ups[2:]), 2.0, after=after,
    )


def cores_one_kernel(place, move, mine, other, half_y, half_x, rest):
    add(half_y, mine[0, 0:2], other[0, 0:2])
    add(half_x, mine[0, 2:4], other[0, 2:4])
    add(rest, mine[1], other[1])


def cores_one(place, mine, other, after):
    dims = mine.shape[1:]
    outs = [shape((2, *dims[1:]))] * 2 + [shape(dims)]
    return call(cores_one_kernel, "cores_one", outs, place, (mine, other), 1.0, after=after)


def exchange_two_kernel(place, move, *refs):
    ups, (keep_in, line_in), (keep, sent, own, line) = refs[:3], refs[3:5], refs[5:]
    move[1](ups[0])
    keep_and_send(ups, keep, sent)
    total = keep_in[...] + line_in[...].astype(F32)
    own[...] = total[0]
    line[...] = total[1].astype(BF16)


def exchange_two(place, ups, keep, line, after):
    dims = ups[0].shape
    outs = [shape((2, *dims[1:]), F32), shape((2, *dims[1:])), shape(dims[1:], F32), shape(dims[1:])]
    return call(
        exchange_two_kernel, "exchange_two", outs, place, (Far(ups[0]), *ups[1:], keep, line), 12.0, after=after
    )


def exchange_three_kernel(place, move, rest, mine, other, first, second, keep, line_in, along_y, along_x, own, line):
    add(along_x.at[0:2], rest[0:2], first[...])
    along_x[2:4] = rest[2:4]
    add(along_y.at[0:2], mine[0, 0:2], other[0, 0:2])
    add(along_y.at[2:4], mine[0, 2:4], other[0, 2:4], second[...])
    total = keep[...] + line_in[...].astype(F32)
    own[...] = total[0]
    line[...] = total[1].astype(BF16)


def exchange_three(place, rest, mine, other, halves_in, keep, line, after):
    dims = rest.shape
    outs = [shape(dims)] * 2 + [shape(dims[1:], F32), shape(dims[1:])]
    return call(
        exchange_three_kernel, "exchange_three", outs, place, (rest, mine, other, *halves_in, keep, line), 1.0,
        after=after,
    )


def core_runs(place):
    for which in range(4):
        for source in range(4):
            run = ((place[0] ^ source) * 4 + (place[2] ^ which)) * 2 + place[3]
            yield which, source, pl.ds(pl.multiple_of(run * 80, 16), 80)


def take_runs_kernel(place, move, full, *outs):
    for which, source, rows in core_runs(place):
        part, offset = (which, source) if which < 3 else (3 + source // 2, source % 2)
        outs[part][offset * 80 : (offset + 1) * 80, :] = full[rows, :]


def take_runs(place, full):
    outs = [shape((QUARTER, D))] * 3 + [shape((QUARTER // 2, D))] * 2
    return call(take_runs_kernel, "take_runs", outs, place, (full,), 1.0)


def place_runs_kernel(place, move, *refs):
    full = refs[5]
    full[...] = jnp.zeros_like(full)
    for which, source, rows in core_runs(place):
        part, offset = (which, source) if which < 3 else (3 + source // 2, source % 2)
        full[rows, :] = refs[part][offset * 80 : (offset + 1) * 80, :].astype(F32)


def place_runs(place, quarters):
    return call(place_runs_kernel, "place_runs", [shape((FF, D), F32)], place, quarters, 2.0)[0]


def pick(array, index):
    return lax.dynamic_index_in_dim(array, index, 0, keepdims=False)


def step_into(rate, gradient, state, outs):
    weight, first, second = state
    grad, second_new, new = outs
    grad[...] = gradient
    second_new[...], new[...] = adamw(weight[...], first[...], second[...], gradient, rate)


def finish_attention_kernel(place, move, own, own_vec, one, two, three, weight, first, second, *outs):
    total = own[...]
    for value in (one, two, three):
        total = total + value[0:HALF, :].astype(F32)
    step_into(0.1, total, (weight, first, second), outs[:3])
    vec = [own_vec[...]]
    for value in (one, two, three):
        vec.append(value[HALF : HALF + VEC_ROWS, :].astype(F32))
    total = 0.0
    for z in range(4):
        came = lax.rem(place[0] + 4 - z, 4)
        total = total + sum(jnp.where(came == steps, vec[steps], 0.0) for steps in range(4))
    outs[3][...] = total


def finish_attention(place, own, own_vec, line, state, after):
    *out, vec = call(
        finish_attention_kernel, "finish_attention", [shape(own.shape, F32)] * 3 + [shape(own_vec.shape, F32)], place,
        (own, own_vec, *line, *[value.T for value in state]), 0.3, after=after,
    )
    return [value.T for value in out], vec


def finish_hidden_kernel(place, move, *refs):
    owns, arrived, refs = refs[:2], refs[2:4], refs[4:]
    for matrix in range(2):
        state = refs[3 * matrix : 3 * matrix + 3]
        for ref in state:
            move[1](ref)
        outs = refs[6 + 3 * matrix : 9 + 3 * matrix]
        step_into(0.1, owns[matrix][...] + arrived[matrix][...].astype(F32), state, outs)


def finish_hidden(place, owns, arrived, state, after):
    out = call(
        finish_hidden_kernel, "finish_hidden", [shape(owns[0].shape, F32)] * 6, place,
        (*owns, *arrived, *[Far(value.T) for value in state]), 0.3, after=after,
    )
    return [value.T for value in out[:3]], [value.T for value in out[3:]]


def result_kernel(place, move, middle, own, pair, vectors, out):
    move[1](middle)
    out[...] = (middle[...] + own[...] + pair[...].astype(F32) + vectors[8:9, :]).astype(BF16)


def result_layer(place, middle, own, pair, vectors, after):
    outs = [shape(middle.shape)]
    return call(result_kernel, "result", outs, place, (Far(middle), own, pair, vectors), 12.0, after=after)[0]


def adamw(weight, first_moment, second_moment, gradient, rate_value):
    first_new = 0.9 * first_moment + 0.1 * gradient
    second_new = 0.999 * second_moment + 0.001 * gradient * gradient
    corrected = first_new / (1.0 - 0.9**STEP) / (jnp.sqrt(second_new / (1.0 - 0.999**STEP)) + 1e-08)
    return (second_new, weight - rate_value * (corrected + 0.01 * weight))


class Layout:
    def __init__(self, total):
        self.total = total
        self.block = 4 * D // total
        self.stride = total // 4
        self.me = lax.axis_index(AXES)
        self.core = lax.rem(self.me, 2)

    def swap(self, value, mask):
        return lax.ppermute(value, AXES, [(i, i ^ mask) for i in range(self.total)])

    def shift(self, value, steps):
        pairs = [(i, (i + self.stride * steps) % self.total) for i in range(self.total)]
        return lax.ppermute(value, AXES, pairs)


    def hidden_index(self):
        order = jnp.arange(16)
        z, plane = self.place[0], self.place[2]
        return ((z ^ lax.rem(order, 4)) * 4 + (plane ^ (order // 4))) * 2 + self.core


class Ring(Layout):
    def __init__(self, total):
        super().__init__(total)
        self.ring = True
        self.z = self.me // 8
        self.plane = lax.rem(self.me // 2, 4)
        self.place = (self.z, self.core, self.plane)

    def along_z(self, value):
        return [value] + [self.shift(value, -s) for s in (1, 2, 3)]

    def in_plane(self, value, each=None):
        return [value] + [self.swap(each[r].reshape(value.shape) if each else value, 2 * r) for r in (1, 2, 3)]

    def corner(self, *value):
        return [self.swap(value[0], 2), self.swap(value[1], 4)]

    def send_plane(self, along_y, along_x):
        return [self.swap(along_y, 2), self.swap(along_x, 4)]

    def plane_total(self, value):
        return ordered_sum(self.vector, 2, self.in_plane(value))


class Whole(Layout):
    def __init__(self, total):
        super().__init__(total)
        self.ring = False
        self.plane = jnp.int32(0)
        self.place = (jnp.int32(0),) * 3

    def gather_core(self, shard):
        return take_runs(self.vector, lax.all_gather(shard, AXES, axis=0, tiled=True))

    def gather(self, attn, up, down):
        full = lax.all_gather(attn, AXES, axis=0, tiled=True).reshape(4, 4, 2, HALF, D)
        mine = [full[:, r, 0] for r in range(4)]
        other = [full[:, r, 1] for r in range(4)]
        return mine, other, self.gather_core(up), self.gather_core(down)

    def scatter_hidden(self, grads):
        return lax.psum_scatter(place_runs(self.vector, grads), AXES, scatter_dimension=0, tiled=True)

    def scatter_attention(self, mine, other):
        full = jnp.stack([jnp.stack(mine, axis=1), jnp.stack(other, axis=1)], axis=2)
        return lax.psum_scatter(full.astype(F32).reshape(4 * D, D), AXES, scatter_dimension=0, tiled=True)


def per_device(
    total,
    tokens,
    cotangent,
    lengths,
    offsets,
    attn_weight,
    attn_first,
    attn_second,
    up_weight,
    up_first,
    up_second,
    down_weight,
    down_first,
    down_second,
    vectors,
    vec_first,
    vec_second,
):
    lay = Ring(total) if total == 32 else Whole(total)
    counts = jnp.minimum(lengths - offsets, SEQ).reshape(-1)
    rows = counts.shape[0] * SEQ
    place = lay.vector = jnp.concatenate([jnp.stack([*lay.place, lay.core]).astype(jnp.int32), counts])
    cos, sin = rope_tables()

    flat = tokens.reshape(rows, D)
    back = cotangent.reshape(rows, D)
    back_pair = lay.swap(back, 1)
    (hidden,) = call(first_norm_kernel, "first_norm", [shape((rows, D))], place, (flat, vectors), 1.0)
    bias = jnp.pad(vectors[2:5].reshape(3, GROUPS, GROUP).transpose(1, 0, 2), ((0, 0), (0, 0), (0, WIDE - GROUP)))

    chosen = (lay.hidden_index()[:, None] == jnp.arange(32)[None, :]).astype(F32)
    bias_up = jnp.dot(chosen, vectors[9:].reshape(32, 80), precision=lax.Precision.HIGHEST).reshape(4, 1, QUARTER)

    if lay.ring:
        shards = jnp.concatenate([up_weight.T, down_weight.T]).astype(BF16)
        attn_parts = lay.along_z(attn_weight.T.astype(BF16))
        far_shard = lay.swap(shards, 16)
        line = make_line(place, attn_parts, [hidden, bias_up, bias])
        groups = lay.in_plane(line)[1:]
        other = lay.swap(line, 1)
        mine = line[None]
    else:
        mine, other, ups, downs = lay.gather(
            attn_weight.T.astype(BF16), up_weight.T.astype(BF16), down_weight.T.astype(BF16)
        )
        mine, packed = mine[0][None], jnp.stack(mine[1:])
        other, packed_other = other[0], jnp.stack(other[1:])
    forward = attention_forward(
        (0,), place, hidden, bias, cos, sin, mine, other[None], [], [shards] if lay.ring else []
    )
    if lay.ring:
        shards = forward.pop()
        shards = [shards, lay.swap(shards, 8), far_shard, lay.swap(far_shard, 8)]
        packed, up_line, down_line = pack(place, groups, shards, [forward[0][2]])
        ups = [value.reshape(QUARTER, D) for value in (up_line, lay.swap(up_line, 2), lay.swap(up_line, 4))]
        downs = [value.reshape(QUARTER, D) for value in (down_line, lay.swap(down_line, 2), lay.swap(down_line, 4))]
        packed_other = lay.swap(packed, 1)
    forward += attention_forward((1, 2, 3), place, hidden, bias, cos, sin, packed, packed_other, [forward[0][2]])
    weights = [group[0] for group in forward]
    middle, normed, mixed, out_weight, *corners = middle_layer(
        place, flat, vectors, [group[6] for group in forward], [group[1] for group in forward],
        ups[1:3] + downs[1:3] if lay.ring else [],
    )
    if lay.ring:
        ups, downs = ups + lay.corner(*corners[:2]), downs + lay.corner(*corners[2:])
    normed_pair = lay.swap(normed, 1)
    both = (normed, normed_pair, back, back_pair)
    active, slope, grad_down = hidden_forward(place, ups, bias_up, *both)
    if lay.ring:
        grad_down = [value.reshape(-1, 80, D) for value in grad_down]
        down_corner = lay.corner(*grad_down[3:])
    grad_pre, own, pair = hidden_backward(place, downs, ups, slope, back, back_pair)
    gradient_after, middle_after, after = [], [], []
    if lay.ring:
        down_sent = merge(place, *grad_down[1:3], *down_corner, [own])
        gradient_after = down_sent[:1]
        down_sent = middle_after = lay.send_plane(*down_sent)
    grad_up, grad_bias_up = up_gradient(place, grad_pre, normed, normed_pair, gradient_after)
    if lay.ring:
        grad_up = [value.reshape(-1, 80, D) for value in grad_up]
        up_corner = lay.corner(*grad_up[3:])
    out_own, out_pair = output_layer(place, active, downs, [grad_bias_up])
    out_pair = lay.swap(out_pair, 1)
    grad_middle, sums, grad_mixed, out_mine, out_other = middle_backward(
        place, own, lay.swap(pair, 1), middle, back, vectors, mixed, out_weight, [out_own] + middle_after
    )

    def backward_of(groups, after):
        saved = [forward[r][2:6] for r in groups]
        return attention_backward(groups, place, grad_mixed, hidden, cos, sin, out_mine, out_other, saved, after)

    if lay.ring:
        keep, line, *up_sent = exchange_one(place, [grad_down[0], *down_sent], [*grad_up[1:3], *up_corner], [sums])
        down_line = lay.swap(line, 16)
        up_sent = lay.send_plane(*up_sent)
        after = [keep]
    later, mine_one, other_one = backward_of((3, 2), after)
    after = [later[0][0]]
    if lay.ring:
        other_one = lay.swap(other_one, 1)
        up_keep, up_line, down_own, down_line = exchange_two(
            place, [grad_up[0], *up_sent], keep, down_line, after
        )
        up_line, down_line = lay.swap(up_line, 16), lay.swap(down_line, 8)
        *attn_corner, rest = cores_one(place, mine_one, other_one, [up_keep])
        attn_corner = lay.corner(*attn_corner)
        after = [up_keep, rest]
    sooner, mine_two, other_two = backward_of((1, 0), after)
    backward = [sooner[1], sooner[0], later[1], later[0]]
    other_two, after = lay.swap(other_two, 1) if lay.ring else other_two, [sooner[0][0]]
    if lay.ring:
        after += [*attn_corner, up_line]
    result = result_layer(place, middle, out_own, out_pair, vectors, after)
    if lay.ring:
        along_y, along_x, up_own, up_line = exchange_three(
            place, rest, mine_two, other_two, attn_corner, up_keep, up_line, [result]
        )
        after = [along_y]
    parts = [value for group in backward for value in group[:3]]
    input_grad, vec_sums = first_backward(
        place, flat, grad_middle, vectors, parts, weights, [group[3] for group in backward], sums, grad_bias_up, after
    )
    state = up_weight, up_first, up_second, down_weight, down_first, down_second
    if lay.ring:
        along_y, along_x = lay.send_plane(along_y, along_x)
        up_line = lay.swap(up_line, 8)
        vec_core = vec_sums + lay.swap(vec_sums, 1)
        attn_own, vec_own, *attn_line = attention_sum(
            place, [mine_two, other_two, along_y, along_x], lay.plane_total(vec_core), [up_line]
        )
        attn_line = [lay.shift(value, s) for value, s in zip(attn_line, (1, 2, 3))]
        (grad_up, up_second_new, up_new), (grad_down, down_second_new, down_new) = finish_hidden(
            place, [up_own, down_own], [up_line, down_line], state, [attn_own]
        )
        (grad_attn, attn_second_new, attn_new), vec_sums = finish_attention(
            place, attn_own, vec_own, attn_line, (attn_weight, attn_first, attn_second), [up_new]
        )
    else:
        grad_up, grad_down = lay.scatter_hidden(grad_up).T, lay.scatter_hidden(grad_down).T
        order = (mine_two[1], mine_two[0], mine_one[1], mine_one[0])
        order_other = (other_two[1], other_two[0], other_one[1], other_one[0])
        grad_attn = lay.scatter_attention(order, order_other).T
        attn_second_new, attn_new = adamw(attn_weight, attn_first, attn_second, grad_attn, 0.1)
        up_second_new, up_new = adamw(*state[:3], grad_up, 0.1)
        down_second_new, down_new = adamw(*state[3:], grad_down, 0.1)
        vec_sums = lax.psum(vec_sums, AXES)
    grad_vec = unpack_vector(vec_sums)
    vec_second_new, vectors_new = adamw(vectors, vec_first, vec_second, grad_vec, 0.5)
    return (
        result.reshape(tokens.shape),
        input_grad.reshape(tokens.shape),
        grad_attn,
        grad_up,
        grad_down,
        grad_vec,
        attn_second_new,
        up_second_new,
        down_second_new,
        vec_second_new,
        attn_new,
        up_new,
        down_new,
        vectors_new,
    )


def solution(mesh):
    total = mesh.shape["wide"] * mesh.shape["narrow"]
    windows = P(None, AXES, None, None)
    counts = P(None, AXES)
    columns = P(None, AXES)
    in_specs = (windows,) * 2 + (counts,) * 2 + (columns,) * 9 + (P(),) * 3
    out_specs = (windows,) * 2 + (columns,) * 3 + (P(),) + (columns,) * 3 + (P(),) + (columns,) * 3 + (P(),)
    return jax.shard_map(
        functools.partial(per_device, total),
        mesh=mesh,
        in_specs=in_specs,
        out_specs=out_specs,
        check_vma=False,
    )
```

```python
import functools
import math

import jax
import jax.numpy as jnp
from jax import lax
from jax.experimental import pallas as pl
from jax.experimental.pallas import tpu as pltpu
from jax.sharding import PartitionSpec as P

D = 640
HEADS = 20
HEAD_DIM = 32
FF = 2560
SEQ = 256
STEP = 10
AXES = ("wide", "narrow")
GROUPS = 4
GROUP_HEADS = HEADS // GROUPS
GROUP = GROUP_HEADS * HEAD_DIM
HALF = GROUP // 2
WIDE = 256
QUARTER = FF // 8
SCALE = HEAD_DIM ** (-0.5)
LOG2_E = 1.4426950408889634
BF16 = jnp.bfloat16
F32 = jnp.float32
PACE = 1.15e9
MARGIN = 8 * 1024 * 1024


def nt(left, right):
    return lax.dot_general(left, right, (((1,), (1,)), ((), ())), preferred_element_type=F32)


def nn(left, right):
    return jnp.dot(left, right, preferred_element_type=F32)


def tn(left, right):
    return lax.dot_general(left, right, (((0,), (0,)), ((), ())), preferred_element_type=F32)


def shape(dims, kind=BF16):
    return jax.ShapeDtypeStruct(dims, kind)


TOKENS = {}


class Kept:
    def __init__(self, dims, kind=BF16):
        self.struct = shape(dims, kind)


class Far:
    def __init__(self, value):
        self.value = value


def call(kernel, name, outs, place, args, micros, scratch=(), after=(), copies=None):
    after = [TOKENS[id(value)][1] if id(value) in TOKENS else value for value in after]
    kept = [place_of for place_of, out in enumerate(outs) if isinstance(out, Kept)]
    outs = [out.struct if isinstance(out, Kept) else out for out in outs]
    far = [place_of for place_of, arg in enumerate(args) if isinstance(arg, Far)]
    args = [
        pltpu.with_memory_space_constraint(arg.value, pltpu.HBM) if isinstance(arg, Far) else arg for arg in args
    ]
    buffers = [pltpu.VMEM(a.shape, a.dtype) for a in [outs[k] for k in kept] + [args[k] for k in far]]
    copies = copies or len(kept)
    size = sum(a.size * a.dtype.itemsize for a in args) + sum(o.size * o.dtype.itemsize for o in outs)
    extra = sum(math.prod(s.shape) * s.dtype.itemsize for s in scratch)
    semaphores = [pltpu.SemaphoreType.DMA((copies + len(far),))] if buffers else []

    def body(place_ref, *refs):
        ins, refs = list(refs[: len(args)]), refs[len(args) + len(after) :]
        out_refs, token, refs = list(refs[: len(outs)]), refs[len(outs)], refs[len(outs) + 1 :]
        token[...] = jnp.zeros((8, 128), F32)
        work, held = refs[: len(scratch)], refs[len(scratch) : len(scratch) + len(buffers)]
        started, targets, coming = [], [], []
        for slot, (k, buffer) in enumerate(zip(far, held[len(kept) :])):
            copy = pltpu.make_async_copy(ins[k], buffer, refs[-1].at[copies + slot])
            copy.start()
            coming.append((buffer, copy))
            ins[k] = buffer
        for k, buffer in zip(kept, held):
            targets.append((buffer, out_refs[k]))
            out_refs[k] = buffer

        def flush(ref, index=None):
            target = next(out for buffer, out in targets if buffer is ref)
            if index is not None:
                ref, target = ref.at[index], target.at[index]
            copy = pltpu.make_async_copy(ref, target, refs[-1].at[len(started)])
            copy.start()
            started.append(copy)

        def fetch(ref):
            next(copy for buffer, copy in coming if buffer is ref).wait()
            return ref

        kernel(place_ref, (flush, fetch), *ins, *out_refs, *work)
        for copy in started:
            copy.wait()

    def spec(space):
        return pl.BlockSpec(memory_space=space)

    *result, token = pl.pallas_call(
        body,
        out_shape=(*[pltpu.HBM(o.shape, o.dtype) if k in kept else o for k, o in enumerate(outs)], shape((8, 128), F32)),
        in_specs=[spec(pltpu.SMEM)]
        + [spec(pl.ANY if k in far else pltpu.VMEM) for k in range(len(args))]
        + [spec(pl.ANY)] * len(after),
        out_specs=(*[spec(pltpu.HBM if k in kept else pltpu.VMEM) for k in range(len(outs))], spec(pltpu.VMEM)),
        scratch_shapes=list(scratch) + buffers + semaphores,
        compiler_params=pltpu.CompilerParams(vmem_limit_bytes=size + extra + MARGIN),
        cost_estimate=pl.CostEstimate(flops=int(micros * PACE), bytes_accessed=size, transcendentals=0),
        name=name,
    )(place, *args, *after)
    TOKENS.update((id(value), (value, token)) for value in result)
    return result


def normalize(rows):
    centered = rows - jnp.mean(rows, axis=-1, keepdims=True)
    scale = lax.rsqrt(jnp.mean(centered * centered, axis=-1, keepdims=True) + 1e-05)
    return centered * scale, scale


def norm_back(grad, scaled, scale, gain):
    weighted = grad * gain
    mean_one = jnp.mean(weighted, axis=-1, keepdims=True)
    mean_two = jnp.mean(weighted * scaled, axis=-1, keepdims=True)
    return scale * (weighted - mean_one - scaled * mean_two)


def column_sum(rows):
    return jnp.sum(rows, axis=0, keepdims=True)


def rope_tables():
    position = jnp.arange(SEQ, dtype=F32)
    frequency = 10000.0 ** (-jnp.arange(0, HEAD_DIM, 2, dtype=F32) / HEAD_DIM)
    angles = position[:, None] * frequency[None, :]
    cos, sin = jnp.cos(angles), jnp.sin(angles)
    return jnp.tile(cos, (1, 8)), jnp.tile(jnp.concatenate([-sin, sin], axis=1), (1, 4))


def swapped(rows):
    low = lax.broadcasted_iota(jnp.int32, rows.shape, 1) % HEAD_DIM < HEAD_DIM // 2
    return jnp.where(low, pltpu.roll(rows, 128 - HEAD_DIM // 2, 1), pltpu.roll(rows, HEAD_DIM // 2, 1))


def group_heads():
    for head in range(GROUP_HEADS):
        yield head, (head // 4) * 128, head % 4


def head_only(rows, lane):
    owner = lax.broadcasted_iota(jnp.int32, rows.shape, 1) // HEAD_DIM
    return jnp.where(owner == lane, rows, jnp.zeros_like(rows))


def halves(place):
    core = place[1]
    return pl.multiple_of(core * HALF, 16), pl.multiple_of((1 - core) * HALF, 16)


def first_norm_kernel(place, move, tokens, vectors, hidden):
    scaled, _ = normalize(tokens[...].astype(F32))
    hidden[...] = (scaled * vectors[0:1, :] + vectors[1:2, :]).astype(BF16)


def stack_into(out, parts):
    for source, part in enumerate(parts):
        out[source] = part[...]


def line_kernel(place, move, *refs):
    stack_into(refs[5], refs[:4])
    refs[6][...] = refs[4][...]


def make_line(place, parts, cargo, after):
    outs = [shape((4, *parts[0].shape)), shape(cargo.shape)]
    return call(line_kernel, "line", outs, place, (*parts, cargo), 0.6, after=after)


def pack_kernel(place, move, *refs):
    groups, shards, (packed, ups, downs) = refs[:3], refs[3:7], refs[7:]
    stack_into(packed, groups)
    rows = ups.shape[0] // 4
    for source in range(4):
        ups[source * rows : (source + 1) * rows, :] = shards[source][:rows, :]
        downs[source * rows : (source + 1) * rows, :] = shards[source][rows:, :]


def pack(place, groups, shards, after):
    outs = [shape((3, *groups[0].shape))] + [shape((2 * shards[0].shape[0], D))] * 2
    return call(pack_kernel, "pack", outs, place, (*groups, *shards), 1.0, after=after)


def attention_forward_kernel(groups, place, move, hidden, bias, cos, sin, *refs):
    flush, fetch = move
    count = len(groups)
    mine, other, *refs = refs
    if len(refs) > 7 * count:
        refs[-1][...] = refs[0][...]
        refs = refs[1:-1]
    weights, weights_out, qs, ks, vs, probs, mixed = [refs[part * count : (part + 1) * count] for part in range(7)]
    z = place[0]
    first, second = halves(place)
    rows = hidden[...]
    windows = rows.shape[0] // SEQ
    for step, which in enumerate(groups):
        weight, prob_out = weights[step], probs[step]
        group = place[2] ^ which
        for part in range(4):
            source = lax.rem(part + 4 - z, 4)
            pieces = mine[step, source], other[step, source]
            for offset, piece in zip((first, second), pieces):
                if part < 3:
                    weight[part, pl.ds(offset, HALF), :] = piece
                else:
                    weights_out[step][pl.ds(offset, HALF), :] = piece
            if part < 3:
                weight[part, GROUP:WIDE, :] = jnp.zeros((WIDE - GROUP, D), BF16)
        flush(weight)
        for part, out in ((0, qs[step]), (1, ks[step]), (2, vs[step])):
            proj = nt(rows, weight[part]) + bias[group, part : part + 1, :]
            for window in range(windows):
                span = slice(window * SEQ, (window + 1) * SEQ)
                for tile in (0, 128):
                    piece = proj[span, tile : tile + 128]
                    if part < 2:
                        piece = piece * cos[...] + swapped(piece) * sin[...]
                    out[span, tile : tile + 128] = piece.astype(BF16)
            flush(out)
        for window in range(windows):
            span = slice(window * SEQ, (window + 1) * SEQ)
            visible = lax.broadcasted_iota(jnp.int32, (SEQ, 1), 0) < place[4 + window]
            probs_of, values_of = [], []
            for head, tile, lane in group_heads():
                keys = head_only(ks[step][span, tile : tile + 128], lane)
                scores = nt(keys, qs[step][span, tile : tile + 128])
                scores = jnp.where(visible, scores, -1e30)
                top = jnp.max(scores, axis=0, keepdims=True)
                exponent = jnp.exp2((scores - top) * (SCALE * LOG2_E))
                prob = (exponent * (1.0 / column_sum(exponent))).astype(BF16)
                prob_out[window * GROUP_HEADS + head] = prob
                flush(prob_out, window * GROUP_HEADS + head)
                probs_of.append(prob)
                values_of.append(head_only(vs[step][span, tile : tile + 128], lane))
            out = tn(jnp.concatenate(probs_of[:4], axis=0), jnp.concatenate(values_of[:4], axis=0))
            mixed[step][0:128, span] = out.astype(BF16).T
            mixed[step][128:GROUP, span] = tn(probs_of[4], values_of[4]).astype(BF16).T[0 : GROUP - 128]


def attention_forward(groups, place, hidden, bias, cos, sin, mine, other, after, cargo=()):
    rows = hidden.shape[0]
    maps = rows // SEQ * GROUP_HEADS
    count = len(groups)
    kinds = [Kept((3, WIDE, D)), shape((GROUP, D))] + [Kept((rows, WIDE))] * 3
    kinds += [Kept((maps, SEQ, SEQ)), shape((GROUP, rows))]
    out = call(
        functools.partial(attention_forward_kernel, groups), "attention_forward",
        [kind for kind in kinds for _ in groups] + [shape(value.shape) for value in cargo], place,
        (hidden, bias, cos, sin, mine, other, *cargo), 4.8 * count,
        after=after, copies=count * (4 + maps),
    )
    return [out[step : 7 * count : count] for step in range(count)] + out[7 * count :]


def take_halves(along_y, along_x, first, second):
    first[...] = along_x[0 : QUARTER // 2, :]
    second[...] = along_y[QUARTER // 2 : QUARTER, :]


def halves_kernel(place, move, *refs):
    take_halves(*refs)


def neighbours_halves(place, along_y, along_x, after):
    outs = [shape((QUARTER // 2, D))] * 2
    return call(halves_kernel, "halves", outs, place, (along_y, along_x), 0.6, after=after)


def middle_kernel(place, move, tokens, vectors, *refs):
    flush, fetch = move
    mixed_in, weight_in, *refs = refs[:4], refs[4:8], *refs[8:]
    if len(refs) > 5:
        take_halves(*refs[:2], *refs[7:9])
        refs[9][...] = refs[2][...]
        refs = refs[3:7] + refs[10:]
    middle, normed, mixed, weight, stage = refs
    for which in range(GROUPS):
        offset = pl.multiple_of((place[2] ^ which) * GROUP, 32)
        stage[pl.ds(offset, GROUP), :] = mixed_in[which][...]
        weight[pl.ds(offset, GROUP), :] = weight_in[which][...]
    mixed[...] = stage[...].T
    flush(weight)
    flush(mixed)
    rows = tokens[...].astype(F32) + nt(mixed[...], weight[...]) + vectors[5:6, :]
    middle[...] = rows
    flush(middle)
    scaled, _ = normalize(rows)
    normed[...] = (scaled * vectors[6:7, :] + vectors[7:8, :]).astype(BF16)


def middle_layer(place, tokens, vectors, mixed, weights, cargo):
    rows = tokens.shape[0]
    outs = [Kept((rows, D), F32), shape((rows, D)), Kept((rows, D)), Kept((D, D))]
    outs += [shape((QUARTER // 2, D))] * 2 + [shape((QUARTER, D))] if cargo else []
    return call(
        middle_kernel, "middle", outs, place, (tokens, vectors, *mixed, *weights, *cargo), 2.5,
        [pltpu.VMEM((D, rows), BF16)],
    )


def store_quarter(outs, which, value, flush):
    low = value.astype(BF16)
    if which < 3:
        outs[which][...] = low
    else:
        outs[3][...], outs[4][...] = low[: QUARTER // 2], low[QUARTER // 2 :]
    for out in outs[which : which + 1] if which < 3 else outs[3:5]:
        flush(out)


def five_parts():
    return [Kept((QUARTER, D))] * 3 + [Kept((QUARTER // 2, D))] * 2


def quarter(parts, which):
    if which < 3:
        return parts[which][...]
    return jnp.concatenate([parts[3][...], parts[4][...]], axis=0)


def hidden_forward_kernel(quarters, place, move, *refs):
    flush, fetch = move
    count = 2 if 3 in quarters else len(quarters)
    parts, (bias, normed, normed_pair, back, back_pair), refs = refs[:count], refs[count : count + 5], refs[count + 5 :]
    active, slopes, grads_down = refs[0], refs[1 : 1 + len(quarters)], refs[1 + len(quarters) :]
    rows = normed.shape[0]
    for step, which in enumerate(quarters):
        if which < 3:
            up = fetch(parts[step])[...]
        else:
            up = quarter((None, None, None, *parts), which)
        column = jnp.broadcast_to(bias[which], (8, QUARTER)).T[:, 0:1]
        total = 0.0
        for part, inputs, grads in ((0, normed, back), (1, normed_pair, back_pair)):
            span = slice(part * rows, (part + 1) * rows)
            pre = nt(up, inputs[...]) + column
            cdf = 0.5 + 0.5 * lax.erf(pre * (0.5**0.5))
            low = (pre * cdf).astype(BF16)
            active[step, :, span] = low
            slopes[step][:, span] = (cdf + pre * jnp.exp(-0.5 * pre * pre) * 0.3989422804014327).astype(BF16)
            total = total + nn(low, grads[...])
        flush(active, step)
        if which < 3:
            store_quarter(grads_down, which, total, flush)
        else:
            store_quarter((None, None, None, *grads_down), which, total, flush)


def hidden_forward(quarters, place, parts, bias, normed, normed_pair, back, back_pair, after):
    rows = 2 * normed.shape[0]
    count = len(quarters)
    kinds = five_parts()
    outs = [Kept((count, QUARTER, rows))] + [shape((QUARTER, rows))] * count
    outs += kinds[3:] if 3 in quarters else kinds[:count]
    active, *rest = call(
        functools.partial(hidden_forward_kernel, quarters), "hidden_forward", outs, place,
        (*[part if 3 in quarters else Far(part) for part in parts], bias, normed, normed_pair, back, back_pair),
        2.2 * count, after=after, copies=len(outs),
    )
    return active, rest[:count], rest[count:]


def far_first(parts):
    return [Far(part) for part in parts[:3]] + list(parts[3:])


def hidden_backward_kernel(place, move, *refs):
    ups, downs, slopes, (back, back_pair), refs = refs[:5], refs[5:10], refs[10:14], refs[14:16], refs[16:]
    grad_pre, own, pair, up = refs
    rows = back.shape[0]
    for part in (*ups[:3], *downs[:3]):
        move[1](part)
    for which in range(4):
        units = slice(which * QUARTER, (which + 1) * QUARTER)
        up[units, :] = quarter(ups, which)
        down = quarter(downs, which)
        for part, grads in ((0, back), (1, back_pair)):
            span = slice(part * rows, (part + 1) * rows)
            wide = nt(down, grads[...]) * slopes[which][:, span].astype(F32)
            grad_pre[units, span] = wide.astype(BF16)
    for out, span in ((pair, slice(rows, 2 * rows)), (own, slice(0, rows))):
        out[...] = tn(grad_pre[:, span], up[...]).astype(out.dtype)


def hidden_backward(place, ups, downs, slopes, back, back_pair):
    rows = back.shape[0]
    outs = [shape((4 * QUARTER, 2 * rows)), shape((rows, D), F32), shape((rows, D))]
    return call(
        hidden_backward_kernel, "hidden_backward", outs, place,
        (*far_first(ups), *far_first(downs), *slopes, back, back_pair), 6.0, [pltpu.VMEM((4 * QUARTER, D), BF16)],
    )


def up_gradient_kernel(place, move, grad_pre, normed, normed_pair, *refs):
    grads, grad_bias = refs[:5], refs[5]
    rows = normed.shape[0]
    for which in range(4):
        units = slice(which * QUARTER, (which + 1) * QUARTER)
        low = grad_pre[units, :]
        store_quarter(grads, which, nn(low[:, :rows], normed[...]) + nn(low[:, rows:], normed_pair[...]), move[0])
        bias = jnp.sum(low.astype(F32), axis=1, keepdims=True)
        for source in range(4):
            grad_bias[4 * which + source] = jnp.broadcast_to(bias[source * 80 : (source + 1) * 80], (80, 8)).T


def up_gradient(place, grad_pre, normed, normed_pair, after):
    outs = five_parts() + [shape((16, 8, 80), F32)]
    *grads, bias = call(
        up_gradient_kernel, "up_gradient", outs, place, (grad_pre, normed, normed_pair), 4.0, after=after
    )
    return grads, bias


def output_kernel(place, move, most, rest, middle, vectors, *refs):
    parts, (own, pair) = refs[:5], refs[5:]
    rows = own.shape[0]
    down = jnp.concatenate([quarter(parts, which) for which in range(4)], axis=0)
    for out, span in ((pair, slice(rows, 2 * rows)), (own, slice(0, rows))):
        left = jnp.concatenate([most[which, :, span] for which in range(3)] + [rest[0, :, span]], axis=0)
        total = tn(left, down)
        if out is own:
            total = total + move[1](middle)[...] + vectors[8:9, :]
        out[...] = total.astype(out.dtype)


def output_layer(place, most, rest, middle, vectors, parts, after):
    rows = most.shape[2] // 2
    outs = [shape((rows, D), F32), shape((rows, D))]
    return call(
        output_kernel, "output", outs, place, (most, rest, Far(middle), vectors, *parts), 2.8, after=after
    )


def middle_backward_kernel(
    place, move, own, pair, middle, back, vectors, mixed, weight, grad_middle, sums, grad_mixed, mine, other, stage, stage_mixed
):
    grad = own[...] + pair[...].astype(F32)
    scaled, scale = normalize(middle[...])
    wide = back[...].astype(F32)
    total = wide + norm_back(grad, scaled, scale, vectors[6:7, :])
    grad_middle[...] = total
    sums[0:1, :] = column_sum(total)
    sums[1:2, :] = column_sum(grad * scaled)
    sums[2:3, :] = column_sum(grad)
    sums[3:4, :] = column_sum(wide)
    sums[4:8, :] = jnp.zeros((4, D), F32)
    low = total.astype(BF16)
    stage_mixed[...] = nt(weight[...].T, low).astype(BF16)
    stage[...] = tn(low, mixed[...]).astype(BF16)
    first, second = halves(place)
    for which in range(GROUPS):
        offset = (place[2] ^ which) * GROUP
        grad_mixed[which] = stage_mixed[pl.ds(pl.multiple_of(offset, 32), GROUP), :]
        mine[which] = stage[pl.ds(pl.multiple_of(offset + first, 16), HALF), :]
        other[which] = stage[pl.ds(pl.multiple_of(offset + second, 16), HALF), :]


def middle_backward(place, own, pair, middle, back, vectors, mixed, weight, after):
    rows = own.shape[0]
    outs = [shape((rows, D), F32), shape((8, D), F32), shape((GROUPS, GROUP, rows))]
    outs += [shape((GROUPS, HALF, D)), shape((GROUPS, HALF, D))]
    return call(
        middle_backward_kernel, "middle_backward", outs, place,
        (own, pair, middle, back, vectors, mixed, weight), 3.0,
        [pltpu.VMEM((D, D), BF16), pltpu.VMEM((D, rows), BF16)], after,
    )


def attention_backward_kernel(groups, place, move, grad_mixed, hidden, cos, sin, out_mine, out_other, *refs):
    count = len(groups)
    qs, ks, vs, probs, dqs, dks, dvs = [refs[part * count : (part + 1) * count] for part in range(7)]
    biases, (mine, other, stage) = refs[7 * count : 8 * count], refs[8 * count :]
    rows = hidden.shape[0]
    first, second = halves(place)
    for step, which in enumerate(groups):
        q, k, v, prob_in, dq_out, dk_out, dv_out = (
            qs[step], ks[step], vs[step], probs[step], dqs[step], dks[step], dvs[step]
        )
        for window in range(rows // SEQ):
            span = slice(window * SEQ, (window + 1) * SEQ)
            grad = grad_mixed[which, :, span].T
            tail = jnp.concatenate([grad[:, 128:GROUP], jnp.zeros((SEQ, WIDE - GROUP), BF16)], axis=1)
            grads = {0: grad[:, :128], 128: tail}
            lows, slopes, grads_of, queries_of, keys_of = [], [], [], [], []
            for head, tile, lane in group_heads():
                cols = slice(tile, tile + 128)
                low = prob_in[window * GROUP_HEADS + head]
                prob = low.astype(F32)
                weighted = prob * nt(head_only(v[span, cols], lane), grads[tile])
                lows.append(low)
                slopes.append((weighted - prob * column_sum(weighted)).astype(BF16))
                grads_of.append(head_only(grads[tile], lane))
                queries_of.append(head_only(q[span, cols], lane))
                keys_of.append(head_only(k[span, cols], lane))
            for tile, heads in ((0, slice(0, 4)), (128, slice(4, 5))):
                cols = slice(tile, tile + 128)
                down = jnp.concatenate(slopes[heads], axis=1)
                dv_out[span, cols] = nn(
                    jnp.concatenate(lows[heads], axis=1), jnp.concatenate(grads_of[heads], axis=0)
                ).astype(BF16)
                piece = nn(down, jnp.concatenate(queries_of[heads], axis=0)) * SCALE
                dk_out[span, cols] = (piece * cos[...] - swapped(piece) * sin[...]).astype(BF16)
                piece = tn(jnp.concatenate(slopes[heads], axis=0), jnp.concatenate(keys_of[heads], axis=0)) * SCALE
                dq_out[span, cols] = (piece * cos[...] - swapped(piece) * sin[...]).astype(BF16)
        biases[step][...] = jnp.zeros((8, WIDE), F32)
        for part, out in ((0, dq_out), (1, dk_out), (2, dv_out)):
            values = out[...]
            stage[step, part] = tn(values, hidden[...]).astype(BF16)
            mine[step, part] = stage[step, part, pl.ds(first, HALF), :]
            other[step, part] = stage[step, part, pl.ds(second, HALF), :]
            biases[step][part : part + 1, :] = column_sum(values.astype(F32))
        mine[step, 3] = out_mine[which]
        other[step, 3] = out_other[which]


def attention_backward(groups, place, grad_mixed, hidden, cos, sin, out_mine, out_other, saved, after):
    rows = hidden.shape[0]
    count = len(groups)
    outs = [shape((rows, WIDE))] * (3 * count) + [shape((8, WIDE), F32)] * count + [shape((count, 4, HALF, D))] * 2
    *out, mine, other = call(
        functools.partial(attention_backward_kernel, groups), "attention_backward", outs, place,
        (grad_mixed, hidden, cos, sin, out_mine, out_other, *[group[k] for k in range(4) for group in saved]),
        4.7 * count,
        [pltpu.VMEM((count, 3, WIDE, D), BF16)], after,
    )
    return [out[step::count] for step in range(count)], mine, other


def first_backward_kernel(place, move, tokens, grad_middle, vectors, *refs):
    parts, weights, biases, (middle_sums, units), refs = refs[:12], refs[12:16], refs[16:20], refs[20:22], refs[22:]
    input_grad, sums, unit_rows = refs
    z, plane, core = place[0], place[2], place[3]
    grad = 0.0
    for which in range(GROUPS):
        for part in range(3):
            grad = grad + nn(parts[which * 3 + part][...], weights[which][part])
    scaled, scale = normalize(tokens[...].astype(F32))
    input_grad[...] = (grad_middle[...] + norm_back(grad, scaled, scale, vectors[0:1, :])).astype(BF16)
    sums[...] = jnp.zeros((24, D), F32)
    sums[0:1, :] = column_sum(grad * scaled)
    sums[1:2, :] = column_sum(grad)
    sums[2:6, :] = middle_sums[0:4, :]
    for group in range(GROUPS):
        value = sum(jnp.where((plane ^ which) == group, biases[which][...], 0.0) for which in range(GROUPS))
        row, column = 8 + 4 * (group // 2), WIDE * (group % 2)
        sums[row : row + 4, column : column + WIDE] = value[0:4]
    unit_rows[...] = jnp.zeros((4, 8, 128), F32)
    for which in range(4):
        for source in range(4):
            row = (plane ^ which) * 2 + core
            unit_rows[z ^ source, pl.ds(row, 1), 0:80] = units[4 * which + source, 0:1, :]
    for line in range(4):
        sums[16:24, line * 128 : (line + 1) * 128] = unit_rows[line]


def first_backward(place, tokens, grad_middle, vectors, parts, weights, biases, middle_sums, units, after):
    rows = tokens.shape[0]
    outs = [shape((rows, D)), shape((24, D), F32)]
    return call(
        first_backward_kernel, "first_backward", outs, place,
        (tokens, grad_middle, vectors, *parts, *weights, *biases, middle_sums, units),
        0.2, [pltpu.VMEM((4, 8, 128), F32)], after,
    )


def unpack_vector(sums):
    group_rows = [sums[8 + 4 * (g // 2) :, WIDE * (g % 2) :][:3, :GROUP] for g in range(GROUPS)]
    units = sums[16:24, :512].reshape(8, 4, 128)[:, :, :80].transpose(1, 0, 2).reshape(4, D)
    return jnp.concatenate([sums[0:2], jnp.concatenate(group_rows, axis=1), sums[2:6], units])


def ordered_sum_kernel(which, place, move, *refs):
    total = 0.0
    for index in range(4):
        total = total + sum(jnp.where((place[which] ^ step) == index, refs[step][...], 0.0) for step in range(4))
    refs[4][...] = total


def ordered_sum(place, which, parts, after=()):
    outs = [shape(parts[0].shape, F32)]
    return call(functools.partial(ordered_sum_kernel, which), "ordered_sum", outs, place, parts, 0.6, after=after)[0]


def attention_sum_kernel(place, move, *refs):
    parts, (own, *sent), stage = refs[:4], refs[4:8], refs[8]
    stage[...] = sum(value[...].astype(F32) for value in parts[2:]) + sum(value[1].astype(F32) for value in parts[:2])
    own[...] = stage[place[0]]
    for steps, out in enumerate(sent):
        out[...] = stage[lax.rem(place[0] + steps + 1, 4)].astype(BF16)


def attention_sum(place, parts, after):
    dims = parts[2].shape
    outs = [shape(dims[1:], F32)] + [shape(dims[1:])] * 3
    return call(
        attention_sum_kernel, "attention_sum", outs, place, parts, 1.0, [pltpu.VMEM(dims, F32)], after=after
    )


def add(out, *parts):
    out[...] = sum(part.astype(F32) for part in parts).astype(out.dtype)


def keep_and_send(parts, keep, sent):
    total = sum(part[...].astype(F32) for part in parts)
    keep[...] = total[0:2]
    sent[...] = total[2:4].astype(BF16)


def merge_into(along_y, along_x, first, second, out_y, out_x):
    out_y[0:2] = along_y[0:2]
    add(out_y.at[2:4], along_y[2:4], second[...])
    add(out_x.at[0:2], along_x[0:2], first[...])
    out_x[2:4] = along_x[2:4]


def merge_kernel(place, move, along_y, along_x, *refs):
    for ref in (along_y, along_x):
        move[1](ref)
    merge_into(along_y, along_x, *refs)


def merge(place, along_y, along_x, first, second, after):
    outs = [shape(along_y.shape)] * 2
    return call(merge_kernel, "merge", outs, place, (Far(along_y), Far(along_x), first, second), 1.5, after=after)


def exchange_one_kernel(place, move, *refs):
    downs, (along_y, along_x, first, second), refs = refs[:3], refs[3:7], refs[7:]
    keep, sent, out_y, out_x = refs
    for ref in (downs[0], along_y, along_x):
        move[1](ref)
    keep_and_send(downs, keep, sent)
    merge_into(along_y, along_x, first, second, out_y, out_x)


def exchange_one(place, downs, ups, after):
    dims = downs[0].shape
    outs = [shape((2, *dims[1:]), F32), shape((2, *dims[1:]))] + [shape(dims)] * 2
    return call(
        exchange_one_kernel, "exchange_one", outs, place,
        (Far(downs[0]), *downs[1:], Far(ups[0]), Far(ups[1]), *ups[2:]), 2.0, after=after,
    )


def cores_one_kernel(place, move, mine, other, half_y, half_x, rest):
    add(half_y, mine[0, 0:2], other[0, 0:2])
    add(half_x, mine[0, 2:4], other[0, 2:4])
    add(rest, mine[1], other[1])


def cores_one(place, mine, other, after):
    dims = mine.shape[1:]
    outs = [shape((2, *dims[1:]))] * 2 + [shape(dims)]
    return call(cores_one_kernel, "cores_one", outs, place, (mine, other), 1.0, after=after)


def exchange_two_kernel(place, move, *refs):
    ups, (keep_in, line_in), (keep, sent, own, line) = refs[:3], refs[3:5], refs[5:]
    move[1](ups[0])
    keep_and_send(ups, keep, sent)
    total = keep_in[...] + line_in[...].astype(F32)
    own[...] = total[0]
    line[...] = total[1].astype(BF16)


def exchange_two(place, ups, keep, line, after):
    dims = ups[0].shape
    outs = [shape((2, *dims[1:]), F32), shape((2, *dims[1:])), shape(dims[1:], F32), shape(dims[1:])]
    return call(
        exchange_two_kernel, "exchange_two", outs, place, (Far(ups[0]), *ups[1:], keep, line), 12.0, after=after
    )


def exchange_three_kernel(
    place, move, rest, mine, other, first, second, keep, line_in, down_line, along_y, along_x, own, line
):
    add(along_x.at[0:2], rest[0:2], first[...])
    along_x[2:4] = rest[2:4]
    add(along_y.at[0:2], mine[0, 0:2], other[0, 0:2])
    add(along_y.at[2:4], mine[0, 2:4], other[0, 2:4], second[...])
    total = keep[...] + line_in[...].astype(F32)
    own[...] = total[0]
    line[0] = total[1].astype(BF16)
    line[1] = down_line[...]


def exchange_three(place, rest, mine, other, halves_in, keep, line, down_line, after):
    dims = rest.shape
    outs = [shape(dims)] * 2 + [shape(dims[1:], F32), shape((2, *dims[1:]))]
    return call(
        exchange_three_kernel, "exchange_three", outs, place, (rest, mine, other, *halves_in, keep, line, down_line), 1.0,
        after=after,
    )


def core_runs(place):
    for which in range(4):
        for source in range(4):
            run = ((place[0] ^ source) * 4 + (place[2] ^ which)) * 2 + place[3]
            yield which, source, pl.ds(pl.multiple_of(run * 80, 16), 80)


def take_runs_kernel(place, move, full, *outs):
    for which, source, rows in core_runs(place):
        part, offset = (which, source) if which < 3 else (3 + source // 2, source % 2)
        outs[part][offset * 80 : (offset + 1) * 80, :] = full[rows, :]


def take_runs(place, full):
    outs = [shape((QUARTER, D))] * 3 + [shape((QUARTER // 2, D))] * 2
    return call(take_runs_kernel, "take_runs", outs, place, (full,), 1.0)


def place_runs_kernel(place, move, *refs):
    full = refs[5]
    full[...] = jnp.zeros_like(full)
    for which, source, rows in core_runs(place):
        part, offset = (which, source) if which < 3 else (3 + source // 2, source % 2)
        full[rows, :] = refs[part][offset * 80 : (offset + 1) * 80, :].astype(F32)


def place_runs(place, quarters):
    return call(place_runs_kernel, "place_runs", [shape((FF, D), F32)], place, quarters, 2.0)[0]


def pick(array, index):
    return lax.dynamic_index_in_dim(array, index, 0, keepdims=False)


def step_into(rate, gradient, state, outs):
    weight, first, second = state
    grad, second_new, new = outs
    grad[...] = gradient
    second_new[...], new[...] = adamw(weight[...], first[...], second[...], gradient, rate)


def finish_attention_kernel(place, move, own, one, two, three, weight, first, second, *outs):
    total = own[...]
    for value in (one, two, three):
        total = total + value[...].astype(F32)
    step_into(0.1, total, (weight, first, second), outs)


def finish_attention(place, own, line, state, after):
    out = call(
        finish_attention_kernel, "finish_attention", [shape(own.shape, F32)] * 3, place,
        (own, *line, *[value.T for value in state]), 0.3, after=after,
    )
    return [value.T for value in out]


def finish_hidden_kernel(place, move, *refs):
    owns, arrived, refs = refs[:2], refs[2], refs[3:]
    for matrix in range(2):
        state = refs[3 * matrix : 3 * matrix + 3]
        for ref in state:
            move[1](ref)
        outs = refs[6 + 3 * matrix : 9 + 3 * matrix]
        step_into(0.1, owns[matrix][...] + arrived[matrix].astype(F32), state, outs)


def finish_hidden(place, owns, arrived, state, after):
    out = call(
        finish_hidden_kernel, "finish_hidden", [shape(owns[0].shape, F32)] * 6, place,
        (*owns, arrived, *[Far(value.T) for value in state]), 0.3, after=after,
    )
    return [value.T for value in out[:3]], [value.T for value in out[3:]], out[0]


def result_kernel(place, move, own, pair, out):
    out[...] = (own[...] + pair[...].astype(F32)).astype(BF16)


def result_layer(place, own, pair, after):
    return call(result_kernel, "result", [shape(pair.shape)], place, (own, pair), 12.0, after=after)[0]


def adamw(weight, first_moment, second_moment, gradient, rate_value):
    first_new = 0.9 * first_moment + 0.1 * gradient
    second_new = 0.999 * second_moment + 0.001 * gradient * gradient
    corrected = first_new / (1.0 - 0.9**STEP) / (jnp.sqrt(second_new / (1.0 - 0.999**STEP)) + 1e-08)
    return (second_new, weight - rate_value * (corrected + 0.01 * weight))


class Layout:
    def __init__(self, total):
        self.total = total
        self.block = 4 * D // total
        self.stride = total // 4
        self.me = lax.axis_index(AXES)
        self.core = lax.rem(self.me, 2)

    def swap(self, value, mask):
        return lax.ppermute(value, AXES, [(i, i ^ mask) for i in range(self.total)])

    def shift(self, value, steps):
        pairs = [(i, (i + self.stride * steps) % self.total) for i in range(self.total)]
        return lax.ppermute(value, AXES, pairs)


    def hidden_index(self):
        order = jnp.arange(16)
        z, plane = self.place[0], self.place[2]
        return ((z ^ lax.rem(order, 4)) * 4 + (plane ^ (order // 4))) * 2 + self.core


class Ring(Layout):
    def __init__(self, total):
        super().__init__(total)
        self.ring = True
        self.z = self.me // 8
        self.plane = lax.rem(self.me // 2, 4)
        self.place = (self.z, self.core, self.plane)

    def along_z(self, value):
        return [value] + [self.shift(value, -s) for s in (1, 2, 3)]

    def in_plane(self, value, each=None):
        return [value] + [self.swap(each[r].reshape(value.shape) if each else value, 2 * r) for r in (1, 2, 3)]

    def corner(self, *value):
        return [self.swap(value[0], 2), self.swap(value[1], 4)]

    def send_plane(self, along_y, along_x):
        return [self.swap(along_y, 2), self.swap(along_x, 4)]

    def all_total(self, value, after):
        value = ordered_sum(self.vector, 2, self.in_plane(value), after)
        return ordered_sum(self.vector, 0, [value] + [self.swap(value, 8 * s) for s in (1, 2, 3)])


class Whole(Layout):
    def __init__(self, total):
        super().__init__(total)
        self.ring = False
        self.plane = jnp.int32(0)
        self.place = (jnp.int32(0),) * 3

    def gather_core(self, shard):
        return take_runs(self.vector, lax.all_gather(shard, AXES, axis=0, tiled=True))

    def gather(self, attn, up, down):
        full = lax.all_gather(attn, AXES, axis=0, tiled=True).reshape(4, 4, 2, HALF, D)
        mine = [full[:, r, 0] for r in range(4)]
        other = [full[:, r, 1] for r in range(4)]
        return mine, other, self.gather_core(up), self.gather_core(down)

    def scatter_hidden(self, grads):
        return lax.psum_scatter(place_runs(self.vector, grads), AXES, scatter_dimension=0, tiled=True)

    def scatter_attention(self, mine, other):
        full = jnp.stack([jnp.stack(mine, axis=1), jnp.stack(other, axis=1)], axis=2)
        return lax.psum_scatter(full.astype(F32).reshape(4 * D, D), AXES, scatter_dimension=0, tiled=True)


def per_device(
    total,
    tokens,
    cotangent,
    lengths,
    offsets,
    attn_weight,
    attn_first,
    attn_second,
    up_weight,
    up_first,
    up_second,
    down_weight,
    down_first,
    down_second,
    vectors,
    vec_first,
    vec_second,
):
    TOKENS.clear()
    lay = Ring(total) if total == 32 else Whole(total)
    counts = jnp.minimum(lengths - offsets, SEQ).reshape(-1)
    rows = counts.shape[0] * SEQ
    place = lay.vector = jnp.concatenate([jnp.stack([*lay.place, lay.core]).astype(jnp.int32), counts])
    cos, sin = rope_tables()

    flat = tokens.reshape(rows, D)
    back = cotangent.reshape(rows, D)
    back_pair = lay.swap(back, 1)
    (hidden,) = call(first_norm_kernel, "first_norm", [shape((rows, D))], place, (flat, vectors), 1.0)
    bias = jnp.pad(vectors[2:5].reshape(3, GROUPS, GROUP).transpose(1, 0, 2), ((0, 0), (0, 0), (0, WIDE - GROUP)))

    chosen = (lay.hidden_index()[:, None] == jnp.arange(32)[None, :]).astype(F32)
    bias_up = jnp.dot(chosen, vectors[9:].reshape(32, 80), precision=lax.Precision.HIGHEST).reshape(4, 1, QUARTER)

    if lay.ring:
        shards = jnp.concatenate([up_weight.T, down_weight.T]).astype(BF16)
        attn_parts = lay.along_z(attn_weight.T.astype(BF16))
        line, shards = make_line(place, attn_parts, shards, [hidden, bias_up, bias])
        far_shard = lay.swap(shards, 16)
        groups = lay.in_plane(line)[1:]
        other = lay.swap(line, 1)
        mine = line[None]
    else:
        mine, other, ups, downs = lay.gather(
            attn_weight.T.astype(BF16), up_weight.T.astype(BF16), down_weight.T.astype(BF16)
        )
        mine, packed = mine[0][None], jnp.stack(mine[1:])
        other, packed_other = other[0], jnp.stack(other[1:])
    forward = attention_forward(
        (0,), place, hidden, bias, cos, sin, mine, other[None], [], [shards] if lay.ring else []
    )
    if lay.ring:
        shards = forward.pop()
        shards = [shards, lay.swap(shards, 8), far_shard, lay.swap(far_shard, 8)]
        packed, up_line, down_line = pack(place, groups, shards, [forward[0][2]])
        ups = [up_line, lay.swap(up_line, 2), lay.swap(up_line, 4)]
        packed_other = lay.swap(packed, 1)
    forward += attention_forward((1, 2, 3), place, hidden, bias, cos, sin, packed, packed_other, [forward[0][2]])
    weights = [group[0] for group in forward]
    middle, normed, mixed, out_weight, *corners = middle_layer(
        place, flat, vectors, [group[6] for group in forward], [group[1] for group in forward],
        [*ups[1:], down_line] if lay.ring else [],
    )
    if lay.ring:
        ups = ups + lay.corner(*corners[:2])
        downs = [corners[2], lay.swap(corners[2], 2), lay.swap(corners[2], 4)]
    normed_pair = lay.swap(normed, 1)
    both = (normed, normed_pair, back, back_pair)
    most, slope, grad_down = hidden_forward((0, 1, 2), place, ups[:3], bias_up, *both, [])
    after = [most]
    if lay.ring:
        corners = neighbours_halves(place, *downs[1:], after)
        after = corners[:1]
        downs = downs + lay.corner(*corners)
    rest, *last = hidden_forward((3,), place, ups[3:], bias_up, *both, after)
    slope, grad_down = slope + last[0], grad_down + last[1]
    if lay.ring:
        grad_down = [value.reshape(-1, 80, D) for value in grad_down]
        down_corner = lay.corner(*grad_down[3:])
    grad_pre, own, pair = hidden_backward(place, ups, downs, slope, back, back_pair)
    gradient_after, middle_after, after = [], [], []
    if lay.ring:
        down_sent = merge(place, *grad_down[1:3], *down_corner, [own])
        gradient_after = down_sent[:1]
        down_sent = middle_after = lay.send_plane(*down_sent)
    grad_up, grad_bias_up = up_gradient(place, grad_pre, normed, normed_pair, gradient_after)
    if lay.ring:
        grad_up = [value.reshape(-1, 80, D) for value in grad_up]
        up_corner = lay.corner(*grad_up[3:])
    out_own, out_pair = output_layer(place, most, rest, middle, vectors, downs, [grad_bias_up])
    out_pair = lay.swap(out_pair, 1)
    grad_middle, sums, grad_mixed, out_mine, out_other = middle_backward(
        place, own, lay.swap(pair, 1), middle, back, vectors, mixed, out_weight, [out_own] + middle_after
    )

    def backward_of(groups, after):
        saved = [forward[r][2:6] for r in groups]
        return attention_backward(groups, place, grad_mixed, hidden, cos, sin, out_mine, out_other, saved, after)

    if lay.ring:
        keep, line, *up_sent = exchange_one(place, [grad_down[0], *down_sent], [*grad_up[1:3], *up_corner], [sums])
        down_line = lay.swap(line, 16)
        up_sent = lay.send_plane(*up_sent)
        after = [keep]
    later, mine_one, other_one = backward_of((3, 2), after)
    after = [later[0][0]]
    if lay.ring:
        other_one = lay.swap(other_one, 1)
        up_keep, up_line, down_own, down_line = exchange_two(
            place, [grad_up[0], *up_sent], keep, down_line, after
        )
        up_line = lay.swap(up_line, 16)
        *attn_corner, along_x = cores_one(place, mine_one, other_one, [up_keep])
        attn_corner = lay.corner(*attn_corner)
        after = [up_keep, along_x]
    sooner, mine_two, other_two = backward_of((1, 0), after)
    backward = [sooner[1], sooner[0], later[1], later[0]]
    other_two, after = lay.swap(other_two, 1) if lay.ring else other_two, [sooner[0][0]]
    if lay.ring:
        after += [*attn_corner, up_line]
    result = result_layer(place, out_own, out_pair, after)
    if lay.ring:
        along_y, along_x, up_own, hidden_line = exchange_three(
            place, along_x, mine_two, other_two, attn_corner, up_keep, up_line, down_line, [result]
        )
        after = [along_y]
    parts = [value for group in backward for value in group[:3]]
    input_grad, vec_sums = first_backward(
        place, flat, grad_middle, vectors, parts, weights, [group[3] for group in backward], sums, grad_bias_up, after
    )
    state = up_weight, up_first, up_second, down_weight, down_first, down_second
    if lay.ring:
        along_y, along_x = lay.send_plane(along_y, along_x)
        hidden_line = lay.swap(hidden_line, 8)
        vec_core = vec_sums + lay.swap(vec_sums, 1)
        attn_own, *attn_line = attention_sum(place, [mine_two, other_two, along_y, along_x], [hidden_line, vec_core])
        vec_sums = lay.all_total(vec_core, [attn_own])
        attn_line = [lay.shift(value, s) for value, s in zip(attn_line, (1, 2, 3))]
        (grad_up, up_second_new, up_new), (grad_down, down_second_new, down_new), done = finish_hidden(
            place, [up_own, down_own], hidden_line, state, [attn_own]
        )
        grad_attn, attn_second_new, attn_new = finish_attention(
            place, attn_own, attn_line, (attn_weight, attn_first, attn_second), [done]
        )
    else:
        grad_up, grad_down = lay.scatter_hidden(grad_up).T, lay.scatter_hidden(grad_down).T
        order = (mine_two[1], mine_two[0], mine_one[1], mine_one[0])
        order_other = (other_two[1], other_two[0], other_one[1], other_one[0])
        grad_attn = lay.scatter_attention(order, order_other).T
        attn_second_new, attn_new = adamw(attn_weight, attn_first, attn_second, grad_attn, 0.1)
        up_second_new, up_new = adamw(*state[:3], grad_up, 0.1)
        down_second_new, down_new = adamw(*state[3:], grad_down, 0.1)
        vec_sums = lax.psum(vec_sums, AXES)
    grad_vec = unpack_vector(vec_sums)
    vec_second_new, vectors_new = adamw(vectors, vec_first, vec_second, grad_vec, 0.5)
    return (
        result.reshape(tokens.shape),
        input_grad.reshape(tokens.shape),
        grad_attn,
        grad_up,
        grad_down,
        grad_vec,
        attn_second_new,
        up_second_new,
        down_second_new,
        vec_second_new,
        attn_new,
        up_new,
        down_new,
        vectors_new,
    )


def solution(mesh):
    total = mesh.shape["wide"] * mesh.shape["narrow"]
    windows = P(None, AXES, None, None)
    counts = P(None, AXES)
    columns = P(None, AXES)
    in_specs = (windows,) * 2 + (counts,) * 2 + (columns,) * 9 + (P(),) * 3
    out_specs = (windows,) * 2 + (columns,) * 3 + (P(),) + (columns,) * 3 + (P(),) + (columns,) * 3 + (P(),)
    return jax.shard_map(
        functools.partial(per_device, total),
        mesh=mesh,
        in_specs=in_specs,
        out_specs=out_specs,
        check_vma=False,
    )
```

```python
import functools
import math

import jax
import jax.numpy as jnp
from jax import lax
from jax.experimental import pallas as pl
from jax.experimental.pallas import tpu as pltpu
from jax.sharding import PartitionSpec as P

D = 640
HEADS = 20
HEAD_DIM = 32
FF = 2560
SEQ = 256
STEP = 10
AXES = ("wide", "narrow")
GROUPS = 4
GROUP_HEADS = HEADS // GROUPS
GROUP = GROUP_HEADS * HEAD_DIM
HALF = GROUP // 2
WIDE = 256
QUARTER = FF // 8
SCALE = HEAD_DIM ** (-0.5)
LOG2_E = 1.4426950408889634
BF16 = jnp.bfloat16
F32 = jnp.float32
PACE = 1.15e9
MARGIN = 8 * 1024 * 1024


def nt(left, right):
    return lax.dot_general(left, right, (((1,), (1,)), ((), ())), preferred_element_type=F32)


def nn(left, right):
    return jnp.dot(left, right, preferred_element_type=F32)


def tn(left, right):
    return lax.dot_general(left, right, (((0,), (0,)), ((), ())), preferred_element_type=F32)


def shape(dims, kind=BF16):
    return jax.ShapeDtypeStruct(dims, kind)


TOKENS = {}


class Kept:
    def __init__(self, dims, kind=BF16):
        self.struct = shape(dims, kind)


class Far:
    def __init__(self, value):
        self.value = value


def call(kernel, name, outs, place, args, micros, scratch=(), after=(), copies=None):
    after = [TOKENS[id(value)][1] if id(value) in TOKENS else value for value in after]
    kept = [place_of for place_of, out in enumerate(outs) if isinstance(out, Kept)]
    outs = [out.struct if isinstance(out, Kept) else out for out in outs]
    far = [place_of for place_of, arg in enumerate(args) if isinstance(arg, Far)]
    args = [
        pltpu.with_memory_space_constraint(arg.value, pltpu.HBM) if isinstance(arg, Far) else arg for arg in args
    ]
    buffers = [pltpu.VMEM(a.shape, a.dtype) for a in [outs[k] for k in kept] + [args[k] for k in far]]
    copies = copies or len(kept)
    size = sum(a.size * a.dtype.itemsize for a in args) + sum(o.size * o.dtype.itemsize for o in outs)
    extra = sum(math.prod(s.shape) * s.dtype.itemsize for s in scratch)
    semaphores = [pltpu.SemaphoreType.DMA((copies + len(far),))] if buffers else []

    def body(place_ref, *refs):
        ins, refs = list(refs[: len(args)]), refs[len(args) + len(after) :]
        out_refs, token, refs = list(refs[: len(outs)]), refs[len(outs)], refs[len(outs) + 1 :]
        token[...] = jnp.zeros((8, 128), F32)
        work, held = refs[: len(scratch)], refs[len(scratch) : len(scratch) + len(buffers)]
        started, targets, coming = [], [], []
        for slot, (k, buffer) in enumerate(zip(far, held[len(kept) :])):
            copy = pltpu.make_async_copy(ins[k], buffer, refs[-1].at[copies + slot])
            copy.start()
            coming.append((buffer, copy))
            ins[k] = buffer
        for k, buffer in zip(kept, held):
            targets.append((buffer, out_refs[k]))
            out_refs[k] = buffer

        def flush(ref, index=None):
            target = next(out for buffer, out in targets if buffer is ref)
            if index is not None:
                ref, target = ref.at[index], target.at[index]
            copy = pltpu.make_async_copy(ref, target, refs[-1].at[len(started)])
            copy.start()
            started.append(copy)

        def fetch(ref):
            next(copy for buffer, copy in coming if buffer is ref).wait()
            return ref

        kernel(place_ref, (flush, fetch), *ins, *out_refs, *work)
        for copy in started:
            copy.wait()

    def spec(space):
        return pl.BlockSpec(memory_space=space)

    *result, token = pl.pallas_call(
        body,
        out_shape=(*[pltpu.HBM(o.shape, o.dtype) if k in kept else o for k, o in enumerate(outs)], shape((8, 128), F32)),
        in_specs=[spec(pltpu.SMEM)]
        + [spec(pl.ANY if k in far else pltpu.VMEM) for k in range(len(args))]
        + [spec(pl.ANY)] * len(after),
        out_specs=(*[spec(pltpu.HBM if k in kept else pltpu.VMEM) for k in range(len(outs))], spec(pltpu.VMEM)),
        scratch_shapes=list(scratch) + buffers + semaphores,
        compiler_params=pltpu.CompilerParams(vmem_limit_bytes=size + extra + MARGIN),
        cost_estimate=pl.CostEstimate(flops=int(micros * PACE), bytes_accessed=size, transcendentals=0),
        name=name,
    )(place, *args, *after)
    TOKENS.update((id(value), (value, token)) for value in result)
    return result


def normalize(rows):
    centered = rows - jnp.mean(rows, axis=-1, keepdims=True)
    scale = lax.rsqrt(jnp.mean(centered * centered, axis=-1, keepdims=True) + 1e-05)
    return centered * scale, scale


def norm_back(grad, scaled, scale, gain):
    weighted = grad * gain
    mean_one = jnp.mean(weighted, axis=-1, keepdims=True)
    mean_two = jnp.mean(weighted * scaled, axis=-1, keepdims=True)
    return scale * (weighted - mean_one - scaled * mean_two)


def column_sum(rows):
    return jnp.sum(rows, axis=0, keepdims=True)


def rope_tables():
    position = jnp.arange(SEQ, dtype=F32)
    frequency = 10000.0 ** (-jnp.arange(0, HEAD_DIM, 2, dtype=F32) / HEAD_DIM)
    angles = position[:, None] * frequency[None, :]
    cos, sin = jnp.cos(angles), jnp.sin(angles)
    return jnp.tile(cos, (1, 8)), jnp.tile(jnp.concatenate([-sin, sin], axis=1), (1, 4))


def swapped(rows):
    low = lax.broadcasted_iota(jnp.int32, rows.shape, 1) % HEAD_DIM < HEAD_DIM // 2
    return jnp.where(low, pltpu.roll(rows, 128 - HEAD_DIM // 2, 1), pltpu.roll(rows, HEAD_DIM // 2, 1))


def group_heads():
    for head in range(GROUP_HEADS):
        yield head, (head // 4) * 128, head % 4


def head_only(rows, lane):
    owner = lax.broadcasted_iota(jnp.int32, rows.shape, 1) // HEAD_DIM
    return jnp.where(owner == lane, rows, jnp.zeros_like(rows))


def halves(place):
    core = place[1]
    return pl.multiple_of(core * HALF, 16), pl.multiple_of((1 - core) * HALF, 16)


def first_norm_kernel(place, move, tokens, vectors, hidden):
    scaled, _ = normalize(tokens[...].astype(F32))
    hidden[...] = (scaled * vectors[0:1, :] + vectors[1:2, :]).astype(BF16)


def stack_into(out, parts):
    for source, part in enumerate(parts):
        out[source] = part[...]


def line_kernel(place, move, *refs):
    cargo = (len(refs) - 5) // 2
    stack_into(refs[4 + cargo], refs[:4])
    for source in range(cargo):
        refs[5 + cargo + source][...] = refs[4 + source][...]


def make_line(place, parts, cargo, after):
    outs = [shape((4, *parts[0].shape))] + [shape(value.shape) for value in cargo]
    return call(line_kernel, "line", outs, place, (*parts, *cargo), 0.6, after=after)


def pack_kernel(place, move, *refs):
    groups, shards, (packed, lines) = refs[:3], refs[3:7], refs[7:]
    stack_into(packed, groups)
    rows = lines.shape[0] // 8
    for source in range(8):
        side, line = source // 4, source % 4
        lines[source * rows : (source + 1) * rows, :] = shards[line][side * rows : (side + 1) * rows, :]


def pack(place, groups, shards, after):
    outs = [shape((3, *groups[0].shape)), shape((4 * shards[0].shape[0], D))]
    return call(pack_kernel, "pack", outs, place, (*groups, *shards), 1.0, after=after)


def attention_forward_kernel(groups, place, move, hidden, bias, cos, sin, *refs):
    flush, fetch = move
    count = len(groups)
    mine, other, *refs = refs
    cargo = (len(refs) - 7 * count) // 2
    if cargo:
        for source in range(cargo):
            refs[7 * count + cargo + source][...] = refs[source][...]
        refs = refs[cargo : cargo + 7 * count]
    weights, weights_out, qs, ks, vs, probs, mixed = [refs[part * count : (part + 1) * count] for part in range(7)]
    z = place[0]
    first, second = halves(place)
    rows = hidden[...]
    windows = rows.shape[0] // SEQ
    for step, which in enumerate(groups):
        weight, prob_out = weights[step], probs[step]
        group = place[2] ^ which
        for part in range(4):
            source = lax.rem(part + 4 - z, 4)
            pieces = mine[step, source], other[step, source]
            for offset, piece in zip((first, second), pieces):
                if part < 3:
                    weight[part, pl.ds(offset, HALF), :] = piece
                else:
                    weights_out[step][pl.ds(offset, HALF), :] = piece
            if part < 3:
                weight[part, GROUP:WIDE, :] = jnp.zeros((WIDE - GROUP, D), BF16)
        flush(weight)
        for part, out in ((0, qs[step]), (1, ks[step]), (2, vs[step])):
            proj = nt(rows, weight[part]) + bias[group, part : part + 1, :]
            for window in range(windows):
                span = slice(window * SEQ, (window + 1) * SEQ)
                for tile in (0, 128):
                    piece = proj[span, tile : tile + 128]
                    if part < 2:
                        piece = piece * cos[...] + swapped(piece) * sin[...]
                    out[span, tile : tile + 128] = piece.astype(BF16)
            flush(out)
        for window in range(windows):
            span = slice(window * SEQ, (window + 1) * SEQ)
            visible = lax.broadcasted_iota(jnp.int32, (SEQ, 1), 0) < place[4 + window]
            probs_of, values_of = [], []
            for head, tile, lane in group_heads():
                keys = head_only(ks[step][span, tile : tile + 128], lane)
                scores = nt(keys, qs[step][span, tile : tile + 128])
                scores = jnp.where(visible, scores, -1e30)
                top = jnp.max(scores, axis=0, keepdims=True)
                exponent = jnp.exp2((scores - top) * (SCALE * LOG2_E))
                prob = (exponent * (1.0 / column_sum(exponent))).astype(BF16)
                prob_out[window * GROUP_HEADS + head] = prob
                flush(prob_out, window * GROUP_HEADS + head)
                probs_of.append(prob)
                values_of.append(head_only(vs[step][span, tile : tile + 128], lane))
            out = tn(jnp.concatenate(probs_of[:4], axis=0), jnp.concatenate(values_of[:4], axis=0))
            mixed[step][0:128, span] = out.astype(BF16).T
            mixed[step][128:GROUP, span] = tn(probs_of[4], values_of[4]).astype(BF16).T[0 : GROUP - 128]


def attention_forward(groups, place, hidden, bias, cos, sin, mine, other, after, cargo=()):
    rows = hidden.shape[0]
    maps = rows // SEQ * GROUP_HEADS
    count = len(groups)
    kinds = [Kept((3, WIDE, D)), shape((GROUP, D))] + [Kept((rows, WIDE))] * 3
    kinds += [Kept((maps, SEQ, SEQ)), shape((GROUP, rows))]
    out = call(
        functools.partial(attention_forward_kernel, groups), "attention_forward",
        [kind for kind in kinds for _ in groups] + [shape(value.shape) for value in cargo], place,
        (hidden, bias, cos, sin, mine, other, *cargo), 4.8 * count,
        after=after, copies=count * (4 + maps),
    )
    return [out[step : 7 * count : count] for step in range(count)] + out[7 * count :]


def middle_kernel(place, move, tokens, vectors, *refs):
    flush, fetch = move
    mixed_in, weight_in, *refs = refs[:4], refs[4:8], *refs[8:]
    middle, normed, mixed, weight, stage = refs
    for which in range(GROUPS):
        offset = pl.multiple_of((place[2] ^ which) * GROUP, 32)
        stage[pl.ds(offset, GROUP), :] = mixed_in[which][...]
        weight[pl.ds(offset, GROUP), :] = weight_in[which][...]
    mixed[...] = stage[...].T
    rows = tokens[...].astype(F32) + nt(mixed[...], weight[...]) + vectors[5:6, :]
    middle[...] = rows
    scaled, _ = normalize(rows)
    normed[...] = (scaled * vectors[6:7, :] + vectors[7:8, :]).astype(BF16)


def middle_layer(place, tokens, vectors, mixed, weights, after):
    rows = tokens.shape[0]
    outs = [shape((rows, D), F32), shape((rows, D)), shape((rows, D)), shape((D, D))]
    return call(
        middle_kernel, "middle", outs, place, (tokens, vectors, *mixed, *weights), 0.2,
        [pltpu.VMEM((D, rows), BF16)], after,
    )


def store_quarter(outs, which, value):
    low = value.astype(BF16)
    if which < 3:
        outs[which][...] = low
    else:
        outs[3][...], outs[4][...] = low[: QUARTER // 2], low[QUARTER // 2 :]


def five_parts():
    return [shape((QUARTER, D))] * 3 + [shape((QUARTER // 2, D))] * 2


def quarter(parts, which, side):
    if which < 3:
        return parts[which][side * QUARTER : (side + 1) * QUARTER, :]
    rows = slice(side * 80, (side + 1) * 80)
    return jnp.concatenate([part[rows, :] for part in parts[3:]], axis=0)


def hidden_forward_kernel(quarters, place, move, *refs):
    count = 4 if 3 in quarters else 3
    parts, (bias, normed, normed_pair, back, back_pair), refs = refs[:count], refs[count : count + 5], refs[count + 5 :]
    parts = parts if count == 3 else (None, None, None, *parts)
    active, slopes, grads_down = refs[0], refs[1 : 1 + len(quarters)], refs[1 + len(quarters) :]
    grads_down = grads_down if count == 3 else (None, None, None, *grads_down)
    rows = normed.shape[0]
    for step, which in enumerate(quarters):
        up = quarter(parts, which, 0)
        column = jnp.broadcast_to(bias[which], (8, QUARTER)).T[:, 0:1]
        total = 0.0
        for part, inputs, grads in ((0, normed, back), (1, normed_pair, back_pair)):
            span = slice(part * rows, (part + 1) * rows)
            value = nt(up, inputs[...]) + column
            cdf = 0.5 + 0.5 * lax.erf(value * (0.5**0.5))
            low = (value * cdf).astype(BF16)
            active[step, :, span] = low
            slopes[step][:, span] = (cdf + value * jnp.exp(-0.5 * value * value) * 0.3989422804014327).astype(BF16)
            total = total + nn(low, grads[...])
        store_quarter(grads_down, which, total)


def hidden_forward(quarters, place, parts, bias, normed, normed_pair, back, back_pair, after):
    rows = 2 * normed.shape[0]
    count = len(quarters)
    outs = [shape((count, QUARTER, rows))] + [shape((QUARTER, rows))] * count
    outs += five_parts()[3:] if 3 in quarters else five_parts()[:3]
    active, *rest = call(
        functools.partial(hidden_forward_kernel, quarters), "hidden_forward", outs, place,
        (*parts, bias, normed, normed_pair, back, back_pair), 1.7 * count, after=after,
    )
    return active, rest[:count], rest[count:]


def hidden_backward_kernel(place, move, *refs):
    parts, slopes, (back, back_pair), refs = refs[:7], refs[7:11], refs[11:13], refs[13:]
    grad_pre, own, pair, up = refs
    rows = back.shape[0]
    for which in range(4):
        units = slice(which * QUARTER, (which + 1) * QUARTER)
        up[units, :] = quarter(parts, which, 0)
        down = quarter(parts, which, 1)
        for part, grads in ((0, back), (1, back_pair)):
            span = slice(part * rows, (part + 1) * rows)
            wide = nt(down, grads[...]) * slopes[which][:, span].astype(F32)
            grad_pre[units, span] = wide.astype(BF16)
    for out, span in ((pair, slice(rows, 2 * rows)), (own, slice(0, rows))):
        out[...] = tn(grad_pre[:, span], up[...]).astype(out.dtype)


def hidden_backward(place, parts, slopes, back, back_pair):
    rows = back.shape[0]
    outs = [shape((4 * QUARTER, 2 * rows)), shape((rows, D), F32), shape((rows, D))]
    return call(
        hidden_backward_kernel, "hidden_backward", outs, place, (*parts, *slopes, back, back_pair), 5.0,
        [pltpu.VMEM((4 * QUARTER, D), BF16)],
    )


def up_gradient_kernel(place, move, grad_pre, normed, normed_pair, *refs):
    grads, grad_bias = refs[:5], refs[5]
    for which in range(4):
        units = slice(which * QUARTER, (which + 1) * QUARTER)
        low = grad_pre[units, :]
        rows = normed.shape[0]
        store_quarter(grads, which, nn(low[:, :rows], normed[...]) + nn(low[:, rows:], normed_pair[...]))
        bias = jnp.sum(low.astype(F32), axis=1, keepdims=True)
        for source in range(4):
            grad_bias[4 * which + source] = jnp.broadcast_to(bias[source * 80 : (source + 1) * 80], (80, 8)).T


def up_gradient(place, grad_pre, normed, normed_pair, after):
    outs = five_parts() + [shape((16, 8, 80), F32)]
    *grads, bias = call(
        up_gradient_kernel, "up_gradient", outs, place, (grad_pre, normed, normed_pair), 4.0, after=after
    )
    return grads, bias


def output_kernel(place, move, most, last, middle, vectors, *refs):
    parts, (own, pair) = refs[:7], refs[7:]
    rows = own.shape[0]
    down = jnp.concatenate([quarter(parts, which, 1) for which in range(4)], axis=0)
    for out, span in ((pair, slice(rows, 2 * rows)), (own, slice(0, rows))):
        left = jnp.concatenate([most[which, :, span] for which in range(3)] + [last[0, :, span]], axis=0)
        total = tn(left, down)
        if out is own:
            total = total + middle[...] + vectors[8:9, :]
        out[...] = total.astype(out.dtype)


def output_layer(place, active, middle, vectors, parts, after):
    rows = middle.shape[0]
    outs = [shape((rows, D), F32), shape((rows, D))]
    return call(
        output_kernel, "output", outs, place, (*active, middle, vectors, *parts), 2.8, after=after
    )


def middle_backward_kernel(
    place, move, own, pair, middle, back, vectors, mixed, weight, grad_middle, sums, grad_mixed, mine, other, stage, stage_mixed
):
    grad = own[...] + pair[...].astype(F32)
    scaled, scale = normalize(middle[...])
    wide = back[...].astype(F32)
    total = wide + norm_back(grad, scaled, scale, vectors[6:7, :])
    grad_middle[...] = total
    sums[0:1, :] = column_sum(total)
    sums[1:2, :] = column_sum(grad * scaled)
    sums[2:3, :] = column_sum(grad)
    sums[3:4, :] = column_sum(wide)
    sums[4:8, :] = jnp.zeros((4, D), F32)
    low = total.astype(BF16)
    stage_mixed[...] = nt(weight[...].T, low).astype(BF16)
    stage[...] = tn(low, mixed[...]).astype(BF16)
    first, second = halves(place)
    for which in range(GROUPS):
        offset = (place[2] ^ which) * GROUP
        grad_mixed[which] = stage_mixed[pl.ds(pl.multiple_of(offset, 32), GROUP), :]
        mine[which] = stage[pl.ds(pl.multiple_of(offset + first, 16), HALF), :]
        other[which] = stage[pl.ds(pl.multiple_of(offset + second, 16), HALF), :]


def middle_backward(place, own, pair, middle, back, vectors, mixed, weight, after):
    rows = own.shape[0]
    outs = [shape((rows, D), F32), shape((8, D), F32), shape((GROUPS, GROUP, rows))]
    outs += [shape((GROUPS, HALF, D)), shape((GROUPS, HALF, D))]
    return call(
        middle_backward_kernel, "middle_backward", outs, place,
        (own, pair, middle, back, vectors, mixed, weight), 3.0,
        [pltpu.VMEM((D, D), BF16), pltpu.VMEM((D, rows), BF16)], after,
    )


def attention_backward_kernel(groups, place, move, grad_mixed, hidden, cos, sin, out_mine, out_other, *refs):
    count = len(groups)
    qs, ks, vs, probs, dqs, dks, dvs = [refs[part * count : (part + 1) * count] for part in range(7)]
    biases, (mine, other, stage) = refs[7 * count : 8 * count], refs[8 * count :]
    rows = hidden.shape[0]
    first, second = halves(place)
    for step, which in enumerate(groups):
        q, k, v, prob_in, dq_out, dk_out, dv_out = (
            qs[step], ks[step], vs[step], probs[step], dqs[step], dks[step], dvs[step]
        )
        for window in range(rows // SEQ):
            span = slice(window * SEQ, (window + 1) * SEQ)
            grad = grad_mixed[which, :, span].T
            tail = jnp.concatenate([grad[:, 128:GROUP], jnp.zeros((SEQ, WIDE - GROUP), BF16)], axis=1)
            grads = {0: grad[:, :128], 128: tail}
            lows, slopes, grads_of, queries_of, keys_of = [], [], [], [], []
            for head, tile, lane in group_heads():
                cols = slice(tile, tile + 128)
                low = prob_in[window * GROUP_HEADS + head]
                prob = low.astype(F32)
                weighted = prob * nt(head_only(v[span, cols], lane), grads[tile])
                lows.append(low)
                slopes.append((weighted - prob * column_sum(weighted)).astype(BF16))
                grads_of.append(head_only(grads[tile], lane))
                queries_of.append(head_only(q[span, cols], lane))
                keys_of.append(head_only(k[span, cols], lane))
            for tile, heads in ((0, slice(0, 4)), (128, slice(4, 5))):
                cols = slice(tile, tile + 128)
                down = jnp.concatenate(slopes[heads], axis=1)
                dv_out[span, cols] = nn(
                    jnp.concatenate(lows[heads], axis=1), jnp.concatenate(grads_of[heads], axis=0)
                ).astype(BF16)
                piece = nn(down, jnp.concatenate(queries_of[heads], axis=0)) * SCALE
                dk_out[span, cols] = (piece * cos[...] - swapped(piece) * sin[...]).astype(BF16)
                piece = tn(jnp.concatenate(slopes[heads], axis=0), jnp.concatenate(keys_of[heads], axis=0)) * SCALE
                dq_out[span, cols] = (piece * cos[...] - swapped(piece) * sin[...]).astype(BF16)
        biases[step][...] = jnp.zeros((8, WIDE), F32)
        for part, out in ((0, dq_out), (1, dk_out), (2, dv_out)):
            values = out[...]
            stage[step, part] = tn(values, hidden[...]).astype(BF16)
            mine[step, part] = stage[step, part, pl.ds(first, HALF), :]
            other[step, part] = stage[step, part, pl.ds(second, HALF), :]
            biases[step][part : part + 1, :] = column_sum(values.astype(F32))
        mine[step, 3] = out_mine[which]
        other[step, 3] = out_other[which]


def attention_backward(groups, place, grad_mixed, hidden, cos, sin, out_mine, out_other, saved, after):
    rows = hidden.shape[0]
    count = len(groups)
    outs = [shape((rows, WIDE))] * (3 * count) + [shape((8, WIDE), F32)] * count + [shape((count, 4, HALF, D))] * 2
    *out, mine, other = call(
        functools.partial(attention_backward_kernel, groups), "attention_backward", outs, place,
        (grad_mixed, hidden, cos, sin, out_mine, out_other, *[group[k] for k in range(4) for group in saved]),
        4.7 * count,
        [pltpu.VMEM((count, 3, WIDE, D), BF16)], after,
    )
    return [out[step::count] for step in range(count)], mine, other


def first_backward_kernel(place, move, tokens, grad_middle, vectors, *refs):
    parts, weights, biases, (middle_sums, units), refs = refs[:12], refs[12:16], refs[16:20], refs[20:22], refs[22:]
    input_grad, sums, unit_rows = refs
    z, plane, core = place[0], place[2], place[3]
    grad = 0.0
    for which in range(GROUPS):
        for part in range(3):
            grad = grad + nn(parts[which * 3 + part][...], weights[which][part])
    scaled, scale = normalize(tokens[...].astype(F32))
    input_grad[...] = (grad_middle[...] + norm_back(grad, scaled, scale, vectors[0:1, :])).astype(BF16)
    sums[...] = jnp.zeros((24, D), F32)
    sums[0:1, :] = column_sum(grad * scaled)
    sums[1:2, :] = column_sum(grad)
    sums[2:6, :] = middle_sums[0:4, :]
    for group in range(GROUPS):
        value = sum(jnp.where((plane ^ which) == group, biases[which][...], 0.0) for which in range(GROUPS))
        row, column = 8 + 4 * (group // 2), WIDE * (group % 2)
        sums[row : row + 4, column : column + WIDE] = value[0:4]
    unit_rows[...] = jnp.zeros((4, 8, 128), F32)
    for which in range(4):
        for source in range(4):
            row = (plane ^ which) * 2 + core
            unit_rows[z ^ source, pl.ds(row, 1), 0:80] = units[4 * which + source, 0:1, :]
    for line in range(4):
        sums[16:24, line * 128 : (line + 1) * 128] = unit_rows[line]


def first_backward(place, tokens, grad_middle, vectors, parts, weights, biases, middle_sums, units, after):
    rows = tokens.shape[0]
    outs = [shape((rows, D)), shape((24, D), F32)]
    return call(
        first_backward_kernel, "first_backward", outs, place,
        (tokens, grad_middle, vectors, *parts, *weights, *biases, middle_sums, units),
        0.2, [pltpu.VMEM((4, 8, 128), F32)], after,
    )


def unpack_vector(sums):
    group_rows = [sums[8 + 4 * (g // 2) :, WIDE * (g % 2) :][:3, :GROUP] for g in range(GROUPS)]
    units = sums[16:24, :512].reshape(8, 4, 128)[:, :, :80].transpose(1, 0, 2).reshape(4, D)
    return jnp.concatenate([sums[0:2], jnp.concatenate(group_rows, axis=1), sums[2:6], units])


def ordered_sum_kernel(which, place, move, *refs):
    total = 0.0
    for index in range(4):
        total = total + sum(jnp.where((place[which] ^ step) == index, refs[step][...], 0.0) for step in range(4))
    refs[4][...] = total


def ordered_sum(place, which, parts, after=()):
    outs = [shape(parts[0].shape, F32)]
    return call(functools.partial(ordered_sum_kernel, which), "ordered_sum", outs, place, parts, 0.6, after=after)[0]


def attention_sum_kernel(place, move, *refs):
    parts, (own, *sent), stage = refs[:4], refs[4:8], refs[8]
    stage[...] = sum(value[...].astype(F32) for value in parts[2:]) + sum(value[1].astype(F32) for value in parts[:2])
    own[...] = stage[place[0]]
    for steps, out in enumerate(sent):
        out[...] = stage[lax.rem(place[0] + steps + 1, 4)].astype(BF16)


def attention_sum(place, parts, after):
    dims = parts[2].shape
    outs = [shape(dims[1:], F32)] + [shape(dims[1:])] * 3
    return call(
        attention_sum_kernel, "attention_sum", outs, place, parts, 1.0, [pltpu.VMEM(dims, F32)], after=after
    )


def add(out, *parts):
    out[...] = sum(part.astype(F32) for part in parts).astype(out.dtype)


def keep_and_send(parts, keep, sent):
    total = sum(part[...].astype(F32) for part in parts)
    keep[...] = total[0:2]
    sent[...] = total[2:4].astype(BF16)


def merge_into(along_y, along_x, first, second, out_y, out_x):
    out_y[0:2] = along_y[0:2]
    add(out_y.at[2:4], along_y[2:4], second[...])
    add(out_x.at[0:2], along_x[0:2], first[...])
    out_x[2:4] = along_x[2:4]


def merge_kernel(place, move, along_y, along_x, *refs):
    merge_into(along_y, along_x, *refs)


def merge(place, along_y, along_x, first, second, after):
    outs = [shape(along_y.shape)] * 2
    return call(merge_kernel, "merge", outs, place, (along_y, along_x, first, second), 1.0, after=after)


def exchange_one_kernel(place, move, *refs):
    downs, (along_y, along_x, first, second), refs = refs[:3], refs[3:7], refs[7:]
    keep, sent, out_y, out_x = refs
    keep_and_send(downs, keep, sent)
    merge_into(along_y, along_x, first, second, out_y, out_x)


def exchange_one(place, downs, ups, after):
    dims = downs[0].shape
    outs = [shape((2, *dims[1:]), F32), shape((2, *dims[1:]))] + [shape(dims)] * 2
    return call(
        exchange_one_kernel, "exchange_one", outs, place,
        (*downs, *ups), 2.0, after=after,
    )


def cores_one_kernel(place, move, mine, other, half_y, half_x, rest):
    add(half_y, mine[0, 0:2], other[0, 0:2])
    add(half_x, mine[0, 2:4], other[0, 2:4])
    add(rest, mine[1], other[1])


def cores_one(place, mine, other, after):
    dims = mine.shape[1:]
    outs = [shape((2, *dims[1:]))] * 2 + [shape(dims)]
    return call(cores_one_kernel, "cores_one", outs, place, (mine, other), 1.0, after=after)


def exchange_two_kernel(place, move, *refs):
    ups, (keep_in, line_in), (keep, sent, own, line) = refs[:3], refs[3:5], refs[5:]
    keep_and_send(ups, keep, sent)
    total = keep_in[...] + line_in[...].astype(F32)
    own[...] = total[0]
    line[...] = total[1].astype(BF16)


def exchange_two(place, ups, keep, line, after):
    dims = ups[0].shape
    outs = [shape((2, *dims[1:]), F32), shape((2, *dims[1:])), shape(dims[1:], F32), shape(dims[1:])]
    return call(
        exchange_two_kernel, "exchange_two", outs, place, (*ups, keep, line), 12.0, after=after
    )


def exchange_three_kernel(
    place, move, rest, mine, other, first, second, keep, line_in, down_line, along_y, along_x, own, line
):
    add(along_x.at[0:2], rest[0:2], first[...])
    along_x[2:4] = rest[2:4]
    add(along_y.at[0:2], mine[0, 0:2], other[0, 0:2])
    add(along_y.at[2:4], mine[0, 2:4], other[0, 2:4], second[...])
    total = keep[...] + line_in[...].astype(F32)
    own[...] = total[0]
    line[0] = total[1].astype(BF16)
    line[1] = down_line[...]


def exchange_three(place, rest, mine, other, halves_in, keep, line, down_line, after):
    dims = rest.shape
    outs = [shape(dims)] * 2 + [shape(dims[1:], F32), shape((2, *dims[1:]))]
    return call(
        exchange_three_kernel, "exchange_three", outs, place, (rest, mine, other, *halves_in, keep, line, down_line), 1.0,
        after=after,
    )


def core_runs(place):
    for which in range(4):
        for source in range(4):
            run = ((place[0] ^ source) * 4 + (place[2] ^ which)) * 2 + place[3]
            yield which, source, pl.ds(pl.multiple_of(run * 80, 16), 80)


def take_runs_kernel(place, move, up, down, *outs):
    for which, source, rows in core_runs(place):
        for side, full in enumerate((up, down)):
            if which < 3:
                start = side * QUARTER + source * 80
                outs[which][start : start + 80, :] = full[rows, :]
            else:
                outs[3 + source][side * 80 : (side + 1) * 80, :] = full[rows, :]


def take_runs(place, full):
    outs = [shape((2 * QUARTER, D))] * 3 + [shape((160, D))] * 4
    return call(take_runs_kernel, "take_runs", outs, place, full, 1.0)


def place_runs_kernel(place, move, *refs):
    full = refs[5]
    full[...] = jnp.zeros_like(full)
    for which, source, rows in core_runs(place):
        part, offset = (which, source) if which < 3 else (3 + source // 2, source % 2)
        full[rows, :] = refs[part][offset * 80 : (offset + 1) * 80, :].astype(F32)


def place_runs(place, quarters):
    return call(place_runs_kernel, "place_runs", [shape((FF, D), F32)], place, quarters, 2.0)[0]


def pick(array, index):
    return lax.dynamic_index_in_dim(array, index, 0, keepdims=False)


def step_into(rate, gradient, state, outs):
    weight, first, second = state
    grad, second_new, new = outs
    grad[...] = gradient
    second_new[...], new[...] = adamw(weight[...], first[...], second[...], gradient, rate)


def finish_attention_kernel(place, move, own, one, two, three, weight, first, second, *outs):
    total = own[...]
    for value in (one, two, three):
        total = total + value[...].astype(F32)
    step_into(0.1, total, (weight, first, second), outs)


def finish_attention(place, own, line, state, after):
    out = call(
        finish_attention_kernel, "finish_attention", [shape(own.shape, F32)] * 3, place,
        (own, *line, *[value.T for value in state]), 0.3, after=after,
    )
    return [value.T for value in out]


def finish_hidden_kernel(place, move, *refs):
    owns, arrived, refs = refs[:2], refs[2], refs[3:]
    for matrix in range(2):
        state = refs[3 * matrix : 3 * matrix + 3]
        outs = refs[6 + 3 * matrix : 9 + 3 * matrix]
        step_into(0.1, owns[matrix][...] + arrived[matrix].astype(F32), state, outs)


def finish_hidden(place, owns, arrived, state, after):
    out = call(
        finish_hidden_kernel, "finish_hidden", [shape(owns[0].shape, F32)] * 6, place,
        (*owns, arrived, *[value.T for value in state]), 0.3, after=after,
    )
    return [value.T for value in out[:3]], [value.T for value in out[3:]], out[0]


def result_kernel(place, move, own, pair, out):
    out[...] = (own[...] + pair[...].astype(F32)).astype(BF16)


def result_layer(place, own, pair, after):
    return call(result_kernel, "result", [shape(pair.shape)], place, (own, pair), 12.0, after=after)[0]


def adamw(weight, first_moment, second_moment, gradient, rate_value):
    first_new = 0.9 * first_moment + 0.1 * gradient
    second_new = 0.999 * second_moment + 0.001 * gradient * gradient
    corrected = first_new / (1.0 - 0.9**STEP) / (jnp.sqrt(second_new / (1.0 - 0.999**STEP)) + 1e-08)
    return (second_new, weight - rate_value * (corrected + 0.01 * weight))


class Layout:
    def __init__(self, total):
        self.total = total
        self.block = 4 * D // total
        self.stride = total // 4
        self.me = lax.axis_index(AXES)
        self.core = lax.rem(self.me, 2)

    def swap(self, value, mask):
        return lax.ppermute(value, AXES, [(i, i ^ mask) for i in range(self.total)])

    def shift(self, value, steps):
        pairs = [(i, (i + self.stride * steps) % self.total) for i in range(self.total)]
        return lax.ppermute(value, AXES, pairs)


    def hidden_index(self):
        order = jnp.arange(16)
        z, plane = self.place[0], self.place[2]
        return ((z ^ lax.rem(order, 4)) * 4 + (plane ^ (order // 4))) * 2 + self.core


class Ring(Layout):
    def __init__(self, total):
        super().__init__(total)
        self.ring = True
        self.z = self.me // 8
        self.plane = lax.rem(self.me // 2, 4)
        self.place = (self.z, self.core, self.plane)

    def along_z(self, value):
        return [value] + [self.shift(value, -s) for s in (1, 2, 3)]

    def in_plane(self, value, each=None):
        return [value] + [self.swap(each[r].reshape(value.shape) if each else value, 2 * r) for r in (1, 2, 3)]

    def corner(self, *value):
        return [self.swap(value[0], 2), self.swap(value[1], 4)]

    def send_plane(self, along_y, along_x):
        return [self.swap(along_y, 2), self.swap(along_x, 4)]

    def all_total(self, value, after):
        value = ordered_sum(self.vector, 2, self.in_plane(value), after)
        return ordered_sum(self.vector, 0, [value] + [self.swap(value, 8 * s) for s in (1, 2, 3)])


class Whole(Layout):
    def __init__(self, total):
        super().__init__(total)
        self.ring = False
        self.plane = jnp.int32(0)
        self.place = (jnp.int32(0),) * 3

    def gather(self, attn, up, down):
        full = lax.all_gather(attn, AXES, axis=0, tiled=True).reshape(4, 4, 2, HALF, D)
        mine = [full[:, r, 0] for r in range(4)]
        other = [full[:, r, 1] for r in range(4)]
        both = [lax.all_gather(value, AXES, axis=0, tiled=True) for value in (up, down)]
        return mine, other, take_runs(self.vector, both)

    def scatter_hidden(self, grads):
        return lax.psum_scatter(place_runs(self.vector, grads), AXES, scatter_dimension=0, tiled=True)

    def scatter_attention(self, mine, other):
        full = jnp.stack([jnp.stack(mine, axis=1), jnp.stack(other, axis=1)], axis=2)
        return lax.psum_scatter(full.astype(F32).reshape(4 * D, D), AXES, scatter_dimension=0, tiled=True)


def per_device(
    total,
    tokens,
    cotangent,
    lengths,
    offsets,
    attn_weight,
    attn_first,
    attn_second,
    up_weight,
    up_first,
    up_second,
    down_weight,
    down_first,
    down_second,
    vectors,
    vec_first,
    vec_second,
):
    TOKENS.clear()
    lay = Ring(total) if total == 32 else Whole(total)
    counts = jnp.minimum(lengths - offsets, SEQ).reshape(-1)
    rows = counts.shape[0] * SEQ
    place = lay.vector = jnp.concatenate([jnp.stack([*lay.place, lay.core]).astype(jnp.int32), counts])
    cos, sin = rope_tables()

    flat = tokens.reshape(rows, D)
    back = cotangent.reshape(rows, D)
    back_pair = lay.swap(back, 1)
    (hidden,) = call(first_norm_kernel, "first_norm", [shape((rows, D))], place, (flat, vectors), 1.0)
    bias = jnp.pad(vectors[2:5].reshape(3, GROUPS, GROUP).transpose(1, 0, 2), ((0, 0), (0, 0), (0, WIDE - GROUP)))

    chosen = (lay.hidden_index()[:, None] == jnp.arange(32)[None, :]).astype(F32)
    bias_up = jnp.dot(chosen, vectors[9:].reshape(32, 80), precision=lax.Precision.HIGHEST).reshape(4, 1, QUARTER)

    if lay.ring:
        shards = jnp.concatenate([up_weight.T, down_weight.T]).astype(BF16)
        attn_parts = lay.along_z(attn_weight.T.astype(BF16))
        line, shards, corner = make_line(
            place, attn_parts, [shards, lay.swap(shards, 6)], [hidden, bias_up, bias, back_pair]
        )
        far_shard = lay.swap(shards, 16)
        groups = lay.in_plane(line)[1:]
        other = lay.swap(line, 1)
        mine = line[None]
    else:
        mine, other, hidden_parts = lay.gather(
            attn_weight.T.astype(BF16), up_weight.T.astype(BF16), down_weight.T.astype(BF16)
        )
        mine, packed = mine[0][None], jnp.stack(mine[1:])
        other, packed_other = other[0], jnp.stack(other[1:])
    forward = attention_forward(
        (0,), place, hidden, bias, cos, sin, mine, other[None], []
    )
    if lay.ring:
        corner_far = lay.swap(corner, 16)
        shards = [shards, lay.swap(shards, 8), far_shard, lay.swap(far_shard, 8)]
        packed, lines = pack(place, groups, shards, [forward[0][2]])
        hidden_parts = [lines, lay.swap(lines, 2), lay.swap(lines, 4)]
        corners = [corner, lay.swap(corner, 8), corner_far, lay.swap(corner_far, 8)]
        hidden_parts = hidden_parts + corners
        packed_other = lay.swap(packed, 1)
    after = [forward[0][2]]
    forward += attention_forward((1, 2, 3), place, hidden, bias, cos, sin, packed, packed_other, after)
    weights = [group[0] for group in forward]
    middle, normed, mixed, out_weight = middle_layer(
        place, flat, vectors, [group[6] for group in forward], [group[1] for group in forward],
        corners[1:3] if lay.ring else [],
    )
    normed_pair = lay.swap(normed, 1)
    both = (normed, normed_pair, back, back_pair)
    most, slope, grad_down = hidden_forward((0, 1, 2), place, hidden_parts[:3], bias_up, *both, [])
    rest, *last = hidden_forward((3,), place, hidden_parts[3:], bias_up, *both, [most])
    active, slope, grad_down = (most, rest), slope + last[0], grad_down + last[1]
    if lay.ring:
        grad_down = [value.reshape(-1, 80, D) for value in grad_down]
        down_corner = lay.corner(*grad_down[3:])
    grad_pre, own, pair = hidden_backward(place, hidden_parts, slope, back, back_pair)
    gradient_after, middle_after, after = [], [], []
    if lay.ring:
        down_sent = merge(place, *grad_down[1:3], *down_corner, [own])
        gradient_after = down_sent[:1]
        down_sent = middle_after = lay.send_plane(*down_sent)
    grad_up, grad_bias_up = up_gradient(place, grad_pre, normed, normed_pair, gradient_after)
    if lay.ring:
        grad_up = [value.reshape(-1, 80, D) for value in grad_up]
        up_corner = lay.corner(*grad_up[3:])
    out_own, out_pair = output_layer(place, active, middle, vectors, hidden_parts, [grad_bias_up])
    out_pair = lay.swap(out_pair, 1)
    grad_middle, sums, grad_mixed, out_mine, out_other = middle_backward(
        place, own, lay.swap(pair, 1), middle, back, vectors, mixed, out_weight, [out_own] + middle_after
    )

    def backward_of(groups, after):
        saved = [forward[r][2:6] for r in groups]
        return attention_backward(groups, place, grad_mixed, hidden, cos, sin, out_mine, out_other, saved, after)

    if lay.ring:
        keep, line, *up_sent = exchange_one(place, [grad_down[0], *down_sent], [*grad_up[1:3], *up_corner], [sums])
        down_line = lay.swap(line, 16)
        up_sent = lay.send_plane(*up_sent)
        after = [keep]
    later, mine_one, other_one = backward_of((3, 2), after)
    after = [later[0][0]]
    if lay.ring:
        other_one = lay.swap(other_one, 1)
        up_keep, up_line, down_own, down_line = exchange_two(
            place, [grad_up[0], *up_sent], keep, down_line, after
        )
        up_line = lay.swap(up_line, 16)
        *attn_corner, along_x = cores_one(place, mine_one, other_one, [up_keep])
        attn_corner = lay.corner(*attn_corner)
        after = [up_keep, along_x]
    sooner, mine_two, other_two = backward_of((1, 0), after)
    backward = [sooner[1], sooner[0], later[1], later[0]]
    other_two, after = lay.swap(other_two, 1) if lay.ring else other_two, [sooner[0][0]]
    if lay.ring:
        after += [*attn_corner, up_line]
    result = result_layer(place, out_own, out_pair, after)
    if lay.ring:
        along_y, along_x, up_own, hidden_line = exchange_three(
            place, along_x, mine_two, other_two, attn_corner, up_keep, up_line, down_line, [result]
        )
        after = [along_y]
    parts = [value for group in backward for value in group[:3]]
    input_grad, vec_sums = first_backward(
        place, flat, grad_middle, vectors, parts, weights, [group[3] for group in backward], sums, grad_bias_up, after
    )
    state = up_weight, up_first, up_second, down_weight, down_first, down_second
    if lay.ring:
        along_y, along_x = lay.send_plane(along_y, along_x)
        hidden_line = lay.swap(hidden_line, 8)
        vec_core = vec_sums + lay.swap(vec_sums, 1)
        attn_own, *attn_line = attention_sum(place, [mine_two, other_two, along_y, along_x], [hidden_line, vec_core])
        vec_sums = lay.all_total(vec_core, [attn_own])
        attn_line = [lay.shift(value, s) for value, s in zip(attn_line, (1, 2, 3))]
        (grad_up, up_second_new, up_new), (grad_down, down_second_new, down_new), done = finish_hidden(
            place, [up_own, down_own], hidden_line, state, [attn_own]
        )
        grad_attn, attn_second_new, attn_new = finish_attention(
            place, attn_own, attn_line, (attn_weight, attn_first, attn_second), [done]
        )
    else:
        grad_up, grad_down = lay.scatter_hidden(grad_up).T, lay.scatter_hidden(grad_down).T
        order = (mine_two[1], mine_two[0], mine_one[1], mine_one[0])
        order_other = (other_two[1], other_two[0], other_one[1], other_one[0])
        grad_attn = lay.scatter_attention(order, order_other).T
        attn_second_new, attn_new = adamw(attn_weight, attn_first, attn_second, grad_attn, 0.1)
        up_second_new, up_new = adamw(*state[:3], grad_up, 0.1)
        down_second_new, down_new = adamw(*state[3:], grad_down, 0.1)
        vec_sums = lax.psum(vec_sums, AXES)
    grad_vec = unpack_vector(vec_sums)
    vec_second_new, vectors_new = adamw(vectors, vec_first, vec_second, grad_vec, 0.5)
    return (
        result.reshape(tokens.shape),
        input_grad.reshape(tokens.shape),
        grad_attn,
        grad_up,
        grad_down,
        grad_vec,
        attn_second_new,
        up_second_new,
        down_second_new,
        vec_second_new,
        attn_new,
        up_new,
        down_new,
        vectors_new,
    )


def solution(mesh):
    total = mesh.shape["wide"] * mesh.shape["narrow"]
    windows = P(None, AXES, None, None)
    counts = P(None, AXES)
    columns = P(None, AXES)
    in_specs = (windows,) * 2 + (counts,) * 2 + (columns,) * 9 + (P(),) * 3
    out_specs = (windows,) * 2 + (columns,) * 3 + (P(),) + (columns,) * 3 + (P(),) + (columns,) * 3 + (P(),)
    return jax.shard_map(
        functools.partial(per_device, total),
        mesh=mesh,
        in_specs=in_specs,
        out_specs=out_specs,
        check_vma=False,
    )
```

```python
import functools
import math

import jax
import jax.numpy as jnp
from jax import lax
from jax.experimental import pallas as pl
from jax.experimental.pallas import tpu as pltpu
from jax.sharding import PartitionSpec as P

D = 640
HEADS = 20
HEAD_DIM = 32
FF = 2560
SEQ = 256
STEP = 10
AXES = ("wide", "narrow")
GROUPS = 4
GROUP_HEADS = HEADS // GROUPS
GROUP = GROUP_HEADS * HEAD_DIM
HALF = GROUP // 2
WIDE = 256
QUARTER = FF // 8
SCALE = HEAD_DIM ** (-0.5)
LOG2_E = 1.4426950408889634
BF16 = jnp.bfloat16
F32 = jnp.float32
PACE = 1.15e9
MARGIN = 8 * 1024 * 1024


def nt(left, right):
    return lax.dot_general(left, right, (((1,), (1,)), ((), ())), preferred_element_type=F32)


def nn(left, right):
    return jnp.dot(left, right, preferred_element_type=F32)


def tn(left, right):
    return lax.dot_general(left, right, (((0,), (0,)), ((), ())), preferred_element_type=F32)


def shape(dims, kind=BF16):
    return jax.ShapeDtypeStruct(dims, kind)


TOKENS = {}


class Kept:
    def __init__(self, dims, kind=BF16):
        self.struct = shape(dims, kind)


class Far:
    def __init__(self, value):
        self.value = value


def call(kernel, name, outs, place, args, micros, scratch=(), after=(), copies=None, token=True):
    after = [TOKENS[id(value)][1] if id(value) in TOKENS else value for value in after]
    kept = [place_of for place_of, out in enumerate(outs) if isinstance(out, Kept)]
    outs = [out.struct if isinstance(out, Kept) else out for out in outs]
    far = [place_of for place_of, arg in enumerate(args) if isinstance(arg, Far)]
    args = [
        pltpu.with_memory_space_constraint(arg.value, pltpu.HBM) if isinstance(arg, Far) else arg for arg in args
    ]
    buffers = [pltpu.VMEM(a.shape, a.dtype) for a in [outs[k] for k in kept] + [args[k] for k in far]]
    copies = copies or len(kept)
    size = sum(a.size * a.dtype.itemsize for a in args) + sum(o.size * o.dtype.itemsize for o in outs)
    extra = sum(math.prod(s.shape) * s.dtype.itemsize for s in scratch)
    semaphores = [pltpu.SemaphoreType.DMA((copies + len(far),))] if buffers else []

    def body(place_ref, *refs):
        ins, refs = list(refs[: len(args)]), refs[len(args) + len(after) :]
        out_refs, refs = list(refs[: len(outs)]), refs[len(outs) :]
        if token:
            refs[0][...] = jnp.zeros((8, 128), F32)
            refs = refs[1:]
        work, held = refs[: len(scratch)], refs[len(scratch) : len(scratch) + len(buffers)]
        started, targets, coming = [], [], []
        for slot, (k, buffer) in enumerate(zip(far, held[len(kept) :])):
            copy = pltpu.make_async_copy(ins[k], buffer, refs[-1].at[copies + slot])
            copy.start()
            coming.append((buffer, copy))
            ins[k] = buffer
        for k, buffer in zip(kept, held):
            targets.append((buffer, out_refs[k]))
            out_refs[k] = buffer

        def flush(ref, index=None):
            target = next(out for buffer, out in targets if buffer is ref)
            if index is not None:
                ref, target = ref.at[index], target.at[index]
            copy = pltpu.make_async_copy(ref, target, refs[-1].at[len(started)])
            copy.start()
            started.append(copy)

        def fetch(ref):
            next(copy for buffer, copy in coming if buffer is ref).wait()
            return ref

        kernel(place_ref, (flush, fetch), *ins, *out_refs, *work)
        for copy in started:
            copy.wait()

    def spec(space):
        return pl.BlockSpec(memory_space=space)

    tokens = [shape((8, 128), F32)] if token else []
    result = pl.pallas_call(
        body,
        out_shape=(*[pltpu.HBM(o.shape, o.dtype) if k in kept else o for k, o in enumerate(outs)], *tokens),
        in_specs=[spec(pltpu.SMEM)]
        + [spec(pl.ANY if k in far else pltpu.VMEM) for k in range(len(args))]
        + [spec(pl.ANY)] * len(after),
        out_specs=(
            *[spec(pltpu.HBM if k in kept else pltpu.VMEM) for k in range(len(outs))],
            *[spec(pltpu.VMEM) for _ in tokens],
        ),
        scratch_shapes=list(scratch) + buffers + semaphores,
        compiler_params=pltpu.CompilerParams(vmem_limit_bytes=size + extra + MARGIN),
        cost_estimate=pl.CostEstimate(flops=int(micros * PACE), bytes_accessed=size, transcendentals=0),
        name=name,
    )(place, *args, *after)
    result = list(result)
    if token:
        ready = result.pop()
        TOKENS.update((id(value), (value, ready)) for value in result)
    return result


def normalize(rows):
    centered = rows - jnp.mean(rows, axis=-1, keepdims=True)
    scale = lax.rsqrt(jnp.mean(centered * centered, axis=-1, keepdims=True) + 1e-05)
    return centered * scale, scale


def norm_back(grad, scaled, scale, gain):
    weighted = grad * gain
    mean_one = jnp.mean(weighted, axis=-1, keepdims=True)
    mean_two = jnp.mean(weighted * scaled, axis=-1, keepdims=True)
    return scale * (weighted - mean_one - scaled * mean_two)


def column_sum(rows):
    return jnp.sum(rows, axis=0, keepdims=True)


def rope_tables():
    position = jnp.arange(SEQ, dtype=F32)
    frequency = 10000.0 ** (-jnp.arange(0, HEAD_DIM, 2, dtype=F32) / HEAD_DIM)
    angles = position[:, None] * frequency[None, :]
    cos, sin = jnp.cos(angles), jnp.sin(angles)
    return jnp.tile(cos, (1, 8)), jnp.tile(jnp.concatenate([-sin, sin], axis=1), (1, 4))


def swapped(rows):
    low = lax.broadcasted_iota(jnp.int32, rows.shape, 1) % HEAD_DIM < HEAD_DIM // 2
    return jnp.where(low, pltpu.roll(rows, 128 - HEAD_DIM // 2, 1), pltpu.roll(rows, HEAD_DIM // 2, 1))


def group_heads():
    for head in range(GROUP_HEADS):
        yield head, (head // 4) * 128, head % 4


def head_only(rows, lane):
    owner = lax.broadcasted_iota(jnp.int32, rows.shape, 1) // HEAD_DIM
    return jnp.where(owner == lane, rows, jnp.zeros_like(rows))


def halves(place):
    core = place[1]
    return pl.multiple_of(core * HALF, 16), pl.multiple_of((1 - core) * HALF, 16)


def first_norm_kernel(place, move, tokens, vectors, hidden):
    scaled, _ = normalize(tokens[...].astype(F32))
    hidden[...] = (scaled * vectors[0:1, :] + vectors[1:2, :]).astype(BF16)


def stack_into(out, parts):
    for source, part in enumerate(parts):
        out[source] = part[...]


def hand_on_kernel(place, move, value, out):
    out[...] = value[...]


def line_kernel(place, move, *refs):
    cargo = (len(refs) - 5) // 2
    stack_into(refs[4 + cargo], refs[:4])
    for source in range(cargo):
        refs[5 + cargo + source][...] = refs[4 + source][...]


def make_line(place, parts, cargo, after):
    outs = [shape((4, *parts[0].shape))] + [shape(value.shape) for value in cargo]
    return call(line_kernel, "line", outs, place, (*parts, *cargo), 0.6, after=after, token=False)


def pack_kernel(place, move, *refs):
    groups, shards, (packed, lines) = refs[:3], refs[3:7], refs[7:]
    stack_into(packed, groups)
    rows = lines.shape[0] // 8
    for source in range(8):
        side, line = source // 4, source % 4
        lines[source * rows : (source + 1) * rows, :] = shards[line][side * rows : (side + 1) * rows, :]


def pack(place, groups, shards, after):
    outs = [shape((3, *groups[0].shape)), shape((4 * shards[0].shape[0], D))]
    return call(pack_kernel, "pack", outs, place, (*groups, *shards), 1.0, after=after, token=False)


def attention_forward_kernel(groups, place, move, hidden, bias, cos, sin, *refs):
    flush, fetch = move
    count = len(groups)
    mine, other, *refs = refs
    cargo = (len(refs) - 7 * count) // 2
    if cargo:
        for source in range(cargo):
            refs[7 * count + cargo + source][...] = refs[source][...]
        refs = refs[cargo : cargo + 7 * count]
    weights, weights_out, qs, ks, vs, probs, mixed = [refs[part * count : (part + 1) * count] for part in range(7)]
    z = place[0]
    first, second = halves(place)
    rows = hidden[...]
    windows = rows.shape[0] // SEQ
    for step, which in enumerate(groups):
        weight, prob_out = weights[step], probs[step]
        group = place[2] ^ which
        for part in range(4):
            source = lax.rem(part + 4 - z, 4)
            pieces = mine[step, source], other[step, source]
            for offset, piece in zip((first, second), pieces):
                if part < 3:
                    weight[part, pl.ds(offset, HALF), :] = piece
                else:
                    weights_out[step][pl.ds(offset, HALF), :] = piece
            if part < 3:
                weight[part, GROUP:WIDE, :] = jnp.zeros((WIDE - GROUP, D), BF16)
        flush(weight)
        for part, out in ((0, qs[step]), (1, ks[step]), (2, vs[step])):
            proj = nt(rows, weight[part]) + bias[group, part : part + 1, :]
            for window in range(windows):
                span = slice(window * SEQ, (window + 1) * SEQ)
                for tile in (0, 128):
                    piece = proj[span, tile : tile + 128]
                    if part < 2:
                        piece = piece * cos[...] + swapped(piece) * sin[...]
                    out[span, tile : tile + 128] = piece.astype(BF16)
            flush(out)
        for window in range(windows):
            span = slice(window * SEQ, (window + 1) * SEQ)
            visible = lax.broadcasted_iota(jnp.int32, (SEQ, 1), 0) < place[4 + window]
            probs_of, values_of = [], []
            for head, tile, lane in group_heads():
                keys = head_only(ks[step][span, tile : tile + 128], lane)
                scores = nt(keys, qs[step][span, tile : tile + 128])
                scores = jnp.where(visible, scores, -1e30)
                top = jnp.max(scores, axis=0, keepdims=True)
                exponent = jnp.exp2((scores - top) * (SCALE * LOG2_E))
                prob = (exponent * (1.0 / column_sum(exponent))).astype(BF16)
                prob_out[window * GROUP_HEADS + head] = prob
                flush(prob_out, window * GROUP_HEADS + head)
                probs_of.append(prob)
                values_of.append(head_only(vs[step][span, tile : tile + 128], lane))
            out = tn(jnp.concatenate(probs_of[:4], axis=0), jnp.concatenate(values_of[:4], axis=0))
            mixed[step][0:128, span] = out.astype(BF16).T
            mixed[step][128:GROUP, span] = tn(probs_of[4], values_of[4]).astype(BF16).T[0 : GROUP - 128]


def attention_forward(groups, place, hidden, bias, cos, sin, mine, other, after, cargo=()):
    rows = hidden.shape[0]
    maps = rows // SEQ * GROUP_HEADS
    count = len(groups)
    kinds = [Kept((3, WIDE, D)), shape((GROUP, D))] + [Kept((rows, WIDE))] * 3
    kinds += [Kept((maps, SEQ, SEQ)), shape((GROUP, rows))]
    out = call(
        functools.partial(attention_forward_kernel, groups), "attention_forward",
        [kind for kind in kinds for _ in groups] + [shape(value.shape) for value in cargo], place,
        (hidden, bias, cos, sin, mine, other, *cargo), 4.8 * count,
        after=after, copies=count * (4 + maps),
    )
    return [out[step : 7 * count : count] for step in range(count)] + out[7 * count :]


def middle_kernel(place, move, tokens, vectors, *refs):
    flush, fetch = move
    mixed_in, weight_in, *refs = refs[:4], refs[4:8], *refs[8:]
    middle, normed, mixed, weight, stage = refs
    for which in range(GROUPS):
        offset = pl.multiple_of((place[2] ^ which) * GROUP, 32)
        stage[pl.ds(offset, GROUP), :] = mixed_in[which][...]
        weight[pl.ds(offset, GROUP), :] = weight_in[which][...]
    mixed[...] = stage[...].T
    rows = tokens[...].astype(F32) + nt(mixed[...], weight[...]) + vectors[5:6, :]
    middle[...] = rows
    scaled, _ = normalize(rows)
    normed[...] = (scaled * vectors[6:7, :] + vectors[7:8, :]).astype(BF16)


def middle_layer(place, tokens, vectors, mixed, weights, after):
    rows = tokens.shape[0]
    outs = [shape((rows, D), F32), shape((rows, D)), shape((rows, D)), shape((D, D))]
    return call(
        middle_kernel, "middle", outs, place, (tokens, vectors, *mixed, *weights), 0.2,
        [pltpu.VMEM((D, rows), BF16)], after, token=False)


def store_quarter(outs, which, value):
    low = value.astype(BF16)
    if which < 3:
        outs[which][...] = low
    else:
        outs[3][...], outs[4][...] = low[: QUARTER // 2], low[QUARTER // 2 :]


def five_parts():
    return [shape((QUARTER, D))] * 3 + [shape((QUARTER // 2, D))] * 2


def quarter(parts, which, side):
    if which < 3:
        return parts[which][side * QUARTER : (side + 1) * QUARTER, :]
    rows = slice(side * 80, (side + 1) * 80)
    return jnp.concatenate([part[rows, :] for part in parts[3:]], axis=0)


def hidden_forward_kernel(quarters, place, move, *refs):
    count = 4 if 3 in quarters else 3
    parts, (bias, normed, normed_pair, back, back_pair), refs = refs[:count], refs[count : count + 5], refs[count + 5 :]
    parts = parts if count == 3 else (None, None, None, *parts)
    active, slopes, grads_down = refs[0], refs[1 : 1 + len(quarters)], refs[1 + len(quarters) :]
    grads_down = grads_down if count == 3 else (None, None, None, *grads_down)
    rows = normed.shape[0]
    for step, which in enumerate(quarters):
        up = quarter(parts, which, 0)
        column = jnp.broadcast_to(bias[which], (8, QUARTER)).T[:, 0:1]
        total = 0.0
        for part, inputs, grads in ((0, normed, back), (1, normed_pair, back_pair)):
            span = slice(part * rows, (part + 1) * rows)
            value = nt(up, inputs[...]) + column
            cdf = 0.5 + 0.5 * lax.erf(value * (0.5**0.5))
            low = (value * cdf).astype(BF16)
            active[step, :, span] = low
            slopes[step][:, span] = (cdf + value * jnp.exp(-0.5 * value * value) * 0.3989422804014327).astype(BF16)
            total = total + nn(low, grads[...])
        store_quarter(grads_down, which, total)


def hidden_forward(quarters, place, parts, bias, normed, normed_pair, back, back_pair, after):
    rows = 2 * normed.shape[0]
    count = len(quarters)
    outs = [shape((count, QUARTER, rows))] + [shape((QUARTER, rows))] * count
    outs += five_parts()[3:] if 3 in quarters else five_parts()[:3]
    active, *rest = call(
        functools.partial(hidden_forward_kernel, quarters), "hidden_forward", outs, place,
        (*parts, bias, normed, normed_pair, back, back_pair), 1.7 * count, after=after,
    )
    return active, rest[:count], rest[count:]


def hidden_backward_kernel(place, move, *refs):
    parts, slopes, (back, back_pair), refs = refs[:7], refs[7:11], refs[11:13], refs[13:]
    grad_pre, own, pair, up = refs
    rows = back.shape[0]
    for which in range(4):
        units = slice(which * QUARTER, (which + 1) * QUARTER)
        up[units, :] = quarter(parts, which, 0)
        down = quarter(parts, which, 1)
        for part, grads in ((0, back), (1, back_pair)):
            span = slice(part * rows, (part + 1) * rows)
            wide = nt(down, grads[...]) * slopes[which][:, span].astype(F32)
            grad_pre[units, span] = wide.astype(BF16)
    for out, span in ((pair, slice(rows, 2 * rows)), (own, slice(0, rows))):
        out[...] = tn(grad_pre[:, span], up[...]).astype(out.dtype)


def hidden_backward(place, parts, slopes, back, back_pair):
    rows = back.shape[0]
    outs = [shape((4 * QUARTER, 2 * rows)), shape((rows, D), F32), shape((rows, D))]
    return call(
        hidden_backward_kernel, "hidden_backward", outs, place, (*parts, *slopes, back, back_pair), 5.0,
        [pltpu.VMEM((4 * QUARTER, D), BF16)],
    )


def up_gradient_kernel(place, move, grad_pre, normed, normed_pair, *refs):
    grads, grad_bias = refs[:5], refs[5]
    for which in range(4):
        units = slice(which * QUARTER, (which + 1) * QUARTER)
        low = grad_pre[units, :]
        rows = normed.shape[0]
        store_quarter(grads, which, nn(low[:, :rows], normed[...]) + nn(low[:, rows:], normed_pair[...]))
        bias = jnp.sum(low.astype(F32), axis=1, keepdims=True)
        for source in range(4):
            grad_bias[4 * which + source] = jnp.broadcast_to(bias[source * 80 : (source + 1) * 80], (80, 8)).T


def up_gradient(place, grad_pre, normed, normed_pair, after):
    outs = five_parts() + [shape((16, 8, 80), F32)]
    *grads, bias = call(
        up_gradient_kernel, "up_gradient", outs, place, (grad_pre, normed, normed_pair), 4.0, after=after
    )
    return grads, bias


def output_kernel(place, move, most, last, middle, vectors, *refs):
    parts, (own, pair) = refs[:7], refs[7:]
    rows = own.shape[0]
    down = jnp.concatenate([quarter(parts, which, 1) for which in range(4)], axis=0)
    for out, span in ((pair, slice(rows, 2 * rows)), (own, slice(0, rows))):
        left = jnp.concatenate([most[which, :, span] for which in range(3)] + [last[0, :, span]], axis=0)
        total = tn(left, down)
        if out is own:
            total = total + middle[...] + vectors[8:9, :]
        out[...] = total.astype(out.dtype)


def output_layer(place, active, middle, vectors, parts, after):
    rows = middle.shape[0]
    outs = [shape((rows, D), F32), shape((rows, D))]
    return call(
        output_kernel, "output", outs, place, (*active, middle, vectors, *parts), 2.8, after=after
    )


def middle_backward_kernel(
    place, move, own, pair, middle, back, vectors, mixed, weight, grad_middle, sums, grad_mixed, mine, other, stage, stage_mixed
):
    grad = own[...] + pair[...].astype(F32)
    scaled, scale = normalize(middle[...])
    wide = back[...].astype(F32)
    total = wide + norm_back(grad, scaled, scale, vectors[6:7, :])
    grad_middle[...] = total
    sums[0:1, :] = column_sum(total)
    sums[1:2, :] = column_sum(grad * scaled)
    sums[2:3, :] = column_sum(grad)
    sums[3:4, :] = column_sum(wide)
    sums[4:8, :] = jnp.zeros((4, D), F32)
    low = total.astype(BF16)
    stage_mixed[...] = nt(weight[...].T, low).astype(BF16)
    stage[...] = tn(low, mixed[...]).astype(BF16)
    first, second = halves(place)
    for which in range(GROUPS):
        offset = (place[2] ^ which) * GROUP
        grad_mixed[which] = stage_mixed[pl.ds(pl.multiple_of(offset, 32), GROUP), :]
        mine[which] = stage[pl.ds(pl.multiple_of(offset + first, 16), HALF), :]
        other[which] = stage[pl.ds(pl.multiple_of(offset + second, 16), HALF), :]


def middle_backward(place, own, pair, middle, back, vectors, mixed, weight, after):
    rows = own.shape[0]
    outs = [shape((rows, D), F32), shape((8, D), F32), shape((GROUPS, GROUP, rows))]
    outs += [shape((GROUPS, HALF, D)), shape((GROUPS, HALF, D))]
    return call(
        middle_backward_kernel, "middle_backward", outs, place,
        (own, pair, middle, back, vectors, mixed, weight), 3.0,
        [pltpu.VMEM((D, D), BF16), pltpu.VMEM((D, rows), BF16)], after,
    )


def attention_backward_kernel(groups, place, move, grad_mixed, hidden, cos, sin, out_mine, out_other, *refs):
    count = len(groups)
    qs, ks, vs, probs, dqs, dks, dvs = [refs[part * count : (part + 1) * count] for part in range(7)]
    biases, (mine, other, stage) = refs[7 * count : 8 * count], refs[8 * count :]
    rows = hidden.shape[0]
    first, second = halves(place)
    for step, which in enumerate(groups):
        q, k, v, prob_in, dq_out, dk_out, dv_out = (
            qs[step], ks[step], vs[step], probs[step], dqs[step], dks[step], dvs[step]
        )
        for window in range(rows // SEQ):
            span = slice(window * SEQ, (window + 1) * SEQ)
            grad = grad_mixed[which, :, span].T
            tail = jnp.concatenate([grad[:, 128:GROUP], jnp.zeros((SEQ, WIDE - GROUP), BF16)], axis=1)
            grads = {0: grad[:, :128], 128: tail}
            lows, slopes, grads_of, queries_of, keys_of = [], [], [], [], []
            for head, tile, lane in group_heads():
                cols = slice(tile, tile + 128)
                low = prob_in[window * GROUP_HEADS + head]
                prob = low.astype(F32)
                weighted = prob * nt(head_only(v[span, cols], lane), grads[tile])
                lows.append(low)
                slopes.append((weighted - prob * column_sum(weighted)).astype(BF16))
                grads_of.append(head_only(grads[tile], lane))
                queries_of.append(head_only(q[span, cols], lane))
                keys_of.append(head_only(k[span, cols], lane))
            for tile, heads in ((0, slice(0, 4)), (128, slice(4, 5))):
                cols = slice(tile, tile + 128)
                down = jnp.concatenate(slopes[heads], axis=1)
                dv_out[span, cols] = nn(
                    jnp.concatenate(lows[heads], axis=1), jnp.concatenate(grads_of[heads], axis=0)
                ).astype(BF16)
                piece = nn(down, jnp.concatenate(queries_of[heads], axis=0)) * SCALE
                dk_out[span, cols] = (piece * cos[...] - swapped(piece) * sin[...]).astype(BF16)
                piece = tn(jnp.concatenate(slopes[heads], axis=0), jnp.concatenate(keys_of[heads], axis=0)) * SCALE
                dq_out[span, cols] = (piece * cos[...] - swapped(piece) * sin[...]).astype(BF16)
        biases[step][...] = jnp.zeros((8, WIDE), F32)
        for part, out in ((0, dq_out), (1, dk_out), (2, dv_out)):
            values = out[...]
            stage[step, part] = tn(values, hidden[...]).astype(BF16)
            mine[step, part] = stage[step, part, pl.ds(first, HALF), :]
            other[step, part] = stage[step, part, pl.ds(second, HALF), :]
            biases[step][part : part + 1, :] = column_sum(values.astype(F32))
        mine[step, 3] = out_mine[which]
        other[step, 3] = out_other[which]


def attention_backward(groups, place, grad_mixed, hidden, cos, sin, out_mine, out_other, saved, after):
    rows = hidden.shape[0]
    count = len(groups)
    outs = [shape((rows, WIDE))] * (3 * count) + [shape((8, WIDE), F32)] * count + [shape((count, 4, HALF, D))] * 2
    *out, mine, other = call(
        functools.partial(attention_backward_kernel, groups), "attention_backward", outs, place,
        (grad_mixed, hidden, cos, sin, out_mine, out_other, *[group[k] for k in range(4) for group in saved]),
        4.7 * count,
        [pltpu.VMEM((count, 3, WIDE, D), BF16)], after,
    )
    return [out[step::count] for step in range(count)], mine, other


def first_backward_kernel(place, move, tokens, grad_middle, vectors, *refs):
    parts, weights, biases, (middle_sums, units), refs = refs[:12], refs[12:16], refs[16:20], refs[20:22], refs[22:]
    input_grad, sums, unit_rows = refs
    z, plane, core = place[0], place[2], place[3]
    grad = 0.0
    for which in range(GROUPS):
        for part in range(3):
            grad = grad + nn(parts[which * 3 + part][...], weights[which][part])
    scaled, scale = normalize(tokens[...].astype(F32))
    input_grad[...] = (grad_middle[...] + norm_back(grad, scaled, scale, vectors[0:1, :])).astype(BF16)
    sums[...] = jnp.zeros((24, D), F32)
    sums[0:1, :] = column_sum(grad * scaled)
    sums[1:2, :] = column_sum(grad)
    sums[2:6, :] = middle_sums[0:4, :]
    for group in range(GROUPS):
        value = sum(jnp.where((plane ^ which) == group, biases[which][...], 0.0) for which in range(GROUPS))
        row, column = 8 + 4 * (group // 2), WIDE * (group % 2)
        sums[row : row + 4, column : column + WIDE] = value[0:4]
    unit_rows[...] = jnp.zeros((4, 8, 128), F32)
    for which in range(4):
        for source in range(4):
            row = (plane ^ which) * 2 + core
            unit_rows[z ^ source, pl.ds(row, 1), 0:80] = units[4 * which + source, 0:1, :]
    for line in range(4):
        sums[16:24, line * 128 : (line + 1) * 128] = unit_rows[line]


def first_backward(place, tokens, grad_middle, vectors, parts, weights, biases, middle_sums, units, after):
    rows = tokens.shape[0]
    outs = [shape((rows, D)), shape((24, D), F32)]
    return call(
        first_backward_kernel, "first_backward", outs, place,
        (tokens, grad_middle, vectors, *parts, *weights, *biases, middle_sums, units),
        0.2, [pltpu.VMEM((4, 8, 128), F32)], after, token=False)


def unpack_vector(sums):
    group_rows = [sums[8 + 4 * (g // 2) :, WIDE * (g % 2) :][:3, :GROUP] for g in range(GROUPS)]
    units = sums[16:24, :512].reshape(8, 4, 128)[:, :, :80].transpose(1, 0, 2).reshape(4, D)
    return jnp.concatenate([sums[0:2], jnp.concatenate(group_rows, axis=1), sums[2:6], units])


def ordered_sum_kernel(which, place, move, *refs):
    total = 0.0
    for index in range(4):
        total = total + sum(jnp.where((place[which] ^ step) == index, refs[step][...], 0.0) for step in range(4))
    refs[4][...] = total


def ordered_sum(place, which, parts, after=()):
    outs = [shape(parts[0].shape, F32)]
    return call(functools.partial(ordered_sum_kernel, which), "ordered_sum", outs, place, parts, 0.6, after=after, token=False)[0]


def attention_sum_kernel(place, move, *refs):
    parts, (own, *sent), stage = refs[:4], refs[4:8], refs[8]
    stage[...] = sum(value[...].astype(F32) for value in parts[2:]) + sum(value[1].astype(F32) for value in parts[:2])
    own[...] = stage[place[0]]
    for steps, out in enumerate(sent):
        out[...] = stage[lax.rem(place[0] + steps + 1, 4)].astype(BF16)


def attention_sum(place, parts, after):
    dims = parts[2].shape
    outs = [shape(dims[1:], F32)] + [shape(dims[1:])] * 3
    return call(
        attention_sum_kernel, "attention_sum", outs, place, parts, 1.0, [pltpu.VMEM(dims, F32)], after=after
    )


def add(out, *parts):
    out[...] = sum(part.astype(F32) for part in parts).astype(out.dtype)


def keep_and_send(parts, keep, sent):
    total = sum(part[...].astype(F32) for part in parts)
    keep[...] = total[0:2]
    sent[...] = total[2:4].astype(BF16)


def merge_into(along_y, along_x, first, second, out_y, out_x):
    out_y[0:2] = along_y[0:2]
    add(out_y.at[2:4], along_y[2:4], second[...])
    add(out_x.at[0:2], along_x[0:2], first[...])
    out_x[2:4] = along_x[2:4]


def merge_kernel(place, move, along_y, along_x, *refs):
    merge_into(along_y, along_x, *refs)


def merge(place, along_y, along_x, first, second, after):
    outs = [shape(along_y.shape)] * 2
    return call(merge_kernel, "merge", outs, place, (along_y, along_x, first, second), 1.0, after=after)


def exchange_one_kernel(place, move, *refs):
    downs, (along_y, along_x, first, second), refs = refs[:3], refs[3:7], refs[7:]
    keep, sent, out_y, out_x = refs
    keep_and_send(downs, keep, sent)
    merge_into(along_y, along_x, first, second, out_y, out_x)


def exchange_one(place, downs, ups, after):
    dims = downs[0].shape
    outs = [shape((2, *dims[1:]), F32), shape((2, *dims[1:]))] + [shape(dims)] * 2
    return call(
        exchange_one_kernel, "exchange_one", outs, place,
        (*downs, *ups), 2.0, after=after,
    )


def cores_one_kernel(place, move, mine, other, half_y, half_x, rest):
    add(half_y, mine[0, 0:2], other[0, 0:2])
    add(half_x, mine[0, 2:4], other[0, 2:4])
    add(rest, mine[1], other[1])


def cores_one(place, mine, other, after):
    dims = mine.shape[1:]
    outs = [shape((2, *dims[1:]))] * 2 + [shape(dims)]
    return call(cores_one_kernel, "cores_one", outs, place, (mine, other), 1.0, after=after)


def exchange_two_kernel(place, move, *refs):
    ups, (keep_in, line_in), (keep, sent, own, line) = refs[:3], refs[3:5], refs[5:]
    keep_and_send(ups, keep, sent)
    total = keep_in[...] + line_in[...].astype(F32)
    own[...] = total[0]
    line[...] = total[1].astype(BF16)


def exchange_two(place, ups, keep, line, after):
    dims = ups[0].shape
    outs = [shape((2, *dims[1:]), F32), shape((2, *dims[1:])), shape(dims[1:], F32), shape(dims[1:])]
    return call(
        exchange_two_kernel, "exchange_two", outs, place, (*ups, keep, line), 12.0, after=after
    )


def exchange_three_kernel(
    place, move, rest, mine, other, first, second, keep, line_in, down_line, along_y, along_x, own, line
):
    add(along_x.at[0:2], rest[0:2], first[...])
    along_x[2:4] = rest[2:4]
    add(along_y.at[0:2], mine[0, 0:2], other[0, 0:2])
    add(along_y.at[2:4], mine[0, 2:4], other[0, 2:4], second[...])
    total = keep[...] + line_in[...].astype(F32)
    own[...] = total[0]
    line[0] = total[1].astype(BF16)
    line[1] = down_line[...]


def exchange_three(place, rest, mine, other, halves_in, keep, line, down_line, after):
    dims = rest.shape
    outs = [shape(dims)] * 2 + [shape(dims[1:], F32), shape((2, *dims[1:]))]
    return call(
        exchange_three_kernel, "exchange_three", outs, place, (rest, mine, other, *halves_in, keep, line, down_line), 1.0,
        after=after,
    )


def core_runs(place):
    for which in range(4):
        for source in range(4):
            run = ((place[0] ^ source) * 4 + (place[2] ^ which)) * 2 + place[3]
            yield which, source, pl.ds(pl.multiple_of(run * 80, 16), 80)


def take_runs_kernel(place, move, up, down, *outs):
    for which, source, rows in core_runs(place):
        for side, full in enumerate((up, down)):
            if which < 3:
                start = side * QUARTER + source * 80
                outs[which][start : start + 80, :] = full[rows, :]
            else:
                outs[3 + source][side * 80 : (side + 1) * 80, :] = full[rows, :]


def take_runs(place, full):
    outs = [shape((2 * QUARTER, D))] * 3 + [shape((160, D))] * 4
    return call(take_runs_kernel, "take_runs", outs, place, full, 1.0, token=False)


def place_runs_kernel(place, move, *refs):
    full = refs[5]
    full[...] = jnp.zeros_like(full)
    for which, source, rows in core_runs(place):
        part, offset = (which, source) if which < 3 else (3 + source // 2, source % 2)
        full[rows, :] = refs[part][offset * 80 : (offset + 1) * 80, :].astype(F32)


def place_runs(place, quarters):
    return call(place_runs_kernel, "place_runs", [shape((FF, D), F32)], place, quarters, 2.0, token=False)[0]


def pick(array, index):
    return lax.dynamic_index_in_dim(array, index, 0, keepdims=False)


def step_into(rate, gradient, state, outs):
    weight, first, second = state
    grad, second_new, new = outs
    grad[...] = gradient
    second_new[...], new[...] = adamw(weight[...], first[...], second[...], gradient, rate)


def finish_attention_kernel(place, move, own, one, two, three, weight, first, second, *outs):
    total = own[...]
    for value in (one, two, three):
        total = total + value[...].astype(F32)
    step_into(0.1, total, (weight, first, second), outs)


def finish_attention(place, own, line, state, after):
    out = call(
        finish_attention_kernel, "finish_attention", [shape(own.shape, F32)] * 3, place,
        (own, *line, *[value.T for value in state]), 0.3, after=after, token=False)
    return [value.T for value in out]


def finish_hidden_kernel(place, move, *refs):
    owns, arrived, refs = refs[:2], refs[2], refs[3:]
    for matrix in range(2):
        state = refs[3 * matrix : 3 * matrix + 3]
        outs = refs[6 + 3 * matrix : 9 + 3 * matrix]
        step_into(0.1, owns[matrix][...] + arrived[matrix].astype(F32), state, outs)


def finish_hidden(place, owns, arrived, state, after):
    out = call(
        finish_hidden_kernel, "finish_hidden", [shape(owns[0].shape, F32)] * 6, place,
        (*owns, arrived, *[value.T for value in state]), 0.3, after=after,
    )
    return [value.T for value in out[:3]], [value.T for value in out[3:]], out[0]


def result_kernel(place, move, own, pair, out):
    out[...] = (own[...] + pair[...].astype(F32)).astype(BF16)


def result_layer(place, own, pair, after):
    return call(result_kernel, "result", [shape(pair.shape)], place, (own, pair), 12.0, after=after)[0]


def adamw(weight, first_moment, second_moment, gradient, rate_value):
    first_new = 0.9 * first_moment + 0.1 * gradient
    second_new = 0.999 * second_moment + 0.001 * gradient * gradient
    corrected = first_new / (1.0 - 0.9**STEP) / (jnp.sqrt(second_new / (1.0 - 0.999**STEP)) + 1e-08)
    return (second_new, weight - rate_value * (corrected + 0.01 * weight))


class Layout:
    def __init__(self, total):
        self.total = total
        self.block = 4 * D // total
        self.stride = total // 4
        self.me = lax.axis_index(AXES)
        self.core = lax.rem(self.me, 2)

    def swap(self, value, mask):
        return lax.ppermute(value, AXES, [(i, i ^ mask) for i in range(self.total)])

    def shift(self, value, steps):
        pairs = [(i, (i + self.stride * steps) % self.total) for i in range(self.total)]
        return lax.ppermute(value, AXES, pairs)


    def hidden_index(self):
        order = jnp.arange(16)
        z, plane = self.place[0], self.place[2]
        return ((z ^ lax.rem(order, 4)) * 4 + (plane ^ (order // 4))) * 2 + self.core


class Ring(Layout):
    def __init__(self, total):
        super().__init__(total)
        self.ring = True
        self.z = self.me // 8
        self.plane = lax.rem(self.me // 2, 4)
        self.place = (self.z, self.core, self.plane)

    def along_z(self, value):
        return [value] + [self.shift(value, -s) for s in (1, 2, 3)]

    def in_plane(self, value, each=None):
        return [value] + [self.swap(each[r].reshape(value.shape) if each else value, 2 * r) for r in (1, 2, 3)]

    def corner(self, *value):
        return [self.swap(value[0], 2), self.swap(value[1], 4)]

    def send_plane(self, along_y, along_x):
        return [self.swap(along_y, 2), self.swap(along_x, 4)]

    def all_total(self, value, after):
        value = ordered_sum(self.vector, 2, self.in_plane(value), after)
        return ordered_sum(self.vector, 0, [value] + [self.swap(value, 8 * s) for s in (1, 2, 3)])


class Whole(Layout):
    def __init__(self, total):
        super().__init__(total)
        self.ring = False
        self.plane = jnp.int32(0)
        self.place = (jnp.int32(0),) * 3

    def gather(self, attn, up, down):
        full = lax.all_gather(attn, AXES, axis=0, tiled=True).reshape(4, 4, 2, HALF, D)
        mine = [full[:, r, 0] for r in range(4)]
        other = [full[:, r, 1] for r in range(4)]
        both = [lax.all_gather(value, AXES, axis=0, tiled=True) for value in (up, down)]
        return mine, other, take_runs(self.vector, both)

    def scatter_hidden(self, grads):
        return lax.psum_scatter(place_runs(self.vector, grads), AXES, scatter_dimension=0, tiled=True)

    def scatter_attention(self, mine, other):
        full = jnp.stack([jnp.stack(mine, axis=1), jnp.stack(other, axis=1)], axis=2)
        return lax.psum_scatter(full.astype(F32).reshape(4 * D, D), AXES, scatter_dimension=0, tiled=True)


def per_device(
    total,
    tokens,
    cotangent,
    lengths,
    offsets,
    attn_weight,
    attn_first,
    attn_second,
    up_weight,
    up_first,
    up_second,
    down_weight,
    down_first,
    down_second,
    vectors,
    vec_first,
    vec_second,
):
    TOKENS.clear()
    lay = Ring(total) if total == 32 else Whole(total)
    counts = jnp.minimum(lengths - offsets, SEQ).reshape(-1)
    rows = counts.shape[0] * SEQ
    place = lay.vector = jnp.concatenate([jnp.stack([*lay.place, lay.core]).astype(jnp.int32), counts])
    cos, sin = rope_tables()

    flat = tokens.reshape(rows, D)
    back = cotangent.reshape(rows, D)
    back_pair = lay.swap(back, 1)
    (hidden,) = call(first_norm_kernel, "first_norm", [shape((rows, D))], place, (flat, vectors), 1.0)
    bias = jnp.pad(vectors[2:5].reshape(3, GROUPS, GROUP).transpose(1, 0, 2), ((0, 0), (0, 0), (0, WIDE - GROUP)))

    chosen = (lay.hidden_index()[:, None] == jnp.arange(32)[None, :]).astype(F32)
    bias_up = jnp.dot(chosen, vectors[9:].reshape(32, 80), precision=lax.Precision.HIGHEST).reshape(4, 1, QUARTER)

    if lay.ring:
        shards = jnp.concatenate([up_weight.T, down_weight.T]).astype(BF16)
        attn_parts = lay.along_z(attn_weight.T.astype(BF16))
        line, shards, corner = make_line(
            place, attn_parts, [shards, lay.swap(shards, 6)], [hidden, bias_up, bias, back_pair]
        )
        far_shard = lay.swap(shards, 16)
        groups = lay.in_plane(line)[1:]
        other = lay.swap(line, 1)
        mine = line[None]
    else:
        mine, other, hidden_parts = lay.gather(
            attn_weight.T.astype(BF16), up_weight.T.astype(BF16), down_weight.T.astype(BF16)
        )
        mine, packed = mine[0][None], jnp.stack(mine[1:])
        other, packed_other = other[0], jnp.stack(other[1:])
    forward = attention_forward(
        (0,), place, hidden, bias, cos, sin, mine, other[None], []
    )
    if lay.ring:
        shards = [shards, lay.swap(shards, 8), far_shard, lay.swap(far_shard, 8)]
        packed, lines = pack(place, groups, shards, [forward[0][2]])
        hidden_parts = [lines, lay.swap(lines, 2), lay.swap(lines, 4)]
        packed_other = lay.swap(packed, 1)
        (corner,) = call(
            hand_on_kernel, "hand_on", [shape(corner.shape)], place, (corner,), 0.4, after=[packed_other], token=False
        )
        corner_far = lay.swap(corner, 16)
        corners = [corner, lay.swap(corner, 8), corner_far, lay.swap(corner_far, 8)]
        hidden_parts = hidden_parts + corners
    after = [forward[0][2]]
    forward += attention_forward((1, 2, 3), place, hidden, bias, cos, sin, packed, packed_other, after)
    weights = [group[0] for group in forward]
    middle, normed, mixed, out_weight = middle_layer(
        place, flat, vectors, [group[6] for group in forward], [group[1] for group in forward],
        corners[1:3] if lay.ring else [],
    )
    normed_pair = lay.swap(normed, 1)
    both = (normed, normed_pair, back, back_pair)
    most, slope, grad_down = hidden_forward((0, 1, 2), place, hidden_parts[:3], bias_up, *both, [])
    rest, *last = hidden_forward((3,), place, hidden_parts[3:], bias_up, *both, [most])
    active, slope, grad_down = (most, rest), slope + last[0], grad_down + last[1]
    if lay.ring:
        grad_down = [value.reshape(-1, 80, D) for value in grad_down]
        down_corner = lay.corner(*grad_down[3:])
    grad_pre, own, pair = hidden_backward(place, hidden_parts, slope, back, back_pair)
    gradient_after, middle_after, after = [], [], []
    if lay.ring:
        down_sent = merge(place, *grad_down[1:3], *down_corner, [own])
        gradient_after = down_sent[:1]
        down_sent = middle_after = lay.send_plane(*down_sent)
    grad_up, grad_bias_up = up_gradient(place, grad_pre, normed, normed_pair, gradient_after)
    if lay.ring:
        grad_up = [value.reshape(-1, 80, D) for value in grad_up]
        up_corner = lay.corner(*grad_up[3:])
    out_own, out_pair = output_layer(place, active, middle, vectors, hidden_parts, [grad_bias_up])
    out_pair = lay.swap(out_pair, 1)
    grad_middle, sums, grad_mixed, out_mine, out_other = middle_backward(
        place, own, lay.swap(pair, 1), middle, back, vectors, mixed, out_weight, [out_own] + middle_after
    )

    def backward_of(groups, after):
        saved = [forward[r][2:6] for r in groups]
        return attention_backward(groups, place, grad_mixed, hidden, cos, sin, out_mine, out_other, saved, after)

    if lay.ring:
        keep, line, *up_sent = exchange_one(place, [grad_down[0], *down_sent], [*grad_up[1:3], *up_corner], [sums])
        down_line = lay.swap(line, 16)
        up_sent = lay.send_plane(*up_sent)
        after = [keep]
    later, mine_one, other_one = backward_of((3, 2), after)
    after = [later[0][0]]
    if lay.ring:
        other_one = lay.swap(other_one, 1)
        up_keep, up_line, down_own, down_line = exchange_two(
            place, [grad_up[0], *up_sent], keep, down_line, after
        )
        up_line = lay.swap(up_line, 16)
        *attn_corner, along_x = cores_one(place, mine_one, other_one, [up_keep])
        attn_corner = lay.corner(*attn_corner)
        after = [up_keep, along_x]
    sooner, mine_two, other_two = backward_of((1, 0), after)
    backward = [sooner[1], sooner[0], later[1], later[0]]
    other_two, after = lay.swap(other_two, 1) if lay.ring else other_two, [sooner[0][0]]
    if lay.ring:
        after += [*attn_corner, up_line]
    result = result_layer(place, out_own, out_pair, after)
    if lay.ring:
        along_y, along_x, up_own, hidden_line = exchange_three(
            place, along_x, mine_two, other_two, attn_corner, up_keep, up_line, down_line, [result]
        )
        after = [along_y]
    parts = [value for group in backward for value in group[:3]]
    input_grad, vec_sums = first_backward(
        place, flat, grad_middle, vectors, parts, weights, [group[3] for group in backward], sums, grad_bias_up, after
    )
    state = up_weight, up_first, up_second, down_weight, down_first, down_second
    if lay.ring:
        along_y, along_x = lay.send_plane(along_y, along_x)
        hidden_line = lay.swap(hidden_line, 8)
        vec_core = vec_sums + lay.swap(vec_sums, 1)
        attn_own, *attn_line = attention_sum(place, [mine_two, other_two, along_y, along_x], [hidden_line, vec_core])
        vec_sums = lay.all_total(vec_core, [attn_own])
        attn_line = [lay.shift(value, s) for value, s in zip(attn_line, (1, 2, 3))]
        (grad_up, up_second_new, up_new), (grad_down, down_second_new, down_new), done = finish_hidden(
            place, [up_own, down_own], hidden_line, state, [attn_own]
        )
        grad_attn, attn_second_new, attn_new = finish_attention(
            place, attn_own, attn_line, (attn_weight, attn_first, attn_second), [done]
        )
    else:
        grad_up, grad_down = lay.scatter_hidden(grad_up).T, lay.scatter_hidden(grad_down).T
        order = (mine_two[1], mine_two[0], mine_one[1], mine_one[0])
        order_other = (other_two[1], other_two[0], other_one[1], other_one[0])
        grad_attn = lay.scatter_attention(order, order_other).T
        attn_second_new, attn_new = adamw(attn_weight, attn_first, attn_second, grad_attn, 0.1)
        up_second_new, up_new = adamw(*state[:3], grad_up, 0.1)
        down_second_new, down_new = adamw(*state[3:], grad_down, 0.1)
        vec_sums = lax.psum(vec_sums, AXES)
    grad_vec = unpack_vector(vec_sums)
    vec_second_new, vectors_new = adamw(vectors, vec_first, vec_second, grad_vec, 0.5)
    return (
        result.reshape(tokens.shape),
        input_grad.reshape(tokens.shape),
        grad_attn,
        grad_up,
        grad_down,
        grad_vec,
        attn_second_new,
        up_second_new,
        down_second_new,
        vec_second_new,
        attn_new,
        up_new,
        down_new,
        vectors_new,
    )


def solution(mesh):
    total = mesh.shape["wide"] * mesh.shape["narrow"]
    windows = P(None, AXES, None, None)
    counts = P(None, AXES)
    columns = P(None, AXES)
    in_specs = (windows,) * 2 + (counts,) * 2 + (columns,) * 9 + (P(),) * 3
    out_specs = (windows,) * 2 + (columns,) * 3 + (P(),) + (columns,) * 3 + (P(),) + (columns,) * 3 + (P(),)
    return jax.shard_map(
        functools.partial(per_device, total),
        mesh=mesh,
        in_specs=in_specs,
        out_specs=out_specs,
        check_vma=False,
    )
```

```python
import functools
import math

import jax
import jax.numpy as jnp
from jax import lax
from jax.experimental import pallas as pl
from jax.experimental.pallas import tpu as pltpu
from jax.sharding import PartitionSpec as P

D = 640
HEADS = 20
HEAD_DIM = 32
FF = 2560
SEQ = 256
STEP = 10
AXES = ("wide", "narrow")
GROUPS = 4
GROUP_HEADS = HEADS // GROUPS
GROUP = GROUP_HEADS * HEAD_DIM
HALF = GROUP // 2
WIDE = 256
QUARTER = FF // 8
SCALE = HEAD_DIM ** (-0.5)
LOG2_E = 1.4426950408889634
BF16 = jnp.bfloat16
F32 = jnp.float32
PACE = 1.15e9
MARGIN = 8 * 1024 * 1024


def nt(left, right):
    return lax.dot_general(left, right, (((1,), (1,)), ((), ())), preferred_element_type=F32)


def nn(left, right):
    return jnp.dot(left, right, preferred_element_type=F32)


def tn(left, right):
    return lax.dot_general(left, right, (((0,), (0,)), ((), ())), preferred_element_type=F32)


def shape(dims, kind=BF16):
    return jax.ShapeDtypeStruct(dims, kind)


TOKENS = {}


class Kept:
    def __init__(self, dims, kind=BF16):
        self.struct = shape(dims, kind)


class Far:
    def __init__(self, value):
        self.value = value


def call(kernel, name, outs, place, args, micros, scratch=(), after=(), copies=None, token=True):
    after = [TOKENS[id(value)][1] if id(value) in TOKENS else value for value in after]
    kept = [place_of for place_of, out in enumerate(outs) if isinstance(out, Kept)]
    outs = [out.struct if isinstance(out, Kept) else out for out in outs]
    far = [place_of for place_of, arg in enumerate(args) if isinstance(arg, Far)]
    args = [
        pltpu.with_memory_space_constraint(arg.value, pltpu.HBM) if isinstance(arg, Far) else arg for arg in args
    ]
    buffers = [pltpu.VMEM(a.shape, a.dtype) for a in [outs[k] for k in kept] + [args[k] for k in far]]
    copies = copies or len(kept)
    size = sum(a.size * a.dtype.itemsize for a in args) + sum(o.size * o.dtype.itemsize for o in outs)
    extra = sum(math.prod(s.shape) * s.dtype.itemsize for s in scratch)
    semaphores = [pltpu.SemaphoreType.DMA((copies + len(far),))] if buffers else []

    def body(place_ref, *refs):
        ins, refs = list(refs[: len(args)]), refs[len(args) + len(after) :]
        out_refs, refs = list(refs[: len(outs)]), refs[len(outs) :]
        if token:
            refs[0][...] = jnp.zeros((8, 128), F32)
            refs = refs[1:]
        work, held = refs[: len(scratch)], refs[len(scratch) : len(scratch) + len(buffers)]
        started, targets, coming = [], [], []
        for slot, (k, buffer) in enumerate(zip(far, held[len(kept) :])):
            copy = pltpu.make_async_copy(ins[k], buffer, refs[-1].at[copies + slot])
            copy.start()
            coming.append((buffer, copy))
            ins[k] = buffer
        for k, buffer in zip(kept, held):
            targets.append((buffer, out_refs[k]))
            out_refs[k] = buffer

        def flush(ref, index=None):
            target = next(out for buffer, out in targets if buffer is ref)
            if index is not None:
                ref, target = ref.at[index], target.at[index]
            copy = pltpu.make_async_copy(ref, target, refs[-1].at[len(started)])
            copy.start()
            started.append(copy)

        def fetch(ref):
            next(copy for buffer, copy in coming if buffer is ref).wait()
            return ref

        kernel(place_ref, (flush, fetch), *ins, *out_refs, *work)
        for copy in started:
            copy.wait()

    def spec(space):
        return pl.BlockSpec(memory_space=space)

    tokens = [shape((8, 128), F32)] if token else []
    result = pl.pallas_call(
        body,
        out_shape=(*[pltpu.HBM(o.shape, o.dtype) if k in kept else o for k, o in enumerate(outs)], *tokens),
        in_specs=[spec(pltpu.SMEM)]
        + [spec(pl.ANY if k in far else pltpu.VMEM) for k in range(len(args))]
        + [spec(pl.ANY)] * len(after),
        out_specs=(
            *[spec(pltpu.HBM if k in kept else pltpu.VMEM) for k in range(len(outs))],
            *[spec(pltpu.VMEM) for _ in tokens],
        ),
        scratch_shapes=list(scratch) + buffers + semaphores,
        compiler_params=pltpu.CompilerParams(vmem_limit_bytes=size + extra + MARGIN),
        cost_estimate=pl.CostEstimate(flops=int(micros * PACE), bytes_accessed=size, transcendentals=0),
        name=name,
    )(place, *args, *after)
    result = list(result)
    if token:
        ready = result.pop()
        TOKENS.update((id(value), (value, ready)) for value in result)
    return result


def normalize(rows):
    centered = rows - jnp.mean(rows, axis=-1, keepdims=True)
    scale = lax.rsqrt(jnp.mean(centered * centered, axis=-1, keepdims=True) + 1e-05)
    return centered * scale, scale


def norm_back(grad, scaled, scale, gain):
    weighted = grad * gain
    mean_one = jnp.mean(weighted, axis=-1, keepdims=True)
    mean_two = jnp.mean(weighted * scaled, axis=-1, keepdims=True)
    return scale * (weighted - mean_one - scaled * mean_two)


def column_sum(rows):
    return jnp.sum(rows, axis=0, keepdims=True)


def rope_tables():
    position = jnp.arange(SEQ, dtype=F32)
    frequency = 10000.0 ** (-jnp.arange(0, HEAD_DIM, 2, dtype=F32) / HEAD_DIM)
    angles = position[:, None] * frequency[None, :]
    cos, sin = jnp.cos(angles), jnp.sin(angles)
    return jnp.tile(cos, (1, 8)), jnp.tile(jnp.concatenate([-sin, sin], axis=1), (1, 4))


def swapped(rows):
    low = lax.broadcasted_iota(jnp.int32, rows.shape, 1) % HEAD_DIM < HEAD_DIM // 2
    return jnp.where(low, pltpu.roll(rows, 128 - HEAD_DIM // 2, 1), pltpu.roll(rows, HEAD_DIM // 2, 1))


def group_heads():
    for head in range(GROUP_HEADS):
        yield head, (head // 4) * 128, head % 4


def head_only(rows, lane):
    owner = lax.broadcasted_iota(jnp.int32, rows.shape, 1) // HEAD_DIM
    return jnp.where(owner == lane, rows, jnp.zeros_like(rows))


def halves(place):
    core = place[1]
    return pl.multiple_of(core * HALF, 16), pl.multiple_of((1 - core) * HALF, 16)


def first_norm_kernel(place, move, tokens, vectors, hidden):
    scaled, _ = normalize(tokens[...].astype(F32))
    hidden[...] = (scaled * vectors[0:1, :] + vectors[1:2, :]).astype(BF16)


def stack_into(out, parts):
    for source, part in enumerate(parts):
        out[source] = part[...]


def hand_on_kernel(place, move, value, out):
    out[...] = value[...]


def line_kernel(place, move, *refs):
    cargo = (len(refs) - 5) // 2
    stack_into(refs[4 + cargo], refs[:4])
    for source in range(cargo):
        refs[5 + cargo + source][...] = refs[4 + source][...]


def make_line(place, parts, cargo, after):
    outs = [shape((4, *parts[0].shape))] + [shape(value.shape) for value in cargo]
    return call(line_kernel, "line", outs, place, (*parts, *cargo), 0.6, after=after, token=False)


def pack_kernel(place, move, *refs):
    groups, shards, (packed, lines) = refs[:3], refs[3:7], refs[7:]
    stack_into(packed, groups)
    rows = lines.shape[0] // 8
    for source in range(8):
        side, line = source // 4, source % 4
        lines[source * rows : (source + 1) * rows, :] = shards[line][side * rows : (side + 1) * rows, :]


def pack(place, groups, shards, after):
    outs = [shape((3, *groups[0].shape)), shape((4 * shards[0].shape[0], D))]
    return call(pack_kernel, "pack", outs, place, (*groups, *shards), 1.0, after=after, token=False)


def attention_forward_kernel(groups, place, move, hidden, bias, cos, sin, *refs):
    flush, fetch = move
    count = len(groups)
    mine, other, *refs = refs
    cargo = (len(refs) - 7 * count) // 2
    if cargo:
        for source in range(cargo):
            refs[7 * count + cargo + source][...] = refs[source][...]
        refs = refs[cargo : cargo + 7 * count]
    weights, weights_out, qs, ks, vs, probs, mixed = [refs[part * count : (part + 1) * count] for part in range(7)]
    z = place[0]
    first, second = halves(place)
    rows = hidden[...]
    windows = rows.shape[0] // SEQ
    for step, which in enumerate(groups):
        weight, prob_out = weights[step], probs[step]
        group = place[2] ^ which
        for part in range(4):
            source = z ^ part
            pieces = mine[step, source], other[step, source]
            for offset, piece in zip((first, second), pieces):
                if part < 3:
                    weight[part, pl.ds(offset, HALF), :] = piece
                else:
                    weights_out[step][pl.ds(offset, HALF), :] = piece
            if part < 3:
                weight[part, GROUP:WIDE, :] = jnp.zeros((WIDE - GROUP, D), BF16)
        flush(weight)
        for part, out in ((0, qs[step]), (1, ks[step]), (2, vs[step])):
            proj = nt(rows, weight[part]) + bias[group, part : part + 1, :]
            for window in range(windows):
                span = slice(window * SEQ, (window + 1) * SEQ)
                for tile in (0, 128):
                    piece = proj[span, tile : tile + 128]
                    if part < 2:
                        piece = piece * cos[...] + swapped(piece) * sin[...]
                    out[span, tile : tile + 128] = piece.astype(BF16)
            flush(out)
        for window in range(windows):
            span = slice(window * SEQ, (window + 1) * SEQ)
            visible = lax.broadcasted_iota(jnp.int32, (SEQ, 1), 0) < place[4 + window]
            probs_of, values_of = [], []
            for head, tile, lane in group_heads():
                keys = head_only(ks[step][span, tile : tile + 128], lane)
                scores = nt(keys, qs[step][span, tile : tile + 128])
                scores = jnp.where(visible, scores, -1e30)
                top = jnp.max(scores, axis=0, keepdims=True)
                exponent = jnp.exp2((scores - top) * (SCALE * LOG2_E))
                prob = (exponent * (1.0 / column_sum(exponent))).astype(BF16)
                prob_out[window * GROUP_HEADS + head] = prob
                flush(prob_out, window * GROUP_HEADS + head)
                probs_of.append(prob)
                values_of.append(head_only(vs[step][span, tile : tile + 128], lane))
            out = tn(jnp.concatenate(probs_of[:4], axis=0), jnp.concatenate(values_of[:4], axis=0))
            mixed[step][0:128, span] = out.astype(BF16).T
            mixed[step][128:GROUP, span] = tn(probs_of[4], values_of[4]).astype(BF16).T[0 : GROUP - 128]


def attention_forward(groups, place, hidden, bias, cos, sin, mine, other, after, cargo=()):
    rows = hidden.shape[0]
    maps = rows // SEQ * GROUP_HEADS
    count = len(groups)
    kinds = [Kept((3, WIDE, D)), shape((GROUP, D))] + [Kept((rows, WIDE))] * 3
    kinds += [Kept((maps, SEQ, SEQ)), shape((GROUP, rows))]
    out = call(
        functools.partial(attention_forward_kernel, groups), "attention_forward",
        [kind for kind in kinds for _ in groups] + [shape(value.shape) for value in cargo], place,
        (hidden, bias, cos, sin, mine, other, *cargo), 4.8 * count,
        after=after, copies=count * (4 + maps),
    )
    return [out[step : 7 * count : count] for step in range(count)] + out[7 * count :]


def middle_kernel(place, move, tokens, vectors, *refs):
    flush, fetch = move
    mixed_in, weight_in, *refs = refs[:4], refs[4:8], *refs[8:]
    middle, normed, mixed, weight, stage = refs
    for which in range(GROUPS):
        offset = pl.multiple_of((place[2] ^ which) * GROUP, 32)
        stage[pl.ds(offset, GROUP), :] = mixed_in[which][...]
        weight[pl.ds(offset, GROUP), :] = weight_in[which][...]
    mixed[...] = stage[...].T
    rows = tokens[...].astype(F32) + nt(mixed[...], weight[...]) + vectors[5:6, :]
    middle[...] = rows
    scaled, _ = normalize(rows)
    normed[...] = (scaled * vectors[6:7, :] + vectors[7:8, :]).astype(BF16)


def middle_layer(place, tokens, vectors, mixed, weights, after):
    rows = tokens.shape[0]
    outs = [shape((rows, D), F32), shape((rows, D)), shape((rows, D)), shape((D, D))]
    return call(
        middle_kernel, "middle", outs, place, (tokens, vectors, *mixed, *weights), 0.2,
        [pltpu.VMEM((D, rows), BF16)], after, token=False)


def store_quarter(outs, which, value):
    low = value.astype(BF16)
    if which < 3:
        outs[which][...] = low
    else:
        outs[3][...], outs[4][...] = low[: QUARTER // 2], low[QUARTER // 2 :]


def five_parts():
    return [shape((QUARTER, D))] * 3 + [shape((QUARTER // 2, D))] * 2


def quarter(parts, which, side):
    if which < 3:
        return parts[which][side * QUARTER : (side + 1) * QUARTER, :]
    rows = slice(side * 80, (side + 1) * 80)
    return jnp.concatenate([part[rows, :] for part in parts[3:]], axis=0)


def hidden_forward_kernel(quarters, place, move, *refs):
    count = 4 if 3 in quarters else 3
    parts, (bias, normed, normed_pair, back, back_pair), refs = refs[:count], refs[count : count + 5], refs[count + 5 :]
    parts = parts if count == 3 else (None, None, None, *parts)
    active, slopes, grads_down = refs[0], refs[1 : 1 + len(quarters)], refs[1 + len(quarters) :]
    grads_down = grads_down if count == 3 else (None, None, None, *grads_down)
    rows = normed.shape[0]
    for step, which in enumerate(quarters):
        up = quarter(parts, which, 0)
        column = jnp.broadcast_to(bias[which], (8, QUARTER)).T[:, 0:1]
        total = 0.0
        for part, inputs, grads in ((0, normed, back), (1, normed_pair, back_pair)):
            span = slice(part * rows, (part + 1) * rows)
            value = nt(up, inputs[...]) + column
            cdf = 0.5 + 0.5 * lax.erf(value * (0.5**0.5))
            low = (value * cdf).astype(BF16)
            active[step, :, span] = low
            slopes[step][:, span] = (cdf + value * jnp.exp(-0.5 * value * value) * 0.3989422804014327).astype(BF16)
            total = total + nn(low, grads[...])
        store_quarter(grads_down, which, total)


def hidden_forward(quarters, place, parts, bias, normed, normed_pair, back, back_pair, after):
    rows = 2 * normed.shape[0]
    count = len(quarters)
    outs = [shape((count, QUARTER, rows))] + [shape((QUARTER, rows))] * count
    outs += five_parts()[3:] if 3 in quarters else five_parts()[:3]
    active, *rest = call(
        functools.partial(hidden_forward_kernel, quarters), "hidden_forward", outs, place,
        (*parts, bias, normed, normed_pair, back, back_pair), 1.7 * count, after=after,
    )
    return active, rest[:count], rest[count:]


def hidden_backward_kernel(place, move, *refs):
    parts, slopes, (back, back_pair), refs = refs[:7], refs[7:11], refs[11:13], refs[13:]
    grad_pre, own, pair, up = refs
    rows = back.shape[0]
    for which in range(4):
        units = slice(which * QUARTER, (which + 1) * QUARTER)
        up[units, :] = quarter(parts, which, 0)
        down = quarter(parts, which, 1)
        for part, grads in ((0, back), (1, back_pair)):
            span = slice(part * rows, (part + 1) * rows)
            wide = nt(down, grads[...]) * slopes[which][:, span].astype(F32)
            grad_pre[units, span] = wide.astype(BF16)
    for out, span in ((pair, slice(rows, 2 * rows)), (own, slice(0, rows))):
        out[...] = tn(grad_pre[:, span], up[...]).astype(out.dtype)


def hidden_backward(place, parts, slopes, back, back_pair):
    rows = back.shape[0]
    outs = [shape((4 * QUARTER, 2 * rows)), shape((rows, D), F32), shape((rows, D))]
    return call(
        hidden_backward_kernel, "hidden_backward", outs, place, (*parts, *slopes, back, back_pair), 5.0,
        [pltpu.VMEM((4 * QUARTER, D), BF16)],
    )


def up_gradient_kernel(place, move, grad_pre, normed, normed_pair, *refs):
    grads, grad_bias = refs[:5], refs[5]
    for which in range(4):
        units = slice(which * QUARTER, (which + 1) * QUARTER)
        low = grad_pre[units, :]
        rows = normed.shape[0]
        store_quarter(grads, which, nn(low[:, :rows], normed[...]) + nn(low[:, rows:], normed_pair[...]))
        bias = jnp.sum(low.astype(F32), axis=1, keepdims=True)
        for source in range(4):
            grad_bias[4 * which + source] = jnp.broadcast_to(bias[source * 80 : (source + 1) * 80], (80, 8)).T


def up_gradient(place, grad_pre, normed, normed_pair, after):
    outs = five_parts() + [shape((16, 8, 80), F32)]
    *grads, bias = call(
        up_gradient_kernel, "up_gradient", outs, place, (grad_pre, normed, normed_pair), 4.0, after=after
    )
    return grads, bias


def output_kernel(place, move, most, last, middle, vectors, *refs):
    parts, (own, pair) = refs[:7], refs[7:]
    rows = own.shape[0]
    down = jnp.concatenate([quarter(parts, which, 1) for which in range(4)], axis=0)
    for out, span in ((pair, slice(rows, 2 * rows)), (own, slice(0, rows))):
        left = jnp.concatenate([most[which, :, span] for which in range(3)] + [last[0, :, span]], axis=0)
        total = tn(left, down)
        if out is own:
            total = total + middle[...] + vectors[8:9, :]
        out[...] = total.astype(out.dtype)


def output_layer(place, active, middle, vectors, parts, after):
    rows = middle.shape[0]
    outs = [shape((rows, D), F32), shape((rows, D))]
    return call(
        output_kernel, "output", outs, place, (*active, middle, vectors, *parts), 2.8, after=after
    )


def middle_backward_kernel(
    place, move, own, pair, middle, back, vectors, mixed, weight, grad_middle, sums, grad_mixed, mine, other, stage, stage_mixed
):
    grad = own[...] + pair[...].astype(F32)
    scaled, scale = normalize(middle[...])
    wide = back[...].astype(F32)
    total = wide + norm_back(grad, scaled, scale, vectors[6:7, :])
    grad_middle[...] = total
    sums[0:1, :] = column_sum(total)
    sums[1:2, :] = column_sum(grad * scaled)
    sums[2:3, :] = column_sum(grad)
    sums[3:4, :] = column_sum(wide)
    sums[4:8, :] = jnp.zeros((4, D), F32)
    low = total.astype(BF16)
    stage_mixed[...] = nt(weight[...].T, low).astype(BF16)
    stage[...] = tn(low, mixed[...]).astype(BF16)
    first, second = halves(place)
    for which in range(GROUPS):
        offset = (place[2] ^ which) * GROUP
        grad_mixed[which] = stage_mixed[pl.ds(pl.multiple_of(offset, 32), GROUP), :]
        mine[which] = stage[pl.ds(pl.multiple_of(offset + first, 16), HALF), :]
        other[which] = stage[pl.ds(pl.multiple_of(offset + second, 16), HALF), :]


def middle_backward(place, own, pair, middle, back, vectors, mixed, weight, after):
    rows = own.shape[0]
    outs = [shape((rows, D), F32), shape((8, D), F32), shape((GROUPS, GROUP, rows))]
    outs += [shape((GROUPS, HALF, D)), shape((GROUPS, HALF, D))]
    return call(
        middle_backward_kernel, "middle_backward", outs, place,
        (own, pair, middle, back, vectors, mixed, weight), 3.0,
        [pltpu.VMEM((D, D), BF16), pltpu.VMEM((D, rows), BF16)], after,
    )


def attention_backward_kernel(groups, place, move, grad_mixed, hidden, cos, sin, out_mine, out_other, *refs):
    count = len(groups)
    qs, ks, vs, probs, dqs, dks, dvs = [refs[part * count : (part + 1) * count] for part in range(7)]
    biases, (mine, other, stage) = refs[7 * count : 8 * count], refs[8 * count :]
    rows = hidden.shape[0]
    first, second = halves(place)
    for step, which in enumerate(groups):
        q, k, v, prob_in, dq_out, dk_out, dv_out = (
            qs[step], ks[step], vs[step], probs[step], dqs[step], dks[step], dvs[step]
        )
        for window in range(rows // SEQ):
            span = slice(window * SEQ, (window + 1) * SEQ)
            grad = grad_mixed[which, :, span].T
            tail = jnp.concatenate([grad[:, 128:GROUP], jnp.zeros((SEQ, WIDE - GROUP), BF16)], axis=1)
            grads = {0: grad[:, :128], 128: tail}
            lows, slopes, grads_of, queries_of, keys_of = [], [], [], [], []
            for head, tile, lane in group_heads():
                cols = slice(tile, tile + 128)
                low = prob_in[window * GROUP_HEADS + head]
                prob = low.astype(F32)
                weighted = prob * nt(head_only(v[span, cols], lane), grads[tile])
                lows.append(low)
                slopes.append((weighted - prob * column_sum(weighted)).astype(BF16))
                grads_of.append(head_only(grads[tile], lane))
                queries_of.append(head_only(q[span, cols], lane))
                keys_of.append(head_only(k[span, cols], lane))
            for tile, heads in ((0, slice(0, 4)), (128, slice(4, 5))):
                cols = slice(tile, tile + 128)
                down = jnp.concatenate(slopes[heads], axis=1)
                dv_out[span, cols] = nn(
                    jnp.concatenate(lows[heads], axis=1), jnp.concatenate(grads_of[heads], axis=0)
                ).astype(BF16)
                piece = nn(down, jnp.concatenate(queries_of[heads], axis=0)) * SCALE
                dk_out[span, cols] = (piece * cos[...] - swapped(piece) * sin[...]).astype(BF16)
                piece = tn(jnp.concatenate(slopes[heads], axis=0), jnp.concatenate(keys_of[heads], axis=0)) * SCALE
                dq_out[span, cols] = (piece * cos[...] - swapped(piece) * sin[...]).astype(BF16)
        biases[step][...] = jnp.zeros((8, WIDE), F32)
        for part, out in ((0, dq_out), (1, dk_out), (2, dv_out)):
            values = out[...]
            stage[step, part] = tn(values, hidden[...]).astype(BF16)
            mine[step, part] = stage[step, part, pl.ds(first, HALF), :]
            other[step, part] = stage[step, part, pl.ds(second, HALF), :]
            biases[step][part : part + 1, :] = column_sum(values.astype(F32))
        mine[step, 3] = out_mine[which]
        other[step, 3] = out_other[which]


def attention_backward(groups, place, grad_mixed, hidden, cos, sin, out_mine, out_other, saved, after):
    rows = hidden.shape[0]
    count = len(groups)
    outs = [shape((rows, WIDE))] * (3 * count) + [shape((8, WIDE), F32)] * count + [shape((count, 4, HALF, D))] * 2
    *out, mine, other = call(
        functools.partial(attention_backward_kernel, groups), "attention_backward", outs, place,
        (grad_mixed, hidden, cos, sin, out_mine, out_other, *[group[k] for k in range(4) for group in saved]),
        4.7 * count,
        [pltpu.VMEM((count, 3, WIDE, D), BF16)], after,
    )
    return [out[step::count] for step in range(count)], mine, other


def first_backward_kernel(place, move, tokens, grad_middle, vectors, *refs):
    parts, weights, biases, (middle_sums, units), refs = refs[:12], refs[12:16], refs[16:20], refs[20:22], refs[22:]
    input_grad, sums, unit_rows = refs
    z, plane, core = place[0], place[2], place[3]
    grad = 0.0
    for which in range(GROUPS):
        for part in range(3):
            grad = grad + nn(parts[which * 3 + part][...], weights[which][part])
    scaled, scale = normalize(tokens[...].astype(F32))
    input_grad[...] = (grad_middle[...] + norm_back(grad, scaled, scale, vectors[0:1, :])).astype(BF16)
    sums[...] = jnp.zeros((24, D), F32)
    sums[0:1, :] = column_sum(grad * scaled)
    sums[1:2, :] = column_sum(grad)
    sums[2:6, :] = middle_sums[0:4, :]
    for group in range(GROUPS):
        value = sum(jnp.where((plane ^ which) == group, biases[which][...], 0.0) for which in range(GROUPS))
        row, column = 8 + 4 * (group // 2), WIDE * (group % 2)
        sums[row : row + 4, column : column + WIDE] = value[0:4]
    unit_rows[...] = jnp.zeros((4, 8, 128), F32)
    for which in range(4):
        for source in range(4):
            row = (plane ^ which) * 2 + core
            unit_rows[z ^ source, pl.ds(row, 1), 0:80] = units[4 * which + source, 0:1, :]
    for line in range(4):
        sums[16:24, line * 128 : (line + 1) * 128] = unit_rows[line]


def first_backward(place, tokens, grad_middle, vectors, parts, weights, biases, middle_sums, units, after):
    rows = tokens.shape[0]
    outs = [shape((rows, D)), shape((24, D), F32)]
    return call(
        first_backward_kernel, "first_backward", outs, place,
        (tokens, grad_middle, vectors, *parts, *weights, *biases, middle_sums, units),
        0.2, [pltpu.VMEM((4, 8, 128), F32)], after, token=False)


def unpack_vector(sums):
    group_rows = [sums[8 + 4 * (g // 2) :, WIDE * (g % 2) :][:3, :GROUP] for g in range(GROUPS)]
    units = sums[16:24, :512].reshape(8, 4, 128)[:, :, :80].transpose(1, 0, 2).reshape(4, D)
    return jnp.concatenate([sums[0:2], jnp.concatenate(group_rows, axis=1), sums[2:6], units])


def ordered_sum_kernel(which, place, move, *refs):
    total = 0.0
    for index in range(4):
        total = total + sum(jnp.where((place[which] ^ step) == index, refs[step][...], 0.0) for step in range(4))
    refs[4][...] = total


def ordered_sum(place, which, parts, after=()):
    outs = [shape(parts[0].shape, F32)]
    return call(functools.partial(ordered_sum_kernel, which), "ordered_sum", outs, place, parts, 0.6, after=after, token=False)[0]


def attention_sum_kernel(place, move, *refs):
    parts, (own, *sent), stage = refs[:4], refs[4:8], refs[8]
    stage[...] = sum(value[...].astype(F32) for value in parts[2:]) + sum(value[1].astype(F32) for value in parts[:2])
    own[...] = stage[place[0]]
    for steps, out in enumerate(sent):
        out[...] = stage[place[0] ^ (steps + 1)].astype(BF16)


def attention_sum(place, parts, after):
    dims = parts[2].shape
    outs = [shape(dims[1:], F32)] + [shape(dims[1:])] * 3
    return call(
        attention_sum_kernel, "attention_sum", outs, place, parts, 1.0, [pltpu.VMEM(dims, F32)], after=after
    )


def add(out, *parts):
    out[...] = sum(part.astype(F32) for part in parts).astype(out.dtype)


def keep_and_send(parts, keep, sent):
    total = sum(part[...].astype(F32) for part in parts)
    keep[...] = total[0:2]
    sent[...] = total[2:4].astype(BF16)


def merge_into(along_y, along_x, first, second, out_y, out_x):
    out_y[0:2] = along_y[0:2]
    add(out_y.at[2:4], along_y[2:4], second[...])
    add(out_x.at[0:2], along_x[0:2], first[...])
    out_x[2:4] = along_x[2:4]


def merge_kernel(place, move, along_y, along_x, *refs):
    merge_into(along_y, along_x, *refs)


def merge(place, along_y, along_x, first, second, after):
    outs = [shape(along_y.shape)] * 2
    return call(merge_kernel, "merge", outs, place, (along_y, along_x, first, second), 1.0, after=after)


def exchange_one_kernel(place, move, *refs):
    downs, (along_y, along_x, first, second), refs = refs[:3], refs[3:7], refs[7:]
    keep, sent, out_y, out_x = refs
    keep_and_send(downs, keep, sent)
    merge_into(along_y, along_x, first, second, out_y, out_x)


def exchange_one(place, downs, ups, after):
    dims = downs[0].shape
    outs = [shape((2, *dims[1:]), F32), shape((2, *dims[1:]))] + [shape(dims)] * 2
    return call(
        exchange_one_kernel, "exchange_one", outs, place,
        (*downs, *ups), 2.0, after=after,
    )


def cores_one_kernel(place, move, mine, other, half_y, half_x, rest):
    add(half_y, mine[0, 0:2], other[0, 0:2])
    add(half_x, mine[0, 2:4], other[0, 2:4])
    add(rest, mine[1], other[1])


def cores_one(place, mine, other, after):
    dims = mine.shape[1:]
    outs = [shape((2, *dims[1:]))] * 2 + [shape(dims)]
    return call(cores_one_kernel, "cores_one", outs, place, (mine, other), 1.0, after=after)


def exchange_two_kernel(place, move, *refs):
    ups, (keep_in, line_in), (keep, sent, own, line) = refs[:3], refs[3:5], refs[5:]
    keep_and_send(ups, keep, sent)
    total = keep_in[...] + line_in[...].astype(F32)
    own[...] = total[0]
    line[...] = total[1].astype(BF16)


def exchange_two(place, ups, keep, line, after):
    dims = ups[0].shape
    outs = [shape((2, *dims[1:]), F32), shape((2, *dims[1:])), shape(dims[1:], F32), shape(dims[1:])]
    return call(
        exchange_two_kernel, "exchange_two", outs, place, (*ups, keep, line), 12.0, after=after
    )


def exchange_three_kernel(
    place, move, rest, mine, other, first, second, keep, line_in, down_line, along_y, along_x, own, line
):
    add(along_x.at[0:2], rest[0:2], first[...])
    along_x[2:4] = rest[2:4]
    add(along_y.at[0:2], mine[0, 0:2], other[0, 0:2])
    add(along_y.at[2:4], mine[0, 2:4], other[0, 2:4], second[...])
    total = keep[...] + line_in[...].astype(F32)
    own[...] = total[0]
    line[0] = total[1].astype(BF16)
    line[1] = down_line[...]


def exchange_three(place, rest, mine, other, halves_in, keep, line, down_line, after):
    dims = rest.shape
    outs = [shape(dims)] * 2 + [shape(dims[1:], F32), shape((2, *dims[1:]))]
    return call(
        exchange_three_kernel, "exchange_three", outs, place, (rest, mine, other, *halves_in, keep, line, down_line), 1.0,
        after=after,
    )


def core_runs(place):
    for which in range(4):
        for source in range(4):
            run = ((place[0] ^ source) * 4 + (place[2] ^ which)) * 2 + place[3]
            yield which, source, pl.ds(pl.multiple_of(run * 80, 16), 80)


def take_runs_kernel(place, move, up, down, *outs):
    for which, source, rows in core_runs(place):
        for side, full in enumerate((up, down)):
            if which < 3:
                start = side * QUARTER + source * 80
                outs[which][start : start + 80, :] = full[rows, :]
            else:
                outs[3 + source][side * 80 : (side + 1) * 80, :] = full[rows, :]


def take_runs(place, full):
    outs = [shape((2 * QUARTER, D))] * 3 + [shape((160, D))] * 4
    return call(take_runs_kernel, "take_runs", outs, place, full, 1.0, token=False)


def place_runs_kernel(place, move, *refs):
    full = refs[5]
    full[...] = jnp.zeros_like(full)
    for which, source, rows in core_runs(place):
        part, offset = (which, source) if which < 3 else (3 + source // 2, source % 2)
        full[rows, :] = refs[part][offset * 80 : (offset + 1) * 80, :].astype(F32)


def place_runs(place, quarters):
    return call(place_runs_kernel, "place_runs", [shape((FF, D), F32)], place, quarters, 2.0, token=False)[0]


def pick(array, index):
    return lax.dynamic_index_in_dim(array, index, 0, keepdims=False)


def step_into(rate, gradient, state, outs):
    weight, first, second = state
    grad, second_new, new = outs
    grad[...] = gradient
    second_new[...], new[...] = adamw(weight[...], first[...], second[...], gradient, rate)


def finish_attention_kernel(place, move, own, one, two, three, weight, first, second, *outs):
    total = own[...]
    for value in (one, two, three):
        total = total + value[...].astype(F32)
    step_into(0.1, total, (weight, first, second), outs)


def finish_attention(place, own, line, state, after):
    out = call(
        finish_attention_kernel, "finish_attention", [shape(own.shape, F32)] * 3, place,
        (own, *line, *[value.T for value in state]), 0.3, after=after, token=False)
    return [value.T for value in out]


def finish_hidden_kernel(place, move, *refs):
    owns, arrived, refs = refs[:2], refs[2], refs[3:]
    for matrix in range(2):
        state = refs[3 * matrix : 3 * matrix + 3]
        outs = refs[6 + 3 * matrix : 9 + 3 * matrix]
        step_into(0.1, owns[matrix][...] + arrived[matrix].astype(F32), state, outs)


def finish_hidden(place, owns, arrived, state, after):
    out = call(
        finish_hidden_kernel, "finish_hidden", [shape(owns[0].shape, F32)] * 6, place,
        (*owns, arrived, *[value.T for value in state]), 0.3, after=after,
    )
    return [value.T for value in out[:3]], [value.T for value in out[3:]], out[0]


def result_kernel(place, move, own, pair, out):
    out[...] = (own[...] + pair[...].astype(F32)).astype(BF16)


def result_layer(place, own, pair, after):
    return call(result_kernel, "result", [shape(pair.shape)], place, (own, pair), 12.0, after=after)[0]


def adamw(weight, first_moment, second_moment, gradient, rate_value):
    first_new = 0.9 * first_moment + 0.1 * gradient
    second_new = 0.999 * second_moment + 0.001 * gradient * gradient
    corrected = first_new / (1.0 - 0.9**STEP) / (jnp.sqrt(second_new / (1.0 - 0.999**STEP)) + 1e-08)
    return (second_new, weight - rate_value * (corrected + 0.01 * weight))


class Layout:
    def __init__(self, total):
        self.total = total
        self.block = 4 * D // total
        self.stride = total // 4
        self.me = lax.axis_index(AXES)
        self.core = lax.rem(self.me, 2)

    def swap(self, value, mask):
        return lax.ppermute(value, AXES, [(i, i ^ mask) for i in range(self.total)])

    def shift(self, value, steps):
        pairs = [(i, (i + self.stride * steps) % self.total) for i in range(self.total)]
        return lax.ppermute(value, AXES, pairs)


    def hidden_index(self):
        order = jnp.arange(16)
        z, plane = self.place[0], self.place[2]
        return ((z ^ lax.rem(order, 4)) * 4 + (plane ^ (order // 4))) * 2 + self.core


class Ring(Layout):
    def __init__(self, total):
        super().__init__(total)
        self.ring = True
        self.z = self.me // 8
        self.plane = lax.rem(self.me // 2, 4)
        self.place = (self.z, self.core, self.plane)

    def along_z(self, value):
        return [value] + [self.swap(value, 8 * s) for s in (1, 2, 3)]

    def in_plane(self, value, each=None):
        return [value] + [self.swap(each[r].reshape(value.shape) if each else value, 2 * r) for r in (1, 2, 3)]

    def corner(self, *value):
        return [self.swap(value[0], 2), self.swap(value[1], 4)]

    def send_plane(self, along_y, along_x):
        return [self.swap(along_y, 2), self.swap(along_x, 4)]

    def all_total(self, value, after):
        value = ordered_sum(self.vector, 2, self.in_plane(value), after)
        return ordered_sum(self.vector, 0, [value] + [self.swap(value, 8 * s) for s in (1, 2, 3)])


class Whole(Layout):
    def __init__(self, total):
        super().__init__(total)
        self.ring = False
        self.plane = jnp.int32(0)
        self.place = (jnp.int32(0),) * 3

    def gather(self, attn, up, down):
        full = lax.all_gather(attn, AXES, axis=0, tiled=True).reshape(4, 4, 2, HALF, D)
        mine = [full[:, r, 0] for r in range(4)]
        other = [full[:, r, 1] for r in range(4)]
        both = [lax.all_gather(value, AXES, axis=0, tiled=True) for value in (up, down)]
        return mine, other, take_runs(self.vector, both)

    def scatter_hidden(self, grads):
        return lax.psum_scatter(place_runs(self.vector, grads), AXES, scatter_dimension=0, tiled=True)

    def scatter_attention(self, mine, other):
        full = jnp.stack([jnp.stack(mine, axis=1), jnp.stack(other, axis=1)], axis=2)
        return lax.psum_scatter(full.astype(F32).reshape(4 * D, D), AXES, scatter_dimension=0, tiled=True)


def per_device(
    total,
    tokens,
    cotangent,
    lengths,
    offsets,
    attn_weight,
    attn_first,
    attn_second,
    up_weight,
    up_first,
    up_second,
    down_weight,
    down_first,
    down_second,
    vectors,
    vec_first,
    vec_second,
):
    TOKENS.clear()
    lay = Ring(total) if total == 32 else Whole(total)
    counts = jnp.minimum(lengths - offsets, SEQ).reshape(-1)
    rows = counts.shape[0] * SEQ
    place = lay.vector = jnp.concatenate([jnp.stack([*lay.place, lay.core]).astype(jnp.int32), counts])
    cos, sin = rope_tables()

    flat = tokens.reshape(rows, D)
    back = cotangent.reshape(rows, D)
    back_pair = lay.swap(back, 1)
    (hidden,) = call(first_norm_kernel, "first_norm", [shape((rows, D))], place, (flat, vectors), 1.0)
    bias = jnp.pad(vectors[2:5].reshape(3, GROUPS, GROUP).transpose(1, 0, 2), ((0, 0), (0, 0), (0, WIDE - GROUP)))

    chosen = (lay.hidden_index()[:, None] == jnp.arange(32)[None, :]).astype(F32)
    bias_up = jnp.dot(chosen, vectors[9:].reshape(32, 80), precision=lax.Precision.HIGHEST).reshape(4, 1, QUARTER)

    if lay.ring:
        shards = jnp.concatenate([up_weight.T, down_weight.T]).astype(BF16)
        attn_parts = lay.along_z(attn_weight.T.astype(BF16))
        corner = lay.swap(shards, 6)
        line, shards = make_line(place, attn_parts, [shards], [hidden, bias_up, bias])
        far_shard = lay.swap(shards, 16)
        groups = lay.in_plane(line)[1:]
        other = lay.swap(line, 1)
        mine = line[None]
    else:
        mine, other, hidden_parts = lay.gather(
            attn_weight.T.astype(BF16), up_weight.T.astype(BF16), down_weight.T.astype(BF16)
        )
        mine, packed = mine[0][None], jnp.stack(mine[1:])
        other, packed_other = other[0], jnp.stack(other[1:])
    forward = attention_forward(
        (0,), place, hidden, bias, cos, sin, mine, other[None], [corner] if lay.ring else []
    )
    if lay.ring:
        shards = [shards, lay.swap(shards, 8), far_shard, lay.swap(far_shard, 8)]
        packed, lines = pack(place, groups, shards, [forward[0][2]])
        hidden_parts = [lines, lay.swap(lines, 2), lay.swap(lines, 4)]
        packed_other = lay.swap(packed, 1)
        (corner,) = call(
            hand_on_kernel, "hand_on", [shape(corner.shape)], place, (corner,), 0.4, after=[packed_other], token=False
        )
        corner_far = lay.swap(corner, 16)
        corners = [corner, lay.swap(corner, 8), corner_far, lay.swap(corner_far, 8)]
        hidden_parts = hidden_parts + corners
    after = [forward[0][2]]
    forward += attention_forward((1, 2, 3), place, hidden, bias, cos, sin, packed, packed_other, after)
    weights = [group[0] for group in forward]
    middle, normed, mixed, out_weight = middle_layer(
        place, flat, vectors, [group[6] for group in forward], [group[1] for group in forward],
        corners[1:3] if lay.ring else [],
    )
    normed_pair = lay.swap(normed, 1)
    both = (normed, normed_pair, back, back_pair)
    most, slope, grad_down = hidden_forward((0, 1, 2), place, hidden_parts[:3], bias_up, *both, [])
    rest, *last = hidden_forward((3,), place, hidden_parts[3:], bias_up, *both, [most])
    active, slope, grad_down = (most, rest), slope + last[0], grad_down + last[1]
    if lay.ring:
        grad_down = [value.reshape(-1, 80, D) for value in grad_down]
        down_corner = lay.corner(*grad_down[3:])
    grad_pre, own, pair = hidden_backward(place, hidden_parts, slope, back, back_pair)
    gradient_after, middle_after, after = [], [], []
    if lay.ring:
        down_sent = merge(place, *grad_down[1:3], *down_corner, [own])
        gradient_after = down_sent[:1]
        down_sent = middle_after = lay.send_plane(*down_sent)
    grad_up, grad_bias_up = up_gradient(place, grad_pre, normed, normed_pair, gradient_after)
    if lay.ring:
        grad_up = [value.reshape(-1, 80, D) for value in grad_up]
        up_corner = lay.corner(*grad_up[3:])
    out_own, out_pair = output_layer(place, active, middle, vectors, hidden_parts, [grad_bias_up])
    out_pair = lay.swap(out_pair, 1)
    grad_middle, sums, grad_mixed, out_mine, out_other = middle_backward(
        place, own, lay.swap(pair, 1), middle, back, vectors, mixed, out_weight, [out_own] + middle_after
    )

    def backward_of(groups, after):
        saved = [forward[r][2:6] for r in groups]
        return attention_backward(groups, place, grad_mixed, hidden, cos, sin, out_mine, out_other, saved, after)

    if lay.ring:
        keep, line, *up_sent = exchange_one(place, [grad_down[0], *down_sent], [*grad_up[1:3], *up_corner], [sums])
        down_line = lay.swap(line, 16)
        up_sent = lay.send_plane(*up_sent)
        after = [keep]
    later, mine_one, other_one = backward_of((3, 2), after)
    after = [later[0][0]]
    if lay.ring:
        other_one = lay.swap(other_one, 1)
        up_keep, up_line, down_own, down_line = exchange_two(
            place, [grad_up[0], *up_sent], keep, down_line, after
        )
        up_line = lay.swap(up_line, 16)
        *attn_corner, along_x = cores_one(place, mine_one, other_one, [up_keep])
        attn_corner = lay.corner(*attn_corner)
        after = [up_keep, along_x]
    sooner, mine_two, other_two = backward_of((1, 0), after)
    backward = [sooner[1], sooner[0], later[1], later[0]]
    other_two, after = lay.swap(other_two, 1) if lay.ring else other_two, [sooner[0][0]]
    if lay.ring:
        after += [*attn_corner, up_line]
    result = result_layer(place, out_own, out_pair, after)
    if lay.ring:
        along_y, along_x, up_own, hidden_line = exchange_three(
            place, along_x, mine_two, other_two, attn_corner, up_keep, up_line, down_line, [result]
        )
        after = [along_y]
    parts = [value for group in backward for value in group[:3]]
    input_grad, vec_sums = first_backward(
        place, flat, grad_middle, vectors, parts, weights, [group[3] for group in backward], sums, grad_bias_up, after
    )
    state = up_weight, up_first, up_second, down_weight, down_first, down_second
    if lay.ring:
        along_y, along_x = lay.send_plane(along_y, along_x)
        hidden_line = lay.swap(hidden_line, 8)
        vec_core = vec_sums + lay.swap(vec_sums, 1)
        attn_own, *attn_line = attention_sum(place, [mine_two, other_two, along_y, along_x], [hidden_line, vec_core])
        vec_sums = lay.all_total(vec_core, [attn_own])
        attn_line = [lay.swap(value, 8 * s) for value, s in zip(attn_line, (1, 2, 3))]
        (grad_up, up_second_new, up_new), (grad_down, down_second_new, down_new), done = finish_hidden(
            place, [up_own, down_own], hidden_line, state, [attn_own]
        )
        grad_attn, attn_second_new, attn_new = finish_attention(
            place, attn_own, attn_line, (attn_weight, attn_first, attn_second), [done]
        )
    else:
        grad_up, grad_down = lay.scatter_hidden(grad_up).T, lay.scatter_hidden(grad_down).T
        order = (mine_two[1], mine_two[0], mine_one[1], mine_one[0])
        order_other = (other_two[1], other_two[0], other_one[1], other_one[0])
        grad_attn = lay.scatter_attention(order, order_other).T
        attn_second_new, attn_new = adamw(attn_weight, attn_first, attn_second, grad_attn, 0.1)
        up_second_new, up_new = adamw(*state[:3], grad_up, 0.1)
        down_second_new, down_new = adamw(*state[3:], grad_down, 0.1)
        vec_sums = lax.psum(vec_sums, AXES)
    grad_vec = unpack_vector(vec_sums)
    vec_second_new, vectors_new = adamw(vectors, vec_first, vec_second, grad_vec, 0.5)
    return (
        result.reshape(tokens.shape),
        input_grad.reshape(tokens.shape),
        grad_attn,
        grad_up,
        grad_down,
        grad_vec,
        attn_second_new,
        up_second_new,
        down_second_new,
        vec_second_new,
        attn_new,
        up_new,
        down_new,
        vectors_new,
    )


def solution(mesh):
    total = mesh.shape["wide"] * mesh.shape["narrow"]
    windows = P(None, AXES, None, None)
    counts = P(None, AXES)
    columns = P(None, AXES)
    in_specs = (windows,) * 2 + (counts,) * 2 + (columns,) * 9 + (P(),) * 3
    out_specs = (windows,) * 2 + (columns,) * 3 + (P(),) + (columns,) * 3 + (P(),) + (columns,) * 3 + (P(),)
    return jax.shard_map(
        functools.partial(per_device, total),
        mesh=mesh,
        in_specs=in_specs,
        out_specs=out_specs,
        check_vma=False,
    )
```

```python
import functools
import math

import jax
import jax.numpy as jnp
from jax import lax
from jax.experimental import pallas as pl
from jax.experimental.pallas import tpu as pltpu
from jax.sharding import PartitionSpec as P

D = 640
HEADS = 20
HEAD_DIM = 32
FF = 2560
SEQ = 256
STEP = 10
AXES = ("wide", "narrow")
GROUPS = 4
GROUP_HEADS = HEADS // GROUPS
GROUP = GROUP_HEADS * HEAD_DIM
HALF = GROUP // 2
WIDE = 256
QUARTER = FF // 8
SCALE = HEAD_DIM ** (-0.5)
LOG2_E = 1.4426950408889634
BF16 = jnp.bfloat16
F32 = jnp.float32
PACE = 1.15e9
MARGIN = 8 * 1024 * 1024


def nt(left, right):
    return lax.dot_general(left, right, (((1,), (1,)), ((), ())), preferred_element_type=F32)


def nn(left, right):
    return jnp.dot(left, right, preferred_element_type=F32)


def tn(left, right):
    return lax.dot_general(left, right, (((0,), (0,)), ((), ())), preferred_element_type=F32)


def shape(dims, kind=BF16):
    return jax.ShapeDtypeStruct(dims, kind)


TOKENS = {}


class Kept:
    def __init__(self, dims, kind=BF16):
        self.struct = shape(dims, kind)


class Far:
    def __init__(self, value):
        self.value = value


def call(kernel, name, outs, place, args, micros, scratch=(), after=(), copies=None, token=True):
    after = [TOKENS[id(value)][1] if id(value) in TOKENS else value for value in after]
    kept = [place_of for place_of, out in enumerate(outs) if isinstance(out, Kept)]
    outs = [out.struct if isinstance(out, Kept) else out for out in outs]
    far = [place_of for place_of, arg in enumerate(args) if isinstance(arg, Far)]
    args = [
        pltpu.with_memory_space_constraint(arg.value, pltpu.HBM) if isinstance(arg, Far) else arg for arg in args
    ]
    buffers = [pltpu.VMEM(a.shape, a.dtype) for a in [outs[k] for k in kept] + [args[k] for k in far]]
    copies = copies or len(kept)
    size = sum(a.size * a.dtype.itemsize for a in args) + sum(o.size * o.dtype.itemsize for o in outs)
    extra = sum(math.prod(s.shape) * s.dtype.itemsize for s in scratch)
    semaphores = [pltpu.SemaphoreType.DMA((copies + len(far),))] if buffers else []

    def body(place_ref, *refs):
        ins, refs = list(refs[: len(args)]), refs[len(args) + len(after) :]
        out_refs, refs = list(refs[: len(outs)]), refs[len(outs) :]
        if token:
            refs[0][...] = jnp.zeros((8, 128), F32)
            refs = refs[1:]
        work, held = refs[: len(scratch)], refs[len(scratch) : len(scratch) + len(buffers)]
        started, targets, coming = [], [], []
        for slot, (k, buffer) in enumerate(zip(far, held[len(kept) :])):
            copy = pltpu.make_async_copy(ins[k], buffer, refs[-1].at[copies + slot])
            copy.start()
            coming.append((buffer, copy))
            ins[k] = buffer
        for k, buffer in zip(kept, held):
            targets.append((buffer, out_refs[k]))
            out_refs[k] = buffer

        def flush(ref, index=None):
            target = next(out for buffer, out in targets if buffer is ref)
            if index is not None:
                ref, target = ref.at[index], target.at[index]
            copy = pltpu.make_async_copy(ref, target, refs[-1].at[len(started)])
            copy.start()
            started.append(copy)

        def fetch(ref):
            next(copy for buffer, copy in coming if buffer is ref).wait()
            return ref

        kernel(place_ref, (flush, fetch), *ins, *out_refs, *work)
        for copy in started:
            copy.wait()

    def spec(space):
        return pl.BlockSpec(memory_space=space)

    tokens = [shape((8, 128), F32)] if token else []
    result = pl.pallas_call(
        body,
        out_shape=(*[pltpu.HBM(o.shape, o.dtype) if k in kept else o for k, o in enumerate(outs)], *tokens),
        in_specs=[spec(pltpu.SMEM)]
        + [spec(pl.ANY if k in far else pltpu.VMEM) for k in range(len(args))]
        + [spec(pl.ANY)] * len(after),
        out_specs=(
            *[spec(pltpu.HBM if k in kept else pltpu.VMEM) for k in range(len(outs))],
            *[spec(pltpu.VMEM) for _ in tokens],
        ),
        scratch_shapes=list(scratch) + buffers + semaphores,
        compiler_params=pltpu.CompilerParams(vmem_limit_bytes=size + extra + MARGIN),
        cost_estimate=pl.CostEstimate(flops=int(micros * PACE), bytes_accessed=size, transcendentals=0),
        name=name,
    )(place, *args, *after)
    result = list(result)
    if token:
        ready = result.pop()
        TOKENS.update((id(value), (value, ready)) for value in result)
    return result


def normalize(rows):
    centered = rows - jnp.mean(rows, axis=-1, keepdims=True)
    scale = lax.rsqrt(jnp.mean(centered * centered, axis=-1, keepdims=True) + 1e-05)
    return centered * scale, scale


def norm_back(grad, scaled, scale, gain):
    weighted = grad * gain
    mean_one = jnp.mean(weighted, axis=-1, keepdims=True)
    mean_two = jnp.mean(weighted * scaled, axis=-1, keepdims=True)
    return scale * (weighted - mean_one - scaled * mean_two)


def column_sum(rows):
    return jnp.sum(rows, axis=0, keepdims=True)


def rope_tables():
    position = jnp.arange(SEQ, dtype=F32)
    frequency = 10000.0 ** (-jnp.arange(0, HEAD_DIM, 2, dtype=F32) / HEAD_DIM)
    angles = position[:, None] * frequency[None, :]
    cos, sin = jnp.cos(angles), jnp.sin(angles)
    return jnp.tile(cos, (1, 8)), jnp.tile(jnp.concatenate([-sin, sin], axis=1), (1, 4))


def swapped(rows):
    low = lax.broadcasted_iota(jnp.int32, rows.shape, 1) % HEAD_DIM < HEAD_DIM // 2
    return jnp.where(low, pltpu.roll(rows, 128 - HEAD_DIM // 2, 1), pltpu.roll(rows, HEAD_DIM // 2, 1))


def group_heads():
    for head in range(GROUP_HEADS):
        yield head, (head // 4) * 128, head % 4


def head_only(rows, lane):
    owner = lax.broadcasted_iota(jnp.int32, rows.shape, 1) // HEAD_DIM
    return jnp.where(owner == lane, rows, jnp.zeros_like(rows))


def halves(place):
    core = place[1]
    return pl.multiple_of(core * HALF, 16), pl.multiple_of((1 - core) * HALF, 16)


def first_norm_kernel(place, move, tokens, vectors, hidden):
    scaled, _ = normalize(tokens[...].astype(F32))
    hidden[...] = (scaled * vectors[0:1, :] + vectors[1:2, :]).astype(BF16)


def stack_into(out, parts):
    for source, part in enumerate(parts):
        out[source] = part[...]


def hand_on_kernel(place, move, value, out):
    out[...] = value[...]


def line_kernel(place, move, *refs):
    cargo = (len(refs) - 5) // 2
    stack_into(refs[4 + cargo], refs[:4])
    for source in range(cargo):
        refs[5 + cargo + source][...] = refs[4 + source][...]


def make_line(place, parts, cargo, after):
    outs = [shape((4, *parts[0].shape))] + [shape(value.shape) for value in cargo]
    return call(line_kernel, "line", outs, place, (*parts, *cargo), 0.6, after=after, token=False)


def pack_kernel(place, move, *refs):
    groups, shards, (packed, lines) = refs[:3], refs[3:7], refs[7:]
    stack_into(packed, groups)
    rows = lines.shape[0] // 8
    for source in range(8):
        side, line = source // 4, source % 4
        lines[source * rows : (source + 1) * rows, :] = shards[line][side * rows : (side + 1) * rows, :]


def pack(place, groups, shards, after):
    outs = [shape((3, *groups[0].shape)), shape((4 * shards[0].shape[0], D))]
    return call(pack_kernel, "pack", outs, place, (*groups, *shards), 1.0, after=after, token=False)


def attention_forward_kernel(groups, place, move, hidden, bias, cos, sin, *refs):
    flush, fetch = move
    count = len(groups)
    mine, other, *refs = refs
    cargo = (len(refs) - 7 * count) // 2
    if cargo:
        for source in range(cargo):
            refs[7 * count + cargo + source][...] = refs[source][...]
        refs = refs[cargo : cargo + 7 * count]
    weights, weights_out, qs, ks, vs, probs, mixed = [refs[part * count : (part + 1) * count] for part in range(7)]
    z = place[0]
    first, second = halves(place)
    rows = hidden[...]
    windows = rows.shape[0] // SEQ
    for step, which in enumerate(groups):
        weight, prob_out = weights[step], probs[step]
        group = place[2] ^ which
        for part in range(4):
            source = z ^ part
            pieces = mine[step, source], other[step, source]
            for offset, piece in zip((first, second), pieces):
                if part < 3:
                    weight[part, pl.ds(offset, HALF), :] = piece
                else:
                    weights_out[step][pl.ds(offset, HALF), :] = piece
            if part < 3:
                weight[part, GROUP:WIDE, :] = jnp.zeros((WIDE - GROUP, D), BF16)
        flush(weight)
        for part, out in ((0, qs[step]), (1, ks[step]), (2, vs[step])):
            proj = nt(rows, weight[part]) + bias[group, part : part + 1, :]
            for window in range(windows):
                span = slice(window * SEQ, (window + 1) * SEQ)
                for tile in (0, 128):
                    piece = proj[span, tile : tile + 128]
                    if part < 2:
                        piece = piece * cos[...] + swapped(piece) * sin[...]
                    out[span, tile : tile + 128] = piece.astype(BF16)
            flush(out)
        for window in range(windows):
            span = slice(window * SEQ, (window + 1) * SEQ)
            visible = lax.broadcasted_iota(jnp.int32, (SEQ, 1), 0) < place[4 + window]
            probs_of, values_of = [], []
            for head, tile, lane in group_heads():
                keys = head_only(ks[step][span, tile : tile + 128], lane)
                scores = nt(keys, qs[step][span, tile : tile + 128])
                scores = jnp.where(visible, scores, -1e30)
                top = jnp.max(scores, axis=0, keepdims=True)
                exponent = jnp.exp2((scores - top) * (SCALE * LOG2_E))
                prob = (exponent * (1.0 / column_sum(exponent))).astype(BF16)
                prob_out[window * GROUP_HEADS + head] = prob
                flush(prob_out, window * GROUP_HEADS + head)
                probs_of.append(prob)
                values_of.append(head_only(vs[step][span, tile : tile + 128], lane))
            out = tn(jnp.concatenate(probs_of[:4], axis=0), jnp.concatenate(values_of[:4], axis=0))
            mixed[step][0:128, span] = out.astype(BF16).T
            mixed[step][128:GROUP, span] = tn(probs_of[4], values_of[4]).astype(BF16).T[0 : GROUP - 128]


def attention_forward(groups, place, hidden, bias, cos, sin, mine, other, after, cargo=()):
    rows = hidden.shape[0]
    maps = rows // SEQ * GROUP_HEADS
    count = len(groups)
    kinds = [Kept((3, WIDE, D)), shape((GROUP, D))] + [Kept((rows, WIDE))] * 3
    kinds += [Kept((maps, SEQ, SEQ)), shape((GROUP, rows))]
    out = call(
        functools.partial(attention_forward_kernel, groups), "attention_forward",
        [kind for kind in kinds for _ in groups] + [shape(value.shape) for value in cargo], place,
        (hidden, bias, cos, sin, mine, other, *cargo), 4.8 * count,
        after=after, copies=count * (4 + maps), token=0 in groups,
    )
    return [out[step : 7 * count : count] for step in range(count)] + out[7 * count :]


def middle_kernel(place, move, tokens, vectors, *refs):
    flush, fetch = move
    mixed_in, weight_in, *refs = refs[:4], refs[4:8], *refs[8:]
    middle, normed, mixed, weight, stage = refs
    for which in range(GROUPS):
        offset = pl.multiple_of((place[2] ^ which) * GROUP, 32)
        stage[pl.ds(offset, GROUP), :] = mixed_in[which][...]
        weight[pl.ds(offset, GROUP), :] = weight_in[which][...]
    mixed[...] = stage[...].T
    rows = tokens[...].astype(F32) + nt(mixed[...], weight[...]) + vectors[5:6, :]
    middle[...] = rows
    scaled, _ = normalize(rows)
    normed[...] = (scaled * vectors[6:7, :] + vectors[7:8, :]).astype(BF16)


def middle_layer(place, tokens, vectors, mixed, weights, after):
    rows = tokens.shape[0]
    outs = [shape((rows, D), F32), shape((rows, D)), shape((rows, D)), shape((D, D))]
    return call(
        middle_kernel, "middle", outs, place, (tokens, vectors, *mixed, *weights), 0.2,
        [pltpu.VMEM((D, rows), BF16)], after, token=False)


def store_quarter(outs, which, value):
    low = value.astype(BF16)
    if which < 3:
        outs[which][...] = low
    else:
        outs[3][...], outs[4][...] = low[: QUARTER // 2], low[QUARTER // 2 :]


def five_parts():
    return [shape((QUARTER, D))] * 3 + [shape((QUARTER // 2, D))] * 2


def quarter(parts, which, side):
    if which < 3:
        return parts[which][side * QUARTER : (side + 1) * QUARTER, :]
    rows = slice(side * 80, (side + 1) * 80)
    return jnp.concatenate([part[rows, :] for part in parts[3:]], axis=0)


def hidden_forward_kernel(quarters, place, move, *refs):
    count = 4 if 3 in quarters else 3
    parts, (bias, normed, normed_pair, back, back_pair), refs = refs[:count], refs[count : count + 5], refs[count + 5 :]
    parts = parts if count == 3 else (None, None, None, *parts)
    active, slopes, grads_down = refs[0], refs[1 : 1 + len(quarters)], refs[1 + len(quarters) :]
    grads_down = grads_down if count == 3 else (None, None, None, *grads_down)
    rows = normed.shape[0]
    for step, which in enumerate(quarters):
        up = quarter(parts, which, 0)
        column = jnp.broadcast_to(bias[which], (8, QUARTER)).T[:, 0:1]
        total = 0.0
        for part, inputs, grads in ((0, normed, back), (1, normed_pair, back_pair)):
            span = slice(part * rows, (part + 1) * rows)
            value = nt(up, inputs[...]) + column
            cdf = 0.5 + 0.5 * lax.erf(value * (0.5**0.5))
            low = (value * cdf).astype(BF16)
            active[step, :, span] = low
            slopes[step][:, span] = (cdf + value * jnp.exp(-0.5 * value * value) * 0.3989422804014327).astype(BF16)
            total = total + nn(low, grads[...])
        store_quarter(grads_down, which, total)


def hidden_forward(quarters, place, parts, bias, normed, normed_pair, back, back_pair, after):
    rows = 2 * normed.shape[0]
    count = len(quarters)
    outs = [shape((count, QUARTER, rows))] + [shape((QUARTER, rows))] * count
    outs += five_parts()[3:] if 3 in quarters else five_parts()[:3]
    active, *rest = call(
        functools.partial(hidden_forward_kernel, quarters), "hidden_forward", outs, place,
        (*parts, bias, normed, normed_pair, back, back_pair), 1.7 * count, after=after, token=3 not in quarters,
    )
    return active, rest[:count], rest[count:]


def hidden_backward_kernel(place, move, *refs):
    parts, slopes, (back, back_pair), refs = refs[:7], refs[7:11], refs[11:13], refs[13:]
    grad_pre, own, pair, up = refs
    rows = back.shape[0]
    for which in range(4):
        units = slice(which * QUARTER, (which + 1) * QUARTER)
        up[units, :] = quarter(parts, which, 0)
        down = quarter(parts, which, 1)
        for part, grads in ((0, back), (1, back_pair)):
            span = slice(part * rows, (part + 1) * rows)
            wide = nt(down, grads[...]) * slopes[which][:, span].astype(F32)
            grad_pre[units, span] = wide.astype(BF16)
    for out, span in ((pair, slice(rows, 2 * rows)), (own, slice(0, rows))):
        out[...] = tn(grad_pre[:, span], up[...]).astype(out.dtype)


def hidden_backward(place, parts, slopes, back, back_pair):
    rows = back.shape[0]
    outs = [shape((4 * QUARTER, 2 * rows)), shape((rows, D), F32), shape((rows, D))]
    return call(
        hidden_backward_kernel, "hidden_backward", outs, place, (*parts, *slopes, back, back_pair), 5.0,
        [pltpu.VMEM((4 * QUARTER, D), BF16)],
    )


def up_gradient_kernel(place, move, grad_pre, normed, normed_pair, *refs):
    grads, grad_bias = refs[:5], refs[5]
    for which in range(4):
        units = slice(which * QUARTER, (which + 1) * QUARTER)
        low = grad_pre[units, :]
        rows = normed.shape[0]
        store_quarter(grads, which, nn(low[:, :rows], normed[...]) + nn(low[:, rows:], normed_pair[...]))
        bias = jnp.sum(low.astype(F32), axis=1, keepdims=True)
        for source in range(4):
            grad_bias[4 * which + source] = jnp.broadcast_to(bias[source * 80 : (source + 1) * 80], (80, 8)).T


def up_gradient(place, grad_pre, normed, normed_pair, after):
    outs = five_parts() + [shape((16, 8, 80), F32)]
    *grads, bias = call(
        up_gradient_kernel, "up_gradient", outs, place, (grad_pre, normed, normed_pair), 4.0, after=after
    )
    return grads, bias


def output_kernel(place, move, most, last, middle, vectors, *refs):
    parts, (own, pair) = refs[:7], refs[7:]
    rows = own.shape[0]
    down = jnp.concatenate([quarter(parts, which, 1) for which in range(4)], axis=0)
    for out, span in ((pair, slice(rows, 2 * rows)), (own, slice(0, rows))):
        left = jnp.concatenate([most[which, :, span] for which in range(3)] + [last[0, :, span]], axis=0)
        total = tn(left, down)
        if out is own:
            total = total + middle[...] + vectors[8:9, :]
        out[...] = total.astype(out.dtype)


def output_layer(place, active, middle, vectors, parts, after):
    rows = middle.shape[0]
    outs = [shape((rows, D), F32), shape((rows, D))]
    return call(
        output_kernel, "output", outs, place, (*active, middle, vectors, *parts), 2.8, after=after
    )


def middle_backward_kernel(
    place, move, own, pair, middle, back, vectors, mixed, weight, grad_middle, sums, grad_mixed, mine, other, stage, stage_mixed
):
    grad = own[...] + pair[...].astype(F32)
    scaled, scale = normalize(middle[...])
    wide = back[...].astype(F32)
    total = wide + norm_back(grad, scaled, scale, vectors[6:7, :])
    grad_middle[...] = total
    sums[0:1, :] = column_sum(total)
    sums[1:2, :] = column_sum(grad * scaled)
    sums[2:3, :] = column_sum(grad)
    sums[3:4, :] = column_sum(wide)
    sums[4:8, :] = jnp.zeros((4, D), F32)
    low = total.astype(BF16)
    stage_mixed[...] = nt(weight[...].T, low).astype(BF16)
    stage[...] = tn(low, mixed[...]).astype(BF16)
    first, second = halves(place)
    for which in range(GROUPS):
        offset = (place[2] ^ which) * GROUP
        grad_mixed[which] = stage_mixed[pl.ds(pl.multiple_of(offset, 32), GROUP), :]
        mine[which] = stage[pl.ds(pl.multiple_of(offset + first, 16), HALF), :]
        other[which] = stage[pl.ds(pl.multiple_of(offset + second, 16), HALF), :]


def middle_backward(place, own, pair, middle, back, vectors, mixed, weight, after):
    rows = own.shape[0]
    outs = [shape((rows, D), F32), shape((8, D), F32), shape((GROUPS, GROUP, rows))]
    outs += [shape((GROUPS, HALF, D)), shape((GROUPS, HALF, D))]
    return call(
        middle_backward_kernel, "middle_backward", outs, place,
        (own, pair, middle, back, vectors, mixed, weight), 3.0,
        [pltpu.VMEM((D, D), BF16), pltpu.VMEM((D, rows), BF16)], after,
    )


def attention_backward_kernel(groups, place, move, grad_mixed, hidden, cos, sin, out_mine, out_other, *refs):
    count = len(groups)
    qs, ks, vs, probs, dqs, dks, dvs = [refs[part * count : (part + 1) * count] for part in range(7)]
    biases, (mine, other, stage) = refs[7 * count : 8 * count], refs[8 * count :]
    rows = hidden.shape[0]
    first, second = halves(place)
    for step, which in enumerate(groups):
        q, k, v, prob_in, dq_out, dk_out, dv_out = (
            qs[step], ks[step], vs[step], probs[step], dqs[step], dks[step], dvs[step]
        )
        for window in range(rows // SEQ):
            span = slice(window * SEQ, (window + 1) * SEQ)
            grad = grad_mixed[which, :, span].T
            tail = jnp.concatenate([grad[:, 128:GROUP], jnp.zeros((SEQ, WIDE - GROUP), BF16)], axis=1)
            grads = {0: grad[:, :128], 128: tail}
            lows, slopes, grads_of, queries_of, keys_of = [], [], [], [], []
            for head, tile, lane in group_heads():
                cols = slice(tile, tile + 128)
                low = prob_in[window * GROUP_HEADS + head]
                prob = low.astype(F32)
                weighted = prob * nt(head_only(v[span, cols], lane), grads[tile])
                lows.append(low)
                slopes.append((weighted - prob * column_sum(weighted)).astype(BF16))
                grads_of.append(head_only(grads[tile], lane))
                queries_of.append(head_only(q[span, cols], lane))
                keys_of.append(head_only(k[span, cols], lane))
            for tile, heads in ((0, slice(0, 4)), (128, slice(4, 5))):
                cols = slice(tile, tile + 128)
                down = jnp.concatenate(slopes[heads], axis=1)
                dv_out[span, cols] = nn(
                    jnp.concatenate(lows[heads], axis=1), jnp.concatenate(grads_of[heads], axis=0)
                ).astype(BF16)
                piece = nn(down, jnp.concatenate(queries_of[heads], axis=0)) * SCALE
                dk_out[span, cols] = (piece * cos[...] - swapped(piece) * sin[...]).astype(BF16)
                piece = tn(jnp.concatenate(slopes[heads], axis=0), jnp.concatenate(keys_of[heads], axis=0)) * SCALE
                dq_out[span, cols] = (piece * cos[...] - swapped(piece) * sin[...]).astype(BF16)
        biases[step][...] = jnp.zeros((8, WIDE), F32)
        for part, out in ((0, dq_out), (1, dk_out), (2, dv_out)):
            values = out[...]
            stage[step, part] = tn(values, hidden[...]).astype(BF16)
            mine[step, part] = stage[step, part, pl.ds(first, HALF), :]
            other[step, part] = stage[step, part, pl.ds(second, HALF), :]
            biases[step][part : part + 1, :] = column_sum(values.astype(F32))
        mine[step, 3] = out_mine[which]
        other[step, 3] = out_other[which]


def attention_backward(groups, place, grad_mixed, hidden, cos, sin, out_mine, out_other, saved, after):
    rows = hidden.shape[0]
    count = len(groups)
    outs = [shape((rows, WIDE))] * (3 * count) + [shape((8, WIDE), F32)] * count + [shape((count, 4, HALF, D))] * 2
    *out, mine, other = call(
        functools.partial(attention_backward_kernel, groups), "attention_backward", outs, place,
        (grad_mixed, hidden, cos, sin, out_mine, out_other, *[group[k] for k in range(4) for group in saved]),
        4.7 * count,
        [pltpu.VMEM((count, 3, WIDE, D), BF16)], after,
    )
    return [out[step::count] for step in range(count)], mine, other


def first_backward_kernel(place, move, tokens, grad_middle, vectors, *refs):
    parts, weights, biases, (middle_sums, units), refs = refs[:12], refs[12:16], refs[16:20], refs[20:22], refs[22:]
    input_grad, sums, unit_rows = refs
    z, plane, core = place[0], place[2], place[3]
    grad = 0.0
    for which in range(GROUPS):
        for part in range(3):
            grad = grad + nn(parts[which * 3 + part][...], weights[which][part])
    scaled, scale = normalize(tokens[...].astype(F32))
    input_grad[...] = (grad_middle[...] + norm_back(grad, scaled, scale, vectors[0:1, :])).astype(BF16)
    sums[...] = jnp.zeros((24, D), F32)
    sums[0:1, :] = column_sum(grad * scaled)
    sums[1:2, :] = column_sum(grad)
    sums[2:6, :] = middle_sums[0:4, :]
    for group in range(GROUPS):
        value = sum(jnp.where((plane ^ which) == group, biases[which][...], 0.0) for which in range(GROUPS))
        row, column = 8 + 4 * (group // 2), WIDE * (group % 2)
        sums[row : row + 4, column : column + WIDE] = value[0:4]
    unit_rows[...] = jnp.zeros((4, 8, 128), F32)
    for which in range(4):
        for source in range(4):
            row = (plane ^ which) * 2 + core
            unit_rows[z ^ source, pl.ds(row, 1), 0:80] = units[4 * which + source, 0:1, :]
    for line in range(4):
        sums[16:24, line * 128 : (line + 1) * 128] = unit_rows[line]


def first_backward(place, tokens, grad_middle, vectors, parts, weights, biases, middle_sums, units, after):
    rows = tokens.shape[0]
    outs = [shape((rows, D)), shape((24, D), F32)]
    return call(
        first_backward_kernel, "first_backward", outs, place,
        (tokens, grad_middle, vectors, *parts, *weights, *biases, middle_sums, units),
        0.2, [pltpu.VMEM((4, 8, 128), F32)], after, token=False)


def unpack_vector(sums):
    group_rows = [sums[8 + 4 * (g // 2) :, WIDE * (g % 2) :][:3, :GROUP] for g in range(GROUPS)]
    units = sums[16:24, :512].reshape(8, 4, 128)[:, :, :80].transpose(1, 0, 2).reshape(4, D)
    return jnp.concatenate([sums[0:2], jnp.concatenate(group_rows, axis=1), sums[2:6], units])


def ordered_sum_kernel(which, place, move, *refs):
    total = 0.0
    for index in range(4):
        total = total + sum(jnp.where((place[which] ^ step) == index, refs[step][...], 0.0) for step in range(4))
    refs[4][...] = total


def ordered_sum(place, which, parts, after=()):
    outs = [shape(parts[0].shape, F32)]
    return call(functools.partial(ordered_sum_kernel, which), "ordered_sum", outs, place, parts, 0.6, after=after, token=False)[0]


def attention_sum_kernel(place, move, *refs):
    parts, (own, *sent), stage = refs[:4], refs[4:8], refs[8]
    stage[...] = sum(value[...].astype(F32) for value in parts[2:]) + sum(value[1].astype(F32) for value in parts[:2])
    own[...] = stage[place[0]]
    for steps, out in enumerate(sent):
        out[...] = stage[place[0] ^ (steps + 1)].astype(BF16)


def attention_sum(place, parts, after):
    dims = parts[2].shape
    outs = [shape(dims[1:], F32)] + [shape(dims[1:])] * 3
    return call(
        attention_sum_kernel, "attention_sum", outs, place, parts, 1.0, [pltpu.VMEM(dims, F32)], after=after
    )


def add(out, *parts):
    out[...] = sum(part.astype(F32) for part in parts).astype(out.dtype)


def keep_and_send(parts, keep, sent):
    total = sum(part[...].astype(F32) for part in parts)
    keep[...] = total[0:2]
    sent[...] = total[2:4].astype(BF16)


def merge_into(along_y, along_x, first, second, out_y, out_x):
    out_y[0:2] = along_y[0:2]
    add(out_y.at[2:4], along_y[2:4], second[...])
    add(out_x.at[0:2], along_x[0:2], first[...])
    out_x[2:4] = along_x[2:4]


def merge_kernel(place, move, along_y, along_x, *refs):
    merge_into(along_y, along_x, *refs)


def merge(place, along_y, along_x, first, second, after):
    outs = [shape(along_y.shape)] * 2
    return call(merge_kernel, "merge", outs, place, (along_y, along_x, first, second), 1.0, after=after)


def exchange_one_kernel(place, move, *refs):
    downs, (along_y, along_x, first, second), refs = refs[:3], refs[3:7], refs[7:]
    keep, sent, out_y, out_x = refs
    keep_and_send(downs, keep, sent)
    merge_into(along_y, along_x, first, second, out_y, out_x)


def exchange_one(place, downs, ups, after):
    dims = downs[0].shape
    outs = [shape((2, *dims[1:]), F32), shape((2, *dims[1:]))] + [shape(dims)] * 2
    return call(
        exchange_one_kernel, "exchange_one", outs, place,
        (*downs, *ups), 2.0, after=after,
    )


def cores_one_kernel(place, move, mine, other, half_y, half_x, rest):
    add(half_y, mine[0, 0:2], other[0, 0:2])
    add(half_x, mine[0, 2:4], other[0, 2:4])
    add(rest, mine[1], other[1])


def cores_one(place, mine, other, after):
    dims = mine.shape[1:]
    outs = [shape((2, *dims[1:]))] * 2 + [shape(dims)]
    return call(cores_one_kernel, "cores_one", outs, place, (mine, other), 1.0, after=after)


def exchange_two_kernel(place, move, *refs):
    ups, (keep_in, line_in), (keep, sent, own, line) = refs[:3], refs[3:5], refs[5:]
    keep_and_send(ups, keep, sent)
    total = keep_in[...] + line_in[...].astype(F32)
    own[...] = total[0]
    line[...] = total[1].astype(BF16)


def exchange_two(place, ups, keep, line, after):
    dims = ups[0].shape
    outs = [shape((2, *dims[1:]), F32), shape((2, *dims[1:])), shape(dims[1:], F32), shape(dims[1:])]
    return call(
        exchange_two_kernel, "exchange_two", outs, place, (*ups, keep, line), 12.0, after=after
    )


def exchange_three_kernel(
    place, move, rest, mine, other, first, second, keep, line_in, down_line, along_y, along_x, own, line
):
    add(along_x.at[0:2], rest[0:2], first[...])
    along_x[2:4] = rest[2:4]
    add(along_y.at[0:2], mine[0, 0:2], other[0, 0:2])
    add(along_y.at[2:4], mine[0, 2:4], other[0, 2:4], second[...])
    total = keep[...] + line_in[...].astype(F32)
    own[...] = total[0]
    line[0] = total[1].astype(BF16)
    line[1] = down_line[...]


def exchange_three(place, rest, mine, other, halves_in, keep, line, down_line, after):
    dims = rest.shape
    outs = [shape(dims)] * 2 + [shape(dims[1:], F32), shape((2, *dims[1:]))]
    return call(
        exchange_three_kernel, "exchange_three", outs, place, (rest, mine, other, *halves_in, keep, line, down_line), 1.0,
        after=after,
    )


def core_runs(place):
    for which in range(4):
        for source in range(4):
            run = ((place[0] ^ source) * 4 + (place[2] ^ which)) * 2 + place[3]
            yield which, source, pl.ds(pl.multiple_of(run * 80, 16), 80)


def take_runs_kernel(place, move, up, down, *outs):
    for which, source, rows in core_runs(place):
        for side, full in enumerate((up, down)):
            if which < 3:
                start = side * QUARTER + source * 80
                outs[which][start : start + 80, :] = full[rows, :]
            else:
                outs[3 + source][side * 80 : (side + 1) * 80, :] = full[rows, :]


def take_runs(place, full):
    outs = [shape((2 * QUARTER, D))] * 3 + [shape((160, D))] * 4
    return call(take_runs_kernel, "take_runs", outs, place, full, 1.0, token=False)


def place_runs_kernel(place, move, *refs):
    full = refs[5]
    full[...] = jnp.zeros_like(full)
    for which, source, rows in core_runs(place):
        part, offset = (which, source) if which < 3 else (3 + source // 2, source % 2)
        full[rows, :] = refs[part][offset * 80 : (offset + 1) * 80, :].astype(F32)


def place_runs(place, quarters):
    return call(place_runs_kernel, "place_runs", [shape((FF, D), F32)], place, quarters, 2.0, token=False)[0]


def pick(array, index):
    return lax.dynamic_index_in_dim(array, index, 0, keepdims=False)


def step_into(rate, gradient, state, outs):
    weight, first, second = state
    grad, second_new, new = outs
    grad[...] = gradient
    second_new[...], new[...] = adamw(weight[...], first[...], second[...], gradient, rate)


def finish_attention_kernel(place, move, own, one, two, three, weight, first, second, *outs):
    total = own[...]
    for value in (one, two, three):
        total = total + value[...].astype(F32)
    step_into(0.1, total, (weight, first, second), outs)


def finish_attention(place, own, line, state, after):
    out = call(
        finish_attention_kernel, "finish_attention", [shape(own.shape, F32)] * 3, place,
        (own, *line, *[value.T for value in state]), 0.3, after=after, token=False)
    return [value.T for value in out]


def finish_hidden_kernel(place, move, *refs):
    owns, arrived, refs = refs[:2], refs[2], refs[3:]
    for matrix in range(2):
        state = refs[3 * matrix : 3 * matrix + 3]
        outs = refs[6 + 3 * matrix : 9 + 3 * matrix]
        step_into(0.1, owns[matrix][...] + arrived[matrix].astype(F32), state, outs)


def finish_hidden(place, owns, arrived, state, after):
    out = call(
        finish_hidden_kernel, "finish_hidden", [shape(owns[0].shape, F32)] * 6, place,
        (*owns, arrived, *[value.T for value in state]), 0.3, after=after,
    )
    return [value.T for value in out[:3]], [value.T for value in out[3:]], out[0]


def result_kernel(place, move, own, pair, out):
    out[...] = (own[...] + pair[...].astype(F32)).astype(BF16)


def result_layer(place, own, pair, after):
    return call(result_kernel, "result", [shape(pair.shape)], place, (own, pair), 12.0, after=after)[0]


def adamw(weight, first_moment, second_moment, gradient, rate_value):
    first_new = 0.9 * first_moment + 0.1 * gradient
    second_new = 0.999 * second_moment + 0.001 * gradient * gradient
    corrected = first_new / (1.0 - 0.9**STEP) / (jnp.sqrt(second_new / (1.0 - 0.999**STEP)) + 1e-08)
    return (second_new, weight - rate_value * (corrected + 0.01 * weight))


class Layout:
    def __init__(self, total):
        self.total = total
        self.block = 4 * D // total
        self.stride = total // 4
        self.me = lax.axis_index(AXES)
        self.core = lax.rem(self.me, 2)

    def swap(self, value, mask):
        return lax.ppermute(value, AXES, [(i, i ^ mask) for i in range(self.total)])

    def shift(self, value, steps):
        pairs = [(i, (i + self.stride * steps) % self.total) for i in range(self.total)]
        return lax.ppermute(value, AXES, pairs)


    def hidden_index(self):
        order = jnp.arange(16)
        z, plane = self.place[0], self.place[2]
        return ((z ^ lax.rem(order, 4)) * 4 + (plane ^ (order // 4))) * 2 + self.core


class Ring(Layout):
    def __init__(self, total):
        super().__init__(total)
        self.ring = True
        self.z = self.me // 8
        self.plane = lax.rem(self.me // 2, 4)
        self.place = (self.z, self.core, self.plane)

    def along_z(self, value):
        return [value] + [self.swap(value, 8 * s) for s in (1, 2, 3)]

    def in_plane(self, value, each=None):
        return [value] + [self.swap(each[r].reshape(value.shape) if each else value, 2 * r) for r in (1, 2, 3)]

    def corner(self, *value):
        return [self.swap(value[0], 2), self.swap(value[1], 4)]

    def send_plane(self, along_y, along_x):
        return [self.swap(along_y, 2), self.swap(along_x, 4)]

    def all_total(self, value, after):
        value = ordered_sum(self.vector, 2, self.in_plane(value), after)
        return ordered_sum(self.vector, 0, [value] + [self.swap(value, 8 * s) for s in (1, 2, 3)])


class Whole(Layout):
    def __init__(self, total):
        super().__init__(total)
        self.ring = False
        self.plane = jnp.int32(0)
        self.place = (jnp.int32(0),) * 3

    def gather(self, attn, up, down):
        full = lax.all_gather(attn, AXES, axis=0, tiled=True).reshape(4, 4, 2, HALF, D)
        mine = [full[:, r, 0] for r in range(4)]
        other = [full[:, r, 1] for r in range(4)]
        both = [lax.all_gather(value, AXES, axis=0, tiled=True) for value in (up, down)]
        return mine, other, take_runs(self.vector, both)

    def scatter_hidden(self, grads):
        return lax.psum_scatter(place_runs(self.vector, grads), AXES, scatter_dimension=0, tiled=True)

    def scatter_attention(self, mine, other):
        full = jnp.stack([jnp.stack(mine, axis=1), jnp.stack(other, axis=1)], axis=2)
        return lax.psum_scatter(full.astype(F32).reshape(4 * D, D), AXES, scatter_dimension=0, tiled=True)


def per_device(
    total,
    tokens,
    cotangent,
    lengths,
    offsets,
    attn_weight,
    attn_first,
    attn_second,
    up_weight,
    up_first,
    up_second,
    down_weight,
    down_first,
    down_second,
    vectors,
    vec_first,
    vec_second,
):
    TOKENS.clear()
    lay = Ring(total) if total == 32 else Whole(total)
    counts = jnp.minimum(lengths - offsets, SEQ).reshape(-1)
    rows = counts.shape[0] * SEQ
    place = lay.vector = jnp.concatenate([jnp.stack([*lay.place, lay.core]).astype(jnp.int32), counts])
    cos, sin = rope_tables()

    flat = tokens.reshape(rows, D)
    back = cotangent.reshape(rows, D)
    back_pair = lay.swap(back, 1)
    (hidden,) = call(first_norm_kernel, "first_norm", [shape((rows, D))], place, (flat, vectors), 1.0)
    bias = jnp.pad(vectors[2:5].reshape(3, GROUPS, GROUP).transpose(1, 0, 2), ((0, 0), (0, 0), (0, WIDE - GROUP)))

    chosen = (lay.hidden_index()[:, None] == jnp.arange(32)[None, :]).astype(F32)
    bias_up = jnp.dot(chosen, vectors[9:].reshape(32, 80), precision=lax.Precision.HIGHEST).reshape(4, 1, QUARTER)

    if lay.ring:
        shards = jnp.concatenate([up_weight.T, down_weight.T]).astype(BF16)
        attn_parts = lay.along_z(attn_weight.T.astype(BF16))
        corner = lay.swap(shards, 6)
        line, shards = make_line(place, attn_parts, [shards], [hidden, bias_up, bias])
        far_shard = lay.swap(shards, 16)
        groups = lay.in_plane(line)[1:]
        other = lay.swap(line, 1)
        mine = line[None]
    else:
        mine, other, hidden_parts = lay.gather(
            attn_weight.T.astype(BF16), up_weight.T.astype(BF16), down_weight.T.astype(BF16)
        )
        mine, packed = mine[0][None], jnp.stack(mine[1:])
        other, packed_other = other[0], jnp.stack(other[1:])
    forward = attention_forward(
        (0,), place, hidden, bias, cos, sin, mine, other[None], [corner] if lay.ring else []
    )
    if lay.ring:
        shards = [shards, lay.swap(shards, 8), far_shard, lay.swap(far_shard, 8)]
        packed, lines = pack(place, groups, shards, [forward[0][2]])
        hidden_parts = [lines, lay.swap(lines, 2), lay.swap(lines, 4)]
        packed_other = lay.swap(packed, 1)
        (corner,) = call(
            hand_on_kernel, "hand_on", [shape(corner.shape)], place, (corner,), 0.4, after=[packed_other], token=False
        )
        corner_far = lay.swap(corner, 16)
        corners = [corner, lay.swap(corner, 8), corner_far, lay.swap(corner_far, 8)]
        hidden_parts = hidden_parts + corners
    after = [forward[0][2]]
    forward += attention_forward((1, 2, 3), place, hidden, bias, cos, sin, packed, packed_other, after)
    weights = [group[0] for group in forward]
    middle, normed, mixed, out_weight = middle_layer(
        place, flat, vectors, [group[6] for group in forward], [group[1] for group in forward],
        corners[1:3] if lay.ring else [],
    )
    normed_pair = lay.swap(normed, 1)
    both = (normed, normed_pair, back, back_pair)
    most, slope, grad_down = hidden_forward((0, 1, 2), place, hidden_parts[:3], bias_up, *both, [])
    rest, *last = hidden_forward((3,), place, hidden_parts[3:], bias_up, *both, [most])
    active, slope, grad_down = (most, rest), slope + last[0], grad_down + last[1]
    if lay.ring:
        grad_down = [value.reshape(-1, 80, D) for value in grad_down]
        down_corner = lay.corner(*grad_down[3:])
    grad_pre, own, pair = hidden_backward(place, hidden_parts, slope, back, back_pair)
    gradient_after, middle_after, after = [], [], []
    if lay.ring:
        down_sent = merge(place, *grad_down[1:3], *down_corner, [own])
        gradient_after = down_sent[:1]
        down_sent = middle_after = lay.send_plane(*down_sent)
    grad_up, grad_bias_up = up_gradient(place, grad_pre, normed, normed_pair, gradient_after)
    if lay.ring:
        grad_up = [value.reshape(-1, 80, D) for value in grad_up]
        up_corner = lay.corner(*grad_up[3:])
    out_own, out_pair = output_layer(place, active, middle, vectors, hidden_parts, [grad_bias_up])
    out_pair = lay.swap(out_pair, 1)
    grad_middle, sums, grad_mixed, out_mine, out_other = middle_backward(
        place, own, lay.swap(pair, 1), middle, back, vectors, mixed, out_weight, [out_own] + middle_after
    )

    def backward_of(groups, after):
        saved = [forward[r][2:6] for r in groups]
        return attention_backward(groups, place, grad_mixed, hidden, cos, sin, out_mine, out_other, saved, after)

    if lay.ring:
        keep, line, *up_sent = exchange_one(place, [grad_down[0], *down_sent], [*grad_up[1:3], *up_corner], [sums])
        down_line = lay.swap(line, 16)
        up_sent = lay.send_plane(*up_sent)
        after = [keep]
    later, mine_one, other_one = backward_of((3, 2), after)
    after = [later[0][0]]
    if lay.ring:
        other_one = lay.swap(other_one, 1)
        up_keep, up_line, down_own, down_line = exchange_two(
            place, [grad_up[0], *up_sent], keep, down_line, after
        )
        up_line = lay.swap(up_line, 16)
        *attn_corner, along_x = cores_one(place, mine_one, other_one, [up_keep])
        attn_corner = lay.corner(*attn_corner)
        after = [up_keep, along_x]
    sooner, mine_two, other_two = backward_of((1, 0), after)
    backward = [sooner[1], sooner[0], later[1], later[0]]
    other_two, after = lay.swap(other_two, 1) if lay.ring else other_two, [sooner[0][0]]
    if lay.ring:
        after += [*attn_corner, up_line]
    result = result_layer(place, out_own, out_pair, after)
    if lay.ring:
        along_y, along_x, up_own, hidden_line = exchange_three(
            place, along_x, mine_two, other_two, attn_corner, up_keep, up_line, down_line, [result]
        )
        after = [along_y]
    parts = [value for group in backward for value in group[:3]]
    input_grad, vec_sums = first_backward(
        place, flat, grad_middle, vectors, parts, weights, [group[3] for group in backward], sums, grad_bias_up, after
    )
    state = up_weight, up_first, up_second, down_weight, down_first, down_second
    if lay.ring:
        along_y, along_x = lay.send_plane(along_y, along_x)
        hidden_line = lay.swap(hidden_line, 8)
        vec_core = vec_sums + lay.swap(vec_sums, 1)
        attn_own, *attn_line = attention_sum(place, [mine_two, other_two, along_y, along_x], [vec_core])
        vec_sums = lay.all_total(vec_core, [attn_own])
        attn_line = [lay.swap(value, 8 * s) for value, s in zip(attn_line, (1, 2, 3))]
        (grad_up, up_second_new, up_new), (grad_down, down_second_new, down_new), done = finish_hidden(
            place, [up_own, down_own], hidden_line, state, [attn_own]
        )
        grad_attn, attn_second_new, attn_new = finish_attention(
            place, attn_own, attn_line, (attn_weight, attn_first, attn_second), [done]
        )
    else:
        grad_up, grad_down = lay.scatter_hidden(grad_up).T, lay.scatter_hidden(grad_down).T
        order = (mine_two[1], mine_two[0], mine_one[1], mine_one[0])
        order_other = (other_two[1], other_two[0], other_one[1], other_one[0])
        grad_attn = lay.scatter_attention(order, order_other).T
        attn_second_new, attn_new = adamw(attn_weight, attn_first, attn_second, grad_attn, 0.1)
        up_second_new, up_new = adamw(*state[:3], grad_up, 0.1)
        down_second_new, down_new = adamw(*state[3:], grad_down, 0.1)
        vec_sums = lax.psum(vec_sums, AXES)
    grad_vec = unpack_vector(vec_sums)
    vec_second_new, vectors_new = adamw(vectors, vec_first, vec_second, grad_vec, 0.5)
    return (
        result.reshape(tokens.shape),
        input_grad.reshape(tokens.shape),
        grad_attn,
        grad_up,
        grad_down,
        grad_vec,
        attn_second_new,
        up_second_new,
        down_second_new,
        vec_second_new,
        attn_new,
        up_new,
        down_new,
        vectors_new,
    )


def solution(mesh):
    total = mesh.shape["wide"] * mesh.shape["narrow"]
    windows = P(None, AXES, None, None)
    counts = P(None, AXES)
    columns = P(None, AXES)
    in_specs = (windows,) * 2 + (counts,) * 2 + (columns,) * 9 + (P(),) * 3
    out_specs = (windows,) * 2 + (columns,) * 3 + (P(),) + (columns,) * 3 + (P(),) + (columns,) * 3 + (P(),)
    return jax.shard_map(
        functools.partial(per_device, total),
        mesh=mesh,
        in_specs=in_specs,
        out_specs=out_specs,
        check_vma=False,
    )
```
